32 devices in a mesh: dp: 2 (over x), expert: 16 (over z, y, core).
Axes of the slice: x: 2, y: 2, z: 4, core: 2. Of those that a mesh axis runs over, the one named last changes fastest.
Arguments:
- tokens: bfloat16 [4096, 1536], P(('dp', 'expert')), may hold values from -6 to 6
- cotangent: bfloat16 [4096, 1536], P(('dp', 'expert')), may hold values from -6 to 6
- norm_attn: bfloat16 [1536], P(('dp', 'expert')), may hold values from 0.5 to 1.5
- w_query: bfloat16 [1536, 1536], P(('dp', 'expert')), may hold values from -0.15625 to 0.15625
- key_projection: bfloat16 [1536, 512], P(('dp', 'expert')), may hold values from -0.15625 to 0.15625
- value_projection: bfloat16 [1536, 512], P(('dp', 'expert')), may hold values from -0.15625 to 0.15625
- w_out: bfloat16 [1536, 1536], P(('dp', 'expert')), may hold values from -0.625 to 0.625
- norm_ffn: bfloat16 [1536], P(('dp', 'expert')), may hold values from 0.5 to 1.5
- w_router: bfloat16 [1536, 16], P(('dp', 'expert')), may hold values from -0.078125 to 0.078125
- expert_gate: bfloat16 [16, 1536, 512], P('expert', 'dp'), may hold values from -0.15625 to 0.15625
- expert_up: bfloat16 [16, 1536, 512], P('expert', 'dp'), may hold values from -0.15625 to 0.15625
- expert_down: bfloat16 [16, 512, 1536], P('expert', None, 'dp'), may hold values from -0.75 to 0.75
- routes: int32 [4096, 8], P(('dp', 'expert')), may hold values from 0 to 15, all different within a row
- slot_order: int32 [32, 1024], P(('dp', 'expert')), may hold values from 0 to 1023, each once within a row
- doc_lengths: int32 [16, 3], P('expert'), may hold values from 1 to 224, 256 in all within a row
- deal: int32 [2, 16, 128], P(None, 'expert'), may hold values from 0 to 255, as said below
Outputs:
- output: bfloat16 [4096, 1536], P(('dp', 'expert'))
- tokens_grad: bfloat16 [4096, 1536], P(('dp', 'expert'))
- norm_attn_grad: float32 [1536], P(('dp', 'expert'))
- w_query_grad: float32 [1536, 1536], P(('dp', 'expert'))
- w_key_grad: float32 [1536, 512], P(('dp', 'expert'))
- w_value_grad: float32 [1536, 512], P(('dp', 'expert'))
- w_out_grad: float32 [1536, 1536], P(('dp', 'expert'))
- norm_ffn_grad: float32 [1536], P(('dp', 'expert'))
- w_router_grad: float32 [1536, 16], P(('dp', 'expert'))
- expert_gate_grad: float32 [16, 1536, 512], P('expert', 'dp')
- expert_up_grad: float32 [16, 1536, 512], P('expert', 'dp')
- expert_down_grad: float32 [16, 512, 1536], P('expert', None, 'dp')
The draws below stay inside these ranges and needn't reach their ends.
Inputs may be any that keep to these rules, and one draw needn't show every extreme that they name: `routes`: the 8 experts of one token are different. `slot_order`: each row lists every number 0 to 1023 once. `doc_lengths`: each row sums to 256; its longest document has 224 tokens. Cut the places of a group into 4 pieces of 64 consecutive places; deal[i, e] lists, in rising order, the places of piece p and of piece 2 * 2 - 1 - p, where p differs over i for each e (so the 2 entries deal[i, e] together list every place once).
All inputs are finite; a program needn't handle non-finite values.
Results may differ from the reference program's by a relative error of at most 0.017.
Values may be sent and summed in bfloat16 or wider, within the bound.
A program may use at most 192 MiB of HBM per device.

```python
import math
from functools import partial
import jax
import jax.numpy as jnp
import numpy as np
from jax import lax

MODEL_DIM = 1536
QUERY_HEADS = 24
KEY_VALUE_HEADS = 8
HEAD_DIM = 64
FF = 512
TOPK = 8
EXPERTS = 16
TOK_DEV = 128
DOCS = 3
GROUP_TOK = 256
MOST_LEN = 224
TOKEN_TOTAL = 4096
CAP = 72
N_DP = 2
N_EXPERT = 16


def piece_order(one_key):
    return jax.random.permutation(one_key, N_DP)


def draw_deal(key, part):
    key = jax.random.fold_in(key, 7)
    half_rows = TOK_DEV // 2
    group_keys = jax.random.split(key, N_EXPERT)
    chosen_pieces = jax.vmap(piece_order)(group_keys).astype(jnp.int32).T
    inside = jnp.arange(half_rows, dtype=jnp.int32)
    early_part = chosen_pieces[:, :, None] * half_rows + inside[None, None, :]
    late_part = (2 * N_DP - 1 - chosen_pieces)[:, :, None] * half_rows + inside[None, None, :]
    return jnp.concatenate([early_part, late_part], axis=2).astype(jnp.int32)


def shard_levels(own_key, dims, cuts, low, high):
    factor_of = 1.0
    for dim, parts in cuts:
        draws = jax.random.uniform(jax.random.fold_in(jax.random.fold_in(own_key, 6), dim), (parts,), jnp.float32, low / len(cuts), high / len(cuts))
        factor_of = factor_of * jnp.repeat(jnp.exp(draws), dims[dim] // parts).reshape((-1,) + (1,) * (len(dims) - 1 - dim))
    return factor_of


def choose_distinct(rng, rows, number_of, top, lift):
    order = jax.random.permutation(jax.random.fold_in(rng, 1), number_of)
    favour = order
    for power in range(3):
        favour = favour * favour // number_of
    favour = favour * lift // number_of
    lots = jax.random.randint(jax.random.fold_in(rng, 2), (rows, number_of), 0, 4096) + favour
    holders = jax.random.permutation(jax.random.fold_in(rng, 3), rows)[jnp.arange(number_of) % rows]
    lots = jnp.where(jnp.arange(rows)[:, None] == holders[None, :], 1 << 14, lots)
    score = lots * number_of + jnp.arange(number_of)
    return lax.top_k(score.astype(jnp.int32), top)[1].astype(jnp.int32)


def split_up(count, total, reach, slope):
    loads = [(1 << 20) // math.isqrt(rank ** slope) + 1 for rank in range(2, count + 1)]
    spare, counts = total - reach - (count - 1), [1] * (count - 1)
    while spare > 0:
        free = [i for i in range(count - 1) if counts[i] < reach]
        pool, left = sum([loads[i] for i in free]), spare
        for i in free:
            addition = min(reach - counts[i], max(1, left * loads[i] // pool), spare)
            counts[i] = counts[i] + addition
            spare = spare - addition
    return np.array([reach] + counts)


def ragged(key, count, total, reach, skew):
    if count == 2:
        one = jax.random.randint(key, (), max(1, total - reach), min(reach, total - 1) + 1)
        return jnp.stack([one, total - one])
    sizes = jnp.asarray(split_up(count, total, reach, skew), jnp.int32)
    pairs = (count - 1) // 2
    giver, taker = sizes[1:1 + 2 * pairs:2], sizes[2:2 + 2 * pairs:2]
    margin = jnp.minimum(giver - 1, reach - taker)
    passed = jax.random.randint(jax.random.fold_in(key, 1), (pairs,), 0, 1 << 20) % (margin + 1)
    sizes = sizes.at[1:1 + 2 * pairs:2].set(giver - passed).at[2:2 + 2 * pairs:2].set(taker + passed)
    return sizes[jax.random.permutation(jax.random.fold_in(key, 2), count)]


def bell_draw(rng, extent, scale, bound, cuts=(), held_as=jnp.bfloat16):
    loudness = shard_levels(rng, extent, cuts, -0.22, 0.18) if cuts else 1.0
    values = jax.random.normal(rng, extent, jnp.float32) * scale * loudness
    return jnp.minimum(jnp.maximum(values, -bound), bound).astype(held_as)


def setup_inputs(seed: int = 0) -> dict:
    keys = jax.random.split(jax.random.key(seed), 17)
    tokens = bell_draw(keys[0], (TOKEN_TOTAL, MODEL_DIM), 1.0, 6.0, ((0, 32),))
    cotangent = bell_draw(keys[1], (TOKEN_TOTAL, MODEL_DIM), 1.0, 6.0, ((0, 32),))
    norm_attn = jnp.clip(1.0 + 0.1 * jax.random.normal(keys[2], (MODEL_DIM,), jnp.float32), 0.5, 1.5).astype(jnp.bfloat16)
    w_query = bell_draw(keys[3], (MODEL_DIM, QUERY_HEADS * HEAD_DIM), MODEL_DIM ** -0.5, 0.15625, ((0, 32),))
    key_projection = bell_draw(keys[4], (MODEL_DIM, KEY_VALUE_HEADS * HEAD_DIM), MODEL_DIM ** -0.5, 0.15625, ((0, 32),))
    value_projection = bell_draw(keys[5], (MODEL_DIM, KEY_VALUE_HEADS * HEAD_DIM), MODEL_DIM ** -0.5, 0.15625, ((0, 32),))
    w_out = bell_draw(keys[6], (QUERY_HEADS * HEAD_DIM, MODEL_DIM), (QUERY_HEADS * HEAD_DIM // 16) ** -0.5, 0.625, ((0, 32),))
    norm_ffn = jnp.clip(1.0 + 0.1 * jax.random.normal(keys[7], (MODEL_DIM,), jnp.float32), 0.5, 1.5).astype(jnp.bfloat16)
    w_router = bell_draw(keys[8], (MODEL_DIM, EXPERTS), (4 * MODEL_DIM) ** -0.5, 0.078125, ((0, 32),))
    expert_gate = bell_draw(keys[9], (EXPERTS, MODEL_DIM, FF), MODEL_DIM ** -0.5, 0.15625, ((0, 16), (1, 2)))
    expert_up = bell_draw(keys[10], (EXPERTS, MODEL_DIM, FF), MODEL_DIM ** -0.5, 0.15625, ((0, 16), (1, 2)))
    expert_down = bell_draw(keys[11], (EXPERTS, FF, MODEL_DIM), (FF // 8) ** -0.5, 0.75, ((0, 16), (2, 2)))
    routes = choose_distinct(keys[12], TOKEN_TOTAL, EXPERTS, TOPK, 8192)
    slot_order = jax.vmap(lambda own: jax.random.permutation(own, TOK_DEV * TOPK))(jax.random.split(keys[13], (N_DP * N_EXPERT))).reshape((N_DP * N_EXPERT, TOK_DEV * TOPK)).astype(jnp.int32)
    doc_lengths = jax.vmap(lambda own: ragged(own, DOCS, GROUP_TOK, MOST_LEN, 2))(jax.random.split(keys[14], N_EXPERT)).reshape((N_EXPERT, DOCS)).astype(jnp.int32)
    deal = draw_deal(jax.random.fold_in(keys[16], 71), 0)
    return {"tokens": tokens, "cotangent": cotangent, "norm_attn": norm_attn, "w_query": w_query, "key_projection": key_projection, "value_projection": value_projection, "w_out": w_out, "norm_ffn": norm_ffn, "w_router": w_router, "expert_gate": expert_gate, "expert_up": expert_up, "expert_down": expert_down, "routes": routes, "slot_order": slot_order, "doc_lengths": doc_lengths, "deal": deal}


NORM_EPS = 1e-05
MASK_FILL = -1e+30
ROPE_BASE = 10000.0

@jax.custom_vjp
def lower_output(v):
    return lax.optimization_barrier(v.astype(jnp.bfloat16)).astype(jnp.float32)

@jax.custom_vjp
def lower_backward(v):
    return v

def low_keep(v):
    return (lower_output(v), None)

def low_pass(kept, grad):
    return (grad,)

def back_keep(v):
    return (v, None)

def back_low(kept, grad):
    return (lower_output(grad),)
lower_output.defvjp(low_keep, low_pass)
lower_backward.defvjp(back_keep, back_low)

def matrix_product(left_side, right_side):
    return jnp.dot(left_side, right_side, precision=lax.Precision.HIGHEST, preferred_element_type=jnp.float32)

def rms_scaled(values, gain):
    return values * lax.rsqrt(lax.optimization_barrier(jnp.mean(values * values, axis=-1, keepdims=True)) + NORM_EPS) * gain

def doc_layout(lengths, places):
    doc_ends = jnp.cumsum(lengths)
    doc_starts = doc_ends - lengths
    doc_ids = lax.optimization_barrier(jnp.sum((places[:, None] >= doc_ends[None, :]).astype(jnp.int32), axis=1))
    member = doc_ids[:, None] == jnp.arange(lengths.shape[0], dtype=jnp.int32)[None, :]
    offsets = places - lax.optimization_barrier(jnp.sum(jnp.where(member, doc_starts[None, :], 0), axis=1))
    return (doc_ids.astype(jnp.int32), offsets.astype(jnp.int32))

def rope_tables(offsets, head_size):
    half_size = head_size // 2
    frequency = ROPE_BASE ** (-2.0 * jnp.arange(half_size, dtype=jnp.float32) / head_size)
    angles = offsets.astype(jnp.float32)[:, None] * frequency[None, :]
    return (jnp.cos(angles), jnp.sin(angles))

def apply_rotation(values, cosine_lookup, sine_lookup):
    half_size = values.shape[-1] // 2
    first_half = values[..., :half_size]
    second = values[..., half_size:]
    cos_rows = cosine_lookup[:, None, :]
    sin_rows = sine_lookup[:, None, :]
    return jnp.concatenate([first_half * cos_rows - second * sin_rows, second * cos_rows + first_half * sin_rows], axis=-1)

def assign_slots(routes, take_order, experts, capacity):
    count_of_rows, top_count = routes.shape
    flat_routes = routes.reshape(-1)
    chosen = flat_routes[take_order]
    expert_hits = (chosen[:, None] == jnp.arange(experts, dtype=jnp.int32)[None, :]).astype(jnp.int32)
    slot_rank = lax.optimization_barrier(jnp.sum(jnp.cumsum(expert_hits, axis=0) * expert_hits, axis=1)) - 1
    slot_index = jnp.where(slot_rank < capacity, chosen * capacity + slot_rank, experts * capacity).astype(jnp.int32)
    pair_slot = jnp.zeros((flat_routes.shape[0],), jnp.int32).at[take_order].set(slot_index)
    slot_token = jnp.full((experts * capacity + 1,), count_of_rows, jnp.int32).at[slot_index].set((take_order // top_count).astype(jnp.int32))
    return (pair_slot, slot_token[:experts * capacity])

def attend(operands):
    query_rows, key_matrix_rows, value_matrix_rows, doc_ids, places = operands
    count_of_rows = query_rows.shape[0]
    visible = (doc_ids[:, None] == doc_ids[None, :]) & (places[:, None] >= places[None, :])
    query_grouped = query_rows.reshape(count_of_rows, KEY_VALUE_HEADS, QUERY_HEADS // KEY_VALUE_HEADS, HEAD_DIM)
    scores = jnp.einsum('qgrd,kgd->grqk', query_grouped, key_matrix_rows, precision=lax.Precision.HIGHEST) * HEAD_DIM ** (-0.5)
    scores = lower_backward(jnp.where(visible[None, None], scores, MASK_FILL))
    probs = jax.nn.softmax(scores, axis=-1)
    attended = jnp.einsum('grqk,kgd->qgrd', lower_output(probs), value_matrix_rows, precision=lax.Precision.HIGHEST)
    return attended.reshape(count_of_rows, QUERY_HEADS * HEAD_DIM)

def reference(tokens, cotangent, norm_attn, w_query, key_projection, value_projection, w_out, norm_ffn, w_router, expert_gate, expert_up, expert_down, routes, slot_order, doc_lengths, deal):
    device_count = N_DP * N_EXPERT
    group_rows = N_DP * TOK_DEV
    routes_block = routes.reshape(device_count, TOK_DEV, TOPK)
    pair_slot, slot_token = jax.vmap(partial(assign_slots, experts=EXPERTS, capacity=CAP))(routes_block, slot_order)
    deal_group = jnp.swapaxes(deal, 0, 1).reshape(N_EXPERT, group_rows)
    doc_ids, offsets = jax.vmap(doc_layout)(doc_lengths, deal_group)

    def to_groups(values):
        shaped = values.reshape((N_DP, N_EXPERT, TOK_DEV) + values.shape[1:])
        return jnp.swapaxes(shaped, 0, 1).reshape((N_EXPERT, group_rows) + values.shape[1:])

    def from_groups(values):
        shaped = values.reshape((N_EXPERT, N_DP, TOK_DEV) + values.shape[2:])
        return jnp.swapaxes(shaped, 0, 1).reshape((TOKEN_TOTAL,) + values.shape[2:])
    cosine_lookup, sine_lookup = rope_tables(from_groups(offsets), HEAD_DIM)
    device_base = jnp.arange(device_count, dtype=jnp.int32)[:, None]
    token_index = jnp.where(slot_token == TOK_DEV, TOKEN_TOTAL, slot_token + device_base * TOK_DEV)
    expert_rows = token_index.reshape(device_count, EXPERTS, CAP).transpose(1, 0, 2).reshape(EXPERTS, device_count * CAP)
    flat_slot = jnp.where(pair_slot == EXPERTS * CAP, EXPERTS * device_count * CAP, pair_slot // CAP * (device_count * CAP) + device_base * CAP + pair_slot % CAP).astype(jnp.int32)
    route_hits = (routes[:, :, None] == jnp.arange(EXPERTS, dtype=jnp.int32)[None, None, :]).astype(jnp.float32)

    def forward(inputs, gain_attn, full_query, gathered_key, gathered_value, full_out, gain_ffn, full_router, gate_all, up_all, down_all):
        attention_input = lower_output(rms_scaled(inputs, gain_attn))
        query_rows = lower_output(apply_rotation(lower_backward(matrix_product(attention_input, full_query)).reshape(TOKEN_TOTAL, QUERY_HEADS, HEAD_DIM), cosine_lookup, sine_lookup))
        key_matrix_rows = lower_output(apply_rotation(lower_backward(matrix_product(attention_input, gathered_key)).reshape(TOKEN_TOTAL, KEY_VALUE_HEADS, HEAD_DIM), cosine_lookup, sine_lookup))
        value_matrix_rows = lower_output(lower_backward(matrix_product(attention_input, gathered_value))).reshape(TOKEN_TOTAL, KEY_VALUE_HEADS, HEAD_DIM)
        attended = lax.map(jax.checkpoint(attend), (to_groups(query_rows), to_groups(key_matrix_rows), to_groups(value_matrix_rows), doc_ids, deal_group))
        attended = lower_output(lower_backward(from_groups(attended)))
        hidden_state = inputs + lower_backward(matrix_product(attended, full_out))
        ffn_in = lower_output(rms_scaled(hidden_state, gain_ffn))
        logits = lower_backward(matrix_product(ffn_in, full_router))
        chosen = lax.optimization_barrier(jnp.sum(route_hits * logits[:, None, :], axis=-1))
        gate_values = jax.nn.softmax(chosen, axis=-1)
        padded_in = jnp.concatenate([ffn_in, jnp.zeros((1, MODEL_DIM), jnp.float32)], axis=0)

        def expert_pass(operands):
            index_row, gate_w, up_w, down_w = operands
            slot_rows = lower_backward(padded_in[index_row])
            gate_pre = lower_backward(matrix_product(slot_rows, gate_w))
            up_pre = lower_backward(matrix_product(slot_rows, up_w))
            hidden = lower_output(jax.nn.silu(gate_pre) * up_pre)
            return lower_output(lower_backward(matrix_product(hidden, down_w)))
        results = lax.map(jax.checkpoint(expert_pass), (expert_rows, gate_all, up_all, down_all)).reshape(-1, MODEL_DIM)
        padded_out = jnp.concatenate([results, jnp.zeros((1, MODEL_DIM), jnp.float32)], axis=0)

        def combine(operands):
            slot_grid, gate_rows = operands
            summed = jnp.zeros((TOK_DEV, MODEL_DIM), jnp.float32)
            for column in range(TOPK):
                summed = summed + gate_rows[:, column:column + 1] * padded_out[slot_grid[:, column]]
            return summed
        mixture = lax.map(jax.checkpoint(combine), (flat_slot.reshape(device_count, TOK_DEV, TOPK), gate_values.reshape(device_count, TOK_DEV, TOPK)))
        return hidden_state + mixture.reshape(TOKEN_TOTAL, MODEL_DIM)
    primal = (tokens.astype(jnp.float32), norm_attn.astype(jnp.float32), w_query.astype(jnp.float32), key_projection.astype(jnp.float32), value_projection.astype(jnp.float32), w_out.astype(jnp.float32), norm_ffn.astype(jnp.float32), w_router.astype(jnp.float32), expert_gate.astype(jnp.float32), expert_up.astype(jnp.float32), expert_down.astype(jnp.float32))
    result, pull = jax.vjp(forward, *primal)
    gradient = pull(cotangent.astype(jnp.float32))
    return (result.astype(jnp.bfloat16), gradient[0].astype(jnp.bfloat16), gradient[1], gradient[2], gradient[3], gradient[4], gradient[5], gradient[6], gradient[7], gradient[8], gradient[9], gradient[10])
```

```python
import functools
import math

import jax
import jax.numpy as jnp
from jax import lax
from jax.experimental import pallas as pl
from jax.experimental.pallas import tpu as pltpu
from jax.sharding import PartitionSpec as P

HEAD_DIM = 64


NORM_EPS = 1e-05
MASK_FILL = -1e30
ROPE_BASE = 10000.0


def dot_plain(left_side, right_side):
    return jnp.dot(left_side, right_side, preferred_element_type=jnp.float32)


def dot_last(left_side, right_side):
    return lax.dot_general(
        left_side, right_side, (((1,), (1,)), ((), ())), preferred_element_type=jnp.float32
    )


def dot_first(left_side, right_side):
    return lax.dot_general(
        left_side, right_side, (((0,), (0,)), ((), ())), preferred_element_type=jnp.float32
    )


def doc_layout(lengths, places):
    doc_ends = jnp.cumsum(lengths)
    doc_starts = doc_ends - lengths
    doc_ids = jnp.sum((places[:, None] >= doc_ends[None, :]).astype(jnp.int32), axis=1)
    member = doc_ids[:, None] == jnp.arange(lengths.shape[0], dtype=jnp.int32)[None, :]
    offsets = places - jnp.sum(jnp.where(member, doc_starts[None, :], 0), axis=1)
    return (doc_ids, offsets)


def rope_tables(offsets, head_size):
    half_size = head_size // 2
    frequency = ROPE_BASE ** (-2.0 * jnp.arange(half_size, dtype=jnp.float32) / head_size)
    angles = offsets.astype(jnp.float32)[:, None] * frequency[None, :]
    return (jnp.cos(angles), jnp.sin(angles))


def apply_rotation(values, cosine_lookup, sine_lookup):
    half_size = values.shape[-1] // 2
    first_half = values[..., :half_size]
    second = values[..., half_size:]
    cos_rows = cosine_lookup[:, None, :]
    sin_rows = sine_lookup[:, None, :]
    return jnp.concatenate(
        [first_half * cos_rows - second * sin_rows, second * cos_rows + first_half * sin_rows],
        axis=-1,
    )


def unrotate(gradient, cosine_lookup, sine_lookup):
    half_size = gradient.shape[-1] // 2
    first_half = gradient[..., :half_size]
    second = gradient[..., half_size:]
    cos_rows = cosine_lookup[:, None, :]
    sin_rows = sine_lookup[:, None, :]
    return jnp.concatenate(
        [first_half * cos_rows + second * sin_rows, second * cos_rows - first_half * sin_rows],
        axis=-1,
    )


def assign_slots(routes, take_order, experts, capacity):
    count_of_rows, top_count = routes.shape
    flat_routes = routes.reshape(-1)
    chosen = flat_routes[take_order]
    expert_hits = (chosen[:, None] == jnp.arange(experts, dtype=jnp.int32)[None, :]).astype(
        jnp.int32
    )
    slot_rank = jnp.sum(jnp.cumsum(expert_hits, axis=0) * expert_hits, axis=1) - 1
    slot_index = jnp.where(slot_rank < capacity, chosen * capacity + slot_rank, experts * capacity)
    pair_slot = jnp.zeros((flat_routes.shape[0],), jnp.int32).at[take_order].set(slot_index)
    slot_token = (
        jnp.full((experts * capacity + 1,), count_of_rows, jnp.int32)
        .at[slot_index]
        .set(take_order // top_count)
    )
    return (pair_slot, slot_token[: experts * capacity])


MESH = pl.DeviceIdType.MESH
BF16 = jnp.bfloat16
F32 = jnp.float32
NAR = 128


def remote(src, dst, send_sem, recv_sem, device):
    return pltpu.make_async_remote_copy(
        src_ref=src,
        dst_ref=dst,
        send_sem=send_sem,
        recv_sem=recv_sem,
        device_id=device,
        device_id_type=MESH,
    )


class Place:
    def __init__(self):
        self.i = lax.axis_index("dp")
        self.e = lax.axis_index("expert")
        self.a = self.e // 4
        self.bc = self.e % 4
        self.y = self.bc // 2
        self.c = self.bc % 2

    def over_x(self):
        return (1 - self.i, self.e)

    def over_y(self):
        return (self.i, self.e + 2 - 4 * self.y)

    def over_core(self):
        return (self.i, self.e + 1 - 2 * self.c)

    def order(self, k):
        turn = (1 - 2 * k) * (1 - k // 2)
        inner = (self.a * (3 - self.a)) // 2
        half = self.a // 2
        step = k + inner * turn
        return step + half * (3 - 2 * step)

    def barrier(self):
        sem = pltpu.get_barrier_semaphore()
        peers = [self.over_x(), self.over_y(), self.over_core()]
        for shift in range(1, 4):
            peers.append((self.i, ((self.a + shift) % 4) * 4 + self.bc))
        for peer in peers:
            pl.semaphore_signal(sem, inc=1, device_id=peer, device_id_type=MESH)
        pl.semaphore_wait(sem, len(peers))


class Gather:
    SENDS = 20
    RECVS = 16

    def __init__(self, place, view, sends, recvs):
        self.p, self.view, self.sends, self.recvs = place, view, sends, recvs

    def copy(self, block, slot, device):
        ref = self.view(block)
        return remote(ref, ref, self.sends.at[slot], self.recvs.at[block], device)

    def right(self, a1):
        return self.copy(a1 * 4 + self.p.bc, a1, (self.p.i, self.p.e + 4))

    def left(self, a1):
        return self.copy(a1 * 4 + self.p.bc, 4 + a1, (self.p.i, self.p.e - 4))

    def across(self, a1):
        return self.copy(a1 * 4 + self.p.bc, 8 + a1, self.p.over_y())

    def core(self, a1, y1):
        return self.copy(a1 * 4 + y1 * 2 + self.p.c, 12 + a1 * 2 + y1, self.p.over_core())

    def landed(self, block):
        self.copy(block, 0, self.p.over_core()).wait_recv()

    def begin(self):
        p = self.p

        @pl.when(p.a < 3)
        def _():
            self.right(p.a).start()

        @pl.when(p.a > 0)
        def _():
            self.left(p.a).start()

        self.across(p.a).start()
        self.core(p.a, p.y).start()

    def along(self, k):
        p = self.p
        a1 = p.order(k)
        self.landed(a1 * 4 + p.bc)

        @pl.when((a1 < p.a) & (p.a < 3))
        def _():
            self.right(a1).start()

        @pl.when((a1 > p.a) & (p.a > 0))
        def _():
            self.left(a1).start()

        self.across(a1).start()
        self.core(a1, p.y).start()

    def cross(self, k):
        p = self.p
        a1 = p.order(k)
        self.landed(a1 * 4 + (1 - p.y) * 2 + p.c)
        self.core(a1, 1 - p.y).start()

    def join(self, k):
        p = self.p
        a1 = p.order(k)
        self.landed(a1 * 4 + (1 - p.c))
        self.landed(a1 * 4 + 2 + (1 - p.c))

    def drain(self):
        p = self.p
        for a1 in range(4):

            @pl.when((a1 <= p.a) & (p.a < 3))
            def _():
                self.right(a1).wait_send()

            @pl.when((a1 >= p.a) & (p.a > 0))
            def _():
                self.left(a1).wait_send()

            self.across(a1).wait_send()
            self.core(a1, 0).wait_send()
            self.core(a1, 1).wait_send()


class Scatter:
    SENDS = 16
    RECVS = 16

    def __init__(self, place, part, core_in, y_in, a_in, sends, recvs):
        self.p, self.part = place, part
        self.core_in, self.y_in, self.a_in = core_in, y_in, a_in
        self.sends, self.recvs = sends, recvs

    def to_core(self, a1, y1):
        p = self.p
        slot = a1 * 2 + y1
        return remote(
            self.part(a1, y1 * 2 + 1 - p.c),
            self.core_in.at[a1, y1],
            self.sends.at[slot],
            self.recvs.at[slot],
            p.over_core(),
        )

    def to_y(self, a1):
        p = self.p
        return remote(
            self.part(a1, (1 - p.y) * 2 + p.c),
            self.y_in.at[a1],
            self.sends.at[8 + a1],
            self.recvs.at[8 + a1],
            p.over_y(),
        )

    def to_a(self, a1):
        p = self.p
        return remote(
            self.part(a1, p.bc),
            self.a_in.at[p.a],
            self.sends.at[12 + a1],
            self.recvs.at[12 + p.a],
            (p.i, a1 * 4 + p.bc),
        )

    def from_a(self, a1):
        p = self.p
        return remote(
            self.a_in.at[a1],
            self.a_in.at[a1],
            self.sends.at[12 + a1],
            self.recvs.at[12 + a1],
            (p.i, a1 * 4 + p.bc),
        )

    def start(self, a1):
        self.to_core(a1, 0).start()
        self.to_core(a1, 1).start()

    def add(self, ref, other):
        ref[...] = (ref[...].astype(F32) + other[...].astype(F32)).astype(ref.dtype)

    def core(self, a1):
        p = self.p
        for y1 in range(2):
            self.to_core(a1, y1).wait_recv()
        self.add(self.part(a1, (1 - p.y) * 2 + p.c), self.core_in.at[a1, 1 - p.y])
        self.to_y(a1).start()
        self.add(self.part(a1, p.bc), self.core_in.at[a1, p.y])

    def cross(self, a1):
        p = self.p
        self.to_y(a1).wait_recv()
        self.add(self.part(a1, p.bc), self.y_in.at[a1])

        @pl.when(a1 != p.a)
        def _():
            self.to_a(a1).start()

        @pl.when(a1 == p.a)
        def _():
            self.a_in[a1] = self.part(a1, p.bc)[...]

    def finish(self):
        p = self.p
        for a1 in range(4):

            @pl.when(a1 != p.a)
            def _():
                self.from_a(a1).wait_recv()

    def total(self):
        return (
            self.a_in[0].astype(F32)
            + self.a_in[1].astype(F32)
            + self.a_in[2].astype(F32)
            + self.a_in[3].astype(F32)
        )

    def drain(self):
        p = self.p
        for a1 in range(4):
            self.to_core(a1, 0).wait_send()
            self.to_core(a1, 1).wait_send()
            self.to_y(a1).wait_send()

            @pl.when(a1 != p.a)
            def _():
                self.to_a(a1).wait_send()


def lane_iota(shape):
    return lax.broadcasted_iota(jnp.int32, shape, len(shape) - 1)


def swap_halves(values):
    lane = lane_iota(values.shape) % HEAD_DIM
    half = HEAD_DIM // 2
    return jnp.where(
        lane < half,
        pltpu.roll(values, values.shape[-1] - half, 1),
        pltpu.roll(values, half, 1),
    )


def split_heads(tile):
    low = lane_iota(tile.shape) < HEAD_DIM
    turned = pltpu.roll(tile, HEAD_DIM, 1)
    zero = jnp.zeros_like(tile)
    return (
        (jnp.where(low, tile, zero), jnp.where(low, zero, turned)),
        (jnp.where(low, turned, zero), jnp.where(low, zero, tile)),
    )


def inverse_rms(values):
    return lax.rsqrt(jnp.mean(values * values, axis=1, keepdims=True) + NORM_EPS)


def gain_rows(narrow, experts):
    shape = (16, narrow.shape[1])
    row = lax.broadcasted_iota(jnp.int32, shape, 0)
    pick = jnp.where(lane_iota(shape) == row + experts, 1.0, 0.0).astype(BF16)
    return dot_last(pick, narrow)


def front_kernel(
    tok, wp, wo, cot, eg, eu, ed, cs, sn, vis, hit, kept,
    w_out_all, wo_out_all, x_all, cot_all, egp, eup, edp, att_in, q_out, k_out, v_out, pr, att, hid, fe, gates,
    w_all, wo_all, klo, khi, vlo, vhi, opart, orecv,
    ga_s, ga_r, gb_s, gb_r, gw_s, gw_r, gc_s, gc_r, xs, xr, loc,
):
    p = Place()
    i, e = p.i, p.e
    rows = tok.shape[0]
    depth = wo.shape[0]
    plane = 16 * depth
    q_width = q_out.shape[1]
    k_width = k_out.shape[1]
    experts = 16
    wide = q_width + 2 * k_width

    def w_row(ip, block):
        return pl.ds(pl.multiple_of(ip * plane + block * depth, 16), depth)

    def row_block(ip):
        return pl.ds(pl.multiple_of(ip * rows, rows), rows)

    p.barrier()
    give_w = remote(wp.at[1 - i], w_all.at[w_row(i, e)], xs.at[0], xr.at[0], p.over_x())
    give_w.start()
    take_w = remote(w_all.at[w_row(1 - i, e)], w_all.at[w_row(1 - i, e)], xs.at[0], xr.at[0], p.over_x())
    give_x = remote(tok, x_all.at[i], xs.at[1], xr.at[1], p.over_x())
    take_x = remote(x_all.at[1 - i], x_all.at[1 - i], xs.at[1], xr.at[1], p.over_x())
    give_x.start()

    ga = Gather(p, lambda block: w_all.at[w_row(i, block)], ga_s, ga_r)
    gb = Gather(p, lambda block: w_all.at[w_row(1 - i, block)], gb_s, gb_r)
    gw = Gather(p, lambda block: wo_all.at[w_row(0, block)], gw_s, gw_r)
    gc = Gather(
        p, lambda block: cot_all.at[block // 4, pl.ds(pl.multiple_of((block % 4) * rows, rows), rows)], gc_s, gc_r
    )

    w_all[w_row(i, e), :] = wp[i]
    ga.begin()
    own_cot = pltpu.make_async_copy(cot, gc.view(e), loc.at[0])
    own_cot.start()
    wo_all[w_row(0, e), :] = wo[...]
    x_all[i] = tok[...]
    take_w.wait_recv()
    gb.begin()
    experts_out = [
        remote(src, dst, xs.at[2 + n], xr.at[2 + n], p.over_x())
        for n, (src, dst) in enumerate(((eg, egp), (eu, eup), (ed, edp)))
    ]
    for one in experts_out:
        one.start()
    for k in range(1, 4):
        ga.along(k)
        ga.cross(k - 1)
        gb.along(k)
        gb.cross(k - 1)
    gw.begin()
    ga.cross(3)
    gb.cross(3)
    own_cot.wait()
    for k in range(4):
        ga.join(k)
        gb.join(k)

    events = []
    for k in range(1, 4):
        events.append(functools.partial(gw.along, k))
        events.append(functools.partial(gw.cross, k - 1))
        if k == 1:
            events.append(gc.begin)
    events.append(functools.partial(gw.cross, 3))
    late = []
    for k in range(1, 4):
        late.append(functools.partial(gc.along, k))
        late.append(functools.partial(gc.cross, k - 1))
    late.append(functools.partial(gc.cross, 3))

    def serve():
        if events:
            events.pop(0)()

    w_save = pltpu.make_async_copy(w_all, w_out_all, loc.at[1])
    w_save.start()
    take_x.wait_recv()
    narrow = w_all[:, wide:]
    gains = gain_rows(narrow, experts)
    for ip in range(2):
        x = x_all[ip].astype(F32)
        att_in[ip * rows : (ip + 1) * rows, :] = (x * inverse_rms(x) * gains[0:1]).astype(BF16)
    serve()
    cos, sin = cs[...], sn[...]

    def rope(values):
        return values * cos + swap_halves(values) * sin

    for tile in range(wide // 256):
        lin = dot_plain(att_in[...], w_all[:, tile * 256 : (tile + 1) * 256])
        for half in range(2):
            col = tile * 256 + half * 128
            part = lin[:, half * 128 : (half + 1) * 128]
            if col < q_width:
                q_out[:, col : col + 128] = rope(part).astype(BF16)
            elif col < q_width + k_width:
                turned = rope(part)
                n = (col - q_width) // 128
                k_out[:, n * 128 : (n + 1) * 128] = turned.astype(BF16)
                for g, (low, high) in enumerate(split_heads(turned)):
                    klo[2 * n + g] = low.astype(BF16)
                    khi[2 * n + g] = high.astype(BF16)
            else:
                n = (col - q_width - k_width) // 128
                v_out[:, n * 128 : (n + 1) * 128] = part.astype(BF16)
                for g, (low, high) in enumerate(split_heads(part)):
                    vlo[2 * n + g] = low.astype(BF16)
                    vhi[2 * n + g] = high.astype(BF16)
    serve()
    ratio = q_width // k_width
    scale = HEAD_DIM**-0.5
    for pair in range(q_width // 128):
        lanes = slice(pair * 128, (pair + 1) * 128)
        out = None
        for side, (keys, vals) in enumerate(((klo, vlo), (khi, vhi))):
            head = 2 * pair + side
            g = head // ratio
            scores = dot_last(q_out[:, lanes], keys[g]) * scale
            scores = jnp.where(vis[...] > 0, scores, MASK_FILL)
            top = jnp.max(scores, axis=1, keepdims=True)
            grown = jnp.exp(scores - top)
            probs = grown / jnp.sum(grown, axis=1, keepdims=True)
            pr[head] = probs
            term = dot_plain(probs.astype(BF16), vals[g])
            out = term if out is None else out + term
        att[:, lanes] = out.astype(BF16)
        serve()
    while events:
        serve()
    for k in range(4):
        gw.join(k)
    wo_save = pltpu.make_async_copy(wo_all, wo_out_all, loc.at[2])
    wo_save.start()
    opart[...] = dot_plain(att[row_block(1 - i), :], wo_all[...]).astype(BF16)
    give_o = remote(opart, orecv, xs.at[5], xr.at[5], p.over_x())
    give_o.start()
    hid[...] = tok[...].astype(F32) + dot_plain(att[row_block(i), :], wo_all[...])
    late[0]()
    late[1]()
    give_o.wait_recv()
    state = hid[...] + orecv[...].astype(F32)
    hid[...] = state
    ffn_in = (state * inverse_rms(state) * gains[1:2]).astype(BF16)
    width = ffn_in.shape[1]
    fe[:, :width] = ffn_in
    logits = dot_plain(ffn_in, narrow)
    chosen = hit[...] > 0
    logits = jnp.where(chosen, logits, MASK_FILL)
    grown = jnp.where(chosen, jnp.exp(logits - jnp.max(logits, axis=1, keepdims=True)), 0.0)
    gate = grown / jnp.sum(grown, axis=1, keepdims=True)
    gates[...] = gate
    gate = gate * kept[...]
    gate_high = gate.astype(BF16).astype(F32)
    fe[:, width:] = (gate_high + pltpu.roll(gate - gate_high, experts, 1)).astype(BF16)
    for one in late[2:]:
        one()
    for k in range(4):
        gc.join(k)
    for one in experts_out:
        one.wait()
    for one in (give_w, give_x, give_o):
        one.wait_send()
    for g in (ga, gb, gw, gc):
        g.drain()
    w_save.wait()
    wo_save.wait()


def middle_kernel(
    fe, cot_all, eg, eu, ed, egp, eup, edp,
    total, mixp, og_own, ou_own, od_own, og_peer, ou_peer, od_peer,
    f_all, part, core_in, y_in, a_in, wg, wu, wd, cot, og, h1, h2, hidden, gp, up, mix, dg, du, dd,
    ga_s, ga_r, sc_s, sc_r, loc, cot_sem, mix_sem,
):
    p = Place()
    i, e = p.i, p.e
    rows = fe.shape[0]
    width = og.shape[1]
    half = width // 2
    experts = 16
    f_all[p.a, pl.ds(pl.multiple_of(p.bc * rows, rows), rows), :] = fe[...]
    p.barrier()
    g = Gather(p, lambda block: f_all.at[block // 4, pl.ds(pl.multiple_of((block % 4) * rows, rows), rows)], ga_s, ga_r)
    g.begin()

    def half_rows(ip):
        return pl.ds(pl.multiple_of(ip * half, half), half)

    loads = []
    for ip, (a1, a2, a3) in ((i, (eg, eu, ed)), (1 - i, (egp, eup, edp))):
        loads.append((a1, wg.at[half_rows(ip)]))
        loads.append((a2, wu.at[half_rows(ip)]))
        loads.append((a3, wd.at[:, half_rows(ip)]))
    loads = [pltpu.make_async_copy(src, dst, loc.at[n]) for n, (src, dst) in enumerate(loads)]
    for one in loads:
        one.start()

    def fetch(k):
        a1 = p.order(k)
        return pltpu.make_async_copy(cot_all.at[a1], cot.at[k % 2], cot_sem.at[k % 2])

    def store_mix(a1):
        return pltpu.make_async_copy(mix, mixp.at[a1], mix_sem)

    fetch(0).start()
    for ref in (dg, du, dd):
        ref[...] = jnp.zeros_like(ref)
    g.cross(0)
    for one in loads:
        one.wait()
    sc = Scatter(
        p,
        lambda a1, b1: part.at[a1, pl.ds(pl.multiple_of(b1 * rows, rows), rows)],
        core_in, y_in, a_in, sc_s, sc_r,
    )

    @pl.loop(0, 4)
    def _(k):
        a1 = p.order(k)
        more = k < 3

        @pl.when(more)
        def _():
            fetch(k + 1).start()

        g.join(k)
        f = f_all.at[a1]
        h1[...] = dot_plain(f[:, :width], wg[...])
        h2[...] = dot_plain(f[:, :width], wu[...])

        @pl.when(more)
        def _():
            g.along(k + 1)

        fetch(k).wait()
        c = cot.at[k % 2]
        meta = f[:, width:].astype(F32)
        lane = lane_iota(meta.shape)
        gate = jnp.sum(jnp.where((lane == e) | (lane == e + experts), meta, 0.0), axis=1, keepdims=True)
        og[...] = (gate * c[...].astype(F32)).astype(BF16)
        hg = dot_last(og[...], wd[...])
        s = jax.nn.sigmoid(h1[...])
        gp[...] = (hg * h2[...] * s * (1.0 + h1[...] * (1.0 - s))).astype(BF16)
        up[...] = (hg * (h1[...] * s)).astype(BF16)
        hidden[...] = (h1[...] * s * h2[...]).astype(BF16)

        @pl.loop(0, 3)
        def _(n):
            cols = pl.ds(pl.multiple_of(n * 512, 512), 512)
            part[a1, :, cols] = (dot_last(gp[...], wg[cols, :]) + dot_last(up[...], wu[cols, :])).astype(BF16)

        @pl.when(k > 0)
        def _():
            store_mix(p.order(k - 1)).wait()

        def project(n, gate_grad):
            cols = pl.ds(pl.multiple_of(n * 512, 512), 512)
            out = dot_plain(hidden[...], wd[:, cols]).astype(BF16).astype(F32)
            mix[:, cols] = (gate * out).astype(BF16)
            return gate_grad + jnp.sum(out * c[:, cols].astype(F32), axis=1, keepdims=True)

        gate_grad = lax.fori_loop(0, 3, project, jnp.zeros((4 * rows, 1), F32))
        store_mix(a1).start()
        high = gate_grad.astype(BF16).astype(F32)
        part[a1, :, width:] = jnp.where(
            lane == e, high, jnp.where(lane == e + experts, gate_grad - high, 0.0)
        ).astype(BF16)
        sc.start(a1)

        @pl.when(more)
        def _():
            g.cross(k + 1)

        @pl.loop(0, 3)
        def _(n):
            cols = pl.ds(pl.multiple_of(n * 512, 512), 512)
            dg[cols, :] += dot_first(f[:, cols], gp[...])
            du[cols, :] += dot_first(f[:, cols], up[...])
            dd[:, cols] += dot_first(hidden[...], og[:, cols])

        sc.core(a1)

        @pl.when(k > 0)
        def _():
            sc.cross(p.order(k - 1))

    outs = [
        (dg.at[half_rows(i)], og_own),
        (du.at[half_rows(i)], ou_own),
        (dd.at[:, half_rows(i)], od_own),
    ]
    outs = [pltpu.make_async_copy(src, dst, loc.at[n]) for n, (src, dst) in enumerate(outs)]
    for one in outs:
        one.start()
    og_peer[...] = dg[half_rows(1 - i), :].astype(BF16)
    ou_peer[...] = du[half_rows(1 - i), :].astype(BF16)
    od_peer[...] = dd[:, half_rows(1 - i)].astype(BF16)
    sc.cross(p.order(3))
    sc.finish()
    total[...] = sc.total()
    store_mix(p.order(3)).wait()
    for one in outs:
        one.wait()
    g.drain()
    sc.drain()


def back_kernel(
    total, mixp, og_peer, ou_peer, od_peer, w_in, wo_in, x_all, att_in, q, kk, vv, pr, att, hid, gates, kept, cot, cs, sn,
    out, tok_grad, dq_out, dk_out, dv_out, dwo_out, gains_out, egr, eur, edr,
    w_all, wo_all, klo, khi, vlo, vhi, bg, ag, dq, dk, dv, apart, asend, arecv, state,
    mpart, m_core, m_y, m_a, opart, o_core, o_y, o_a, wpart, w_core, w_y, w_a, wsend, wrecv,
    sm_s, sm_r, so_s, so_r, sw_s, sw_r, xs, xr, loc,
):
    p = Place()
    i, e = p.i, p.e
    rows = cot.shape[0]
    width = cot.shape[1]
    q_width, k_width = q.shape[1], kk.shape[1]
    wide = q_width + 2 * k_width
    depth = dq_out.shape[0]
    plane = 16 * depth
    experts = 16
    ratio = q_width // k_width
    scale = HEAD_DIM**-0.5

    def row_block(ip):
        return pl.ds(pl.multiple_of(ip * rows, rows), rows)

    load_mix = [pltpu.make_async_copy(mixp.at[a1], mpart.at[a1], loc.at[2 + a1]) for a1 in range(4)]
    for one in load_mix:
        one.start()
    load_w = pltpu.make_async_copy(w_in, w_all, loc.at[0])
    load_wo = pltpu.make_async_copy(wo_in, wo_all, loc.at[1])
    load_w.start()
    load_wo.start()
    p.barrier()
    sm = Scatter(p, lambda a1, b1: mpart.at[a1, row_block(b1)], m_core, m_y, m_a, sm_s, sm_r)
    so = Scatter(
        p,
        lambda a1, b1: opart.at[pl.ds(pl.multiple_of((a1 * 4 + b1) * depth, 16), depth)],
        o_core, o_y, o_a, so_s, so_r,
    )
    sw = Scatter(
        p,
        lambda a1, b1: wpart.at[:, pl.ds(pl.multiple_of((a1 * 4 + b1) * depth, 16), depth)],
        w_core, w_y, w_a, sw_s, sw_r,
    )
    for a1 in range(4):
        load_mix[a1].wait()
        sm.start(a1)

    load_w.wait()
    narrow = w_all[:, wide:]
    gains = gain_rows(narrow, experts)
    lane = lane_iota((rows, NAR))
    meta = total[:, width:]
    gate_grad = (meta + pltpu.roll(meta, NAR - experts, 1)) * kept[...]
    gate = gates[...]
    logit_grad = (gate * (gate_grad - jnp.sum(gate * gate_grad, axis=1, keepdims=True))).astype(BF16)
    ffn_grad = total[:, :width] + dot_last(logit_grad, narrow)
    hidden = hid[...]
    r2 = inverse_rms(hidden)
    n2 = hidden * r2
    ffn_in = (n2 * gains[1:2]).astype(BF16)
    d2 = ffn_grad * gains[1:2]
    state[...] = cot[...].astype(F32) + r2 * (d2 - n2 * jnp.mean(d2 * n2, axis=1, keepdims=True))
    branch = state[...].astype(BF16)
    bg[row_block(i), :] = branch
    give_b = remote(bg.at[row_block(i)], bg.at[row_block(i)], xs.at[0], xr.at[0], p.over_x())
    take_b = remote(bg.at[row_block(1 - i)], bg.at[row_block(1 - i)], xs.at[0], xr.at[0], p.over_x())
    give_b.start()
    ones = jnp.where(lane == experts + 1, 1.0, 0.0).astype(BF16)
    gain_term = ffn_grad * n2
    gain_high = gain_term.astype(BF16)
    gain_low = (gain_term - gain_high.astype(F32)).astype(BF16)
    small = dot_first(ffn_in, logit_grad) + dot_first(gain_high, ones) + dot_first(gain_low, ones)
    small_ref = apart
    small_ref[...] = small
    for a1 in range(4):
        sm.core(a1)

    for n in range(k_width // 128):
        for (tile, los, his) in ((kk, klo, khi), (vv, vlo, vhi)):
            for g, (low, high) in enumerate(split_heads(tile[:, n * 128 : (n + 1) * 128].astype(F32))):
                los[2 * n + g] = low.astype(BF16)
                his[2 * n + g] = high.astype(BF16)
    dk[...] = jnp.zeros_like(dk)
    dv[...] = jnp.zeros_like(dv)
    cos, sin = cs[...], sn[...]
    low_lane = lane_iota((2 * rows, 128)) < HEAD_DIM

    def unrope(values):
        return values * cos - swap_halves(values) * sin

    load_wo.wait()
    take_b.wait_recv()
    experts_out = [
        remote(src, dst, xs.at[2 + n], xr.at[2 + n], p.over_x())
        for n, (src, dst) in enumerate(((og_peer, egr), (ou_peer, eur), (od_peer, edr)))
    ]
    for one in experts_out:
        one.start()
    for n in range(q_width // 256):
        lanes = slice(n * 256, (n + 1) * 256)
        ag[:, lanes] = dot_last(bg[...], wo_all[lanes, :]).astype(BF16)
    for n in range(q_width // 256):
        lanes = slice(n * 256, (n + 1) * 256)
        opart[lanes, :] = dot_first(att[:, lanes], bg[...]).astype(BF16)
    for a1 in range(4):
        so.start(a1)
    for a1 in range(4):
        sm.cross(a1)

    for pair in range(q_width // 128):
        lanes = slice(pair * 128, (pair + 1) * 128)
        grad_in = ag[:, lanes]
        q_pair = q[:, lanes]
        q_grad = None
        for side, (keys, vals) in enumerate(((klo, vlo), (khi, vhi))):
            head = 2 * pair + side
            g = head // ratio
            probs = pr[head]
            prob_grad = dot_last(grad_in, vals[g])
            shift = jnp.sum(probs * prob_grad, axis=1, keepdims=True)
            score_grad = (probs * (prob_grad - shift)).astype(BF16)
            term = dot_plain(score_grad, keys[g])
            q_grad = term if q_grad is None else q_grad + term
            mine = low_lane if side == 0 else jnp.logical_not(low_lane)
            k_term = jnp.where(mine, dot_first(score_grad, q_pair), 0.0)
            v_term = jnp.where(mine, dot_first(probs.astype(BF16), grad_in), 0.0)
            if g % 2 != side:
                k_term = pltpu.roll(k_term, HEAD_DIM, 1)
                v_term = pltpu.roll(v_term, HEAD_DIM, 1)
            tile = slice((g // 2) * 128, (g // 2 + 1) * 128)
            dk[:, tile] += k_term
            dv[:, tile] += v_term
        dq[:, lanes] = unrope(scale * q_grad).astype(BF16)
        if pair < 4:
            so.core(pair)
    for n in range(k_width // 128):
        lanes = slice(n * 128, (n + 1) * 128)
        dq[:, q_width + n * 128 : q_width + (n + 1) * 128] = unrope(scale * dk[:, lanes]).astype(BF16)
        dq[:, q_width + k_width + n * 128 : q_width + k_width + (n + 1) * 128] = dv[:, lanes].astype(BF16)
    for a1 in range(4):
        so.cross(a1)

    back = [None, None]
    for first in range(2):
        ip = 1 - i if first == 0 else i
        part = dot_last(dq[row_block(ip), :], w_all[:, :wide])
        x = x_all[ip].astype(F32)
        term = part * (x * inverse_rms(x))
        high = term.astype(BF16)
        low = (term - high.astype(F32)).astype(BF16)
        pick = jnp.where(lane == experts, 1.0, 0.0).astype(BF16)
        small_ref[...] += dot_first(high, pick) + dot_first(low, pick)
        if first == 0:
            asend[...] = part.astype(BF16)
            give_a = remote(asend, arecv, xs.at[1], xr.at[1], p.over_x())
            give_a.start()
        else:
            back = part
    for ip in range(2):
        for n in range(plane // 256):
            block = slice(n * 256, (n + 1) * 256)
            lanes = slice(ip * plane + n * 256, ip * plane + (n + 1) * 256)
            wpart[ip, block, :wide] = dot_first(att_in[:, lanes], dq[...]).astype(BF16)
        wpart[ip, :, wide:] = small_ref[ip * plane : (ip + 1) * plane, :].astype(BF16)
    for a1 in range(4):
        sw.start(a1)
    give_a.wait_recv()
    attn_grad = back + arecv[...].astype(F32)
    x = x_all[i].astype(F32)
    r1 = inverse_rms(x)
    n1 = x * r1
    d1 = attn_grad * gains[0:1]
    tok_grad[...] = (state[...] + r1 * (d1 - n1 * jnp.mean(d1 * n1, axis=1, keepdims=True))).astype(BF16)
    for a1 in range(4):
        sw.core(a1)
    sm.finish()
    out[...] = (hidden + sm.total()).astype(BF16)
    so.finish()
    dwo_out[...] = so.total()
    for a1 in range(4):
        sw.cross(a1)
    sw.finish()
    summed = sw.total()
    wsend[...] = summed
    give_s = remote(wsend.at[1 - i], wrecv, xs.at[5], xr.at[5], p.over_x())
    give_s.start()

    def place_half(ip, values):
        dq_out[:, pl.ds(pl.multiple_of(ip * q_width, 128), q_width)] = values[:, :q_width]
        dk_out[:, pl.ds(pl.multiple_of(ip * k_width, 128), k_width)] = values[:, q_width : q_width + k_width]
        dv_out[:, pl.ds(pl.multiple_of(ip * k_width, 128), k_width)] = values[:, q_width + k_width : wide]

    mine = wsend[i]
    place_half(i, mine)
    give_s.wait_recv()
    theirs = wrecv[...]
    place_half(1 - i, theirs)
    gains_out[...] = mine[:, wide:] + theirs[:, wide:]
    for one in experts_out:
        one.wait()
    for one in (give_b, give_a, give_s):
        one.wait_send()
    for s in (sm, so, sw):
        s.drain()


def paired_body(
    tokens, cotangent, norm_attn, w_query, key_projection, value_projection, w_out, norm_ffn, w_router,
    expert_gate, expert_up, expert_down, routes, slot_order, doc_lengths, deal,
):
    rows, width = tokens.shape
    depth = w_query.shape[0]
    top_count = routes.shape[1]
    experts = 16
    capacity = 9 * rows * top_count // (8 * experts)
    q_width = w_query.shape[1] // 2
    k_width = key_projection.shape[1] // 2
    wide = q_width + 2 * k_width
    ff = expert_gate.shape[2]
    half = width // 2
    vm = pl.BlockSpec(memory_space=pltpu.VMEM)
    hb = pl.BlockSpec(memory_space=pl.ANY)

    def shaped(*dims, dtype=BF16):
        return jax.ShapeDtypeStruct(dims, dtype)

    def sems(n):
        return pltpu.SemaphoreType.DMA((n,))

    narrow = jnp.concatenate(
        [w_router, norm_attn[:, None], norm_ffn[:, None], jnp.zeros((depth, NAR - experts - 2), BF16)], axis=1
    )
    packed = jnp.stack(
        [
            jnp.concatenate(
                [
                    w_query[:, h * q_width : (h + 1) * q_width],
                    key_projection[:, h * k_width : (h + 1) * k_width],
                    value_projection[:, h * k_width : (h + 1) * k_width],
                    narrow,
                ],
                axis=1,
            )
            for h in range(2)
        ]
    )
    group_places = deal[:, 0, :].reshape(-1)
    group_docs, group_offsets = doc_layout(doc_lengths[0], group_places)
    cosine, sine = rope_tables(group_offsets, HEAD_DIM)
    cs = jnp.concatenate([cosine] * 4, axis=1)
    sn = jnp.concatenate([-sine, sine, -sine, sine], axis=1)
    vis = (
        (group_docs[:, None] == group_docs[None, :]) & (group_places[:, None] >= group_places[None, :])
    ).astype(F32)
    pairs = rows * top_count
    number = jnp.arange(pairs, dtype=jnp.int32)
    taken_at = jnp.sum(
        jnp.where(slot_order[0][None, :] == number[:, None], number[None, :], 0), axis=1
    ).reshape(rows, top_count)
    names = jnp.arange(experts, dtype=jnp.int32)
    match = routes[:, :, None] == names[None, None, :]
    hit = jnp.any(match, axis=1)
    when = jnp.sum(jnp.where(match, taken_at[:, :, None], 0), axis=1)
    rank = jnp.sum((hit[None, :, :] & (when[None, :, :] < when[:, None, :])).astype(jnp.int32), axis=1)
    kept = hit & (rank < capacity)
    pad = ((0, 0), (0, NAR - experts))
    hit = jnp.pad(hit.astype(F32), pad)
    kept = jnp.pad(kept.astype(F32), pad)

    heads = q_width // HEAD_DIM
    groups = k_width // HEAD_DIM
    group_rows = 2 * rows
    (w_all, wo_all, x_all, cot_all, egp, eup, edp, att_in, q, kk, vv, pr, att, hid, fe, gates) = pl.pallas_call(
        front_kernel,
        name="front",
        out_shape=(
            shaped(2 * 16 * depth, wide + NAR),
            shaped(16 * depth, width),
            shaped(2, rows, width),
            shaped(4, 4 * rows, width),
            shaped(half, ff),
            shaped(half, ff),
            shaped(ff, half),
            shaped(group_rows, width),
            shaped(group_rows, q_width),
            shaped(group_rows, k_width),
            shaped(group_rows, k_width),
            shaped(heads, group_rows, group_rows, dtype=F32),
            shaped(group_rows, q_width),
            shaped(rows, width, dtype=F32),
            shaped(rows, width + NAR),
            shaped(rows, NAR, dtype=F32),
        ),
        in_specs=[vm, vm, vm, hb, hb, hb, hb, vm, vm, vm, vm, vm],
        out_specs=(hb, hb, vm, hb, hb, hb, hb, vm, vm, vm, vm, vm, vm, vm, vm, vm),
        scratch_shapes=[
            pltpu.VMEM((2 * 16 * depth, wide + NAR), BF16),
            pltpu.VMEM((16 * depth, width), BF16),
            pltpu.VMEM((groups, group_rows, 128), BF16),
            pltpu.VMEM((groups, group_rows, 128), BF16),
            pltpu.VMEM((groups, group_rows, 128), BF16),
            pltpu.VMEM((groups, group_rows, 128), BF16),
            pltpu.VMEM((rows, width), BF16),
            pltpu.VMEM((rows, width), BF16),
        ]
        + [sems(Gather.SENDS), sems(Gather.RECVS)] * 4
        + [sems(6), sems(6), sems(3)],
        compiler_params=pltpu.CompilerParams(collective_id=1, has_side_effects=True, vmem_limit_bytes=56 << 20),
    )(
        tokens, packed, w_out, cotangent, expert_gate[0], expert_up[0], expert_down[0], cs, sn, vis, hit, kept
    )

    (total, mixp, og_own, ou_own, od_own, og_peer, ou_peer, od_peer) = pl.pallas_call(
        middle_kernel,
        name="middle",
        out_shape=(
            shaped(rows, width + NAR, dtype=F32),
            shaped(4, 4 * rows, width),
            shaped(half, ff, dtype=F32),
            shaped(half, ff, dtype=F32),
            shaped(ff, half, dtype=F32),
            shaped(half, ff),
            shaped(half, ff),
            shaped(ff, half),
        ),
        in_specs=[vm] + [hb] * 7,
        out_specs=(vm, hb, hb, hb, hb, vm, vm, vm),
        scratch_shapes=[
            pltpu.VMEM((4, 4 * rows, width + NAR), BF16),
            pltpu.VMEM((4, 4 * rows, width + NAR), BF16),
            pltpu.VMEM((4, 2, rows, width + NAR), BF16),
            pltpu.VMEM((4, rows, width + NAR), BF16),
            pltpu.VMEM((4, rows, width + NAR), BF16),
            pltpu.VMEM((width, ff), BF16),
            pltpu.VMEM((width, ff), BF16),
            pltpu.VMEM((ff, width), BF16),
            pltpu.VMEM((2, 4 * rows, width), BF16),
            pltpu.VMEM((4 * rows, width), BF16),
            pltpu.VMEM((4 * rows, ff), F32),
            pltpu.VMEM((4 * rows, ff), F32),
            pltpu.VMEM((4 * rows, ff), BF16),
            pltpu.VMEM((4 * rows, ff), BF16),
            pltpu.VMEM((4 * rows, ff), BF16),
            pltpu.VMEM((4 * rows, width), BF16),
            pltpu.VMEM((width, ff), F32),
            pltpu.VMEM((width, ff), F32),
            pltpu.VMEM((ff, width), F32),
            sems(Gather.SENDS),
            sems(Gather.RECVS),
            sems(Scatter.SENDS),
            sems(Scatter.RECVS),
            sems(6),
            sems(2),
            pltpu.SemaphoreType.DMA(()),
        ],
        compiler_params=pltpu.CompilerParams(collective_id=2, has_side_effects=True, vmem_limit_bytes=60 << 20),
    )(fe, cot_all, expert_gate[0], expert_up[0], expert_down[0], egp, eup, edp)

    def landing(block):
        return [
            pltpu.VMEM((4, 2) + block, BF16),
            pltpu.VMEM((4,) + block, BF16),
            pltpu.VMEM((4,) + block, BF16),
        ]

    (out, tok_grad, dq, dk, dv, dwo, gains, egr, eur, edr) = pl.pallas_call(
        back_kernel,
        name="back",
        out_shape=(
            shaped(rows, width),
            shaped(rows, width),
            shaped(depth, 2 * q_width, dtype=F32),
            shaped(depth, 2 * k_width, dtype=F32),
            shaped(depth, 2 * k_width, dtype=F32),
            shaped(depth, width, dtype=F32),
            shaped(depth, NAR, dtype=F32),
            shaped(half, ff),
            shaped(half, ff),
            shaped(ff, half),
        ),
        in_specs=[vm, hb, hb, hb, hb, hb, hb] + [vm] * 13,
        out_specs=(vm, vm, vm, vm, vm, vm, vm, hb, hb, hb),
        scratch_shapes=[
            pltpu.VMEM((2 * 16 * depth, wide + NAR), BF16),
            pltpu.VMEM((16 * depth, width), BF16),
            pltpu.VMEM((groups, group_rows, 128), BF16),
            pltpu.VMEM((groups, group_rows, 128), BF16),
            pltpu.VMEM((groups, group_rows, 128), BF16),
            pltpu.VMEM((groups, group_rows, 128), BF16),
            pltpu.VMEM((group_rows, width), BF16),
            pltpu.VMEM((group_rows, q_width), BF16),
            pltpu.VMEM((group_rows, wide), BF16),
            pltpu.VMEM((group_rows, k_width), F32),
            pltpu.VMEM((group_rows, k_width), F32),
            pltpu.VMEM((2 * 16 * depth, NAR), F32),
            pltpu.VMEM((rows, width), BF16),
            pltpu.VMEM((rows, width), BF16),
            pltpu.VMEM((rows, width), F32),
            pltpu.VMEM((4, 4 * rows, width), BF16),
        ]
        + landing((rows, width))
        + [pltpu.VMEM((16 * depth, width), BF16)]
        + landing((depth, width))
        + [pltpu.VMEM((2, 16 * depth, wide + NAR), BF16)]
        + landing((2, depth, wide + NAR))
        + [
            pltpu.VMEM((2, depth, wide + NAR), F32),
            pltpu.VMEM((depth, wide + NAR), F32),
        ]
        + [sems(Scatter.SENDS), sems(Scatter.RECVS)] * 3
        + [sems(6), sems(6), sems(6)],
        compiler_params=pltpu.CompilerParams(collective_id=3, has_side_effects=True, vmem_limit_bytes=60 << 20),
    )(
        total, mixp, og_peer, ou_peer, od_peer, w_all, wo_all, x_all, att_in, q, kk, vv, pr, att, hid, gates, kept,
        cotangent, cs, sn,
    )
    return (
        out,
        tok_grad,
        gains[:, experts],
        dq,
        dk,
        dv,
        dwo,
        gains[:, experts + 1],
        gains[:, :experts],
        (og_own + egr.astype(F32))[None],
        (ou_own + eur.astype(F32))[None],
        (od_own + edr.astype(F32))[None],
    )


def general_body(
    tokens,
    cotangent,
    norm_attn,
    w_query,
    key_projection,
    value_projection,
    w_out,
    norm_ffn,
    w_router,
    expert_gate,
    expert_up,
    expert_down,
    routes,
    slot_order,
    doc_lengths,
    deal,
):
    gain_attn, full_query, gathered_key, gathered_value, full_out, gain_ffn, full_router = (
        lax.all_gather(norm_attn, ("dp", "expert"), axis=0, tiled=True),
        lax.all_gather(w_query, ("dp", "expert"), axis=0, tiled=True),
        lax.all_gather(key_projection, ("dp", "expert"), axis=0, tiled=True),
        lax.all_gather(value_projection, ("dp", "expert"), axis=0, tiled=True),
        lax.all_gather(w_out, ("dp", "expert"), axis=0, tiled=True),
        lax.all_gather(norm_ffn, ("dp", "expert"), axis=0, tiled=True),
        lax.all_gather(w_router, ("dp", "expert"), axis=0, tiled=True),
    )
    full_gate, full_up, full_down = (
        lax.all_gather(expert_gate[0], "dp", axis=0, tiled=True),
        lax.all_gather(expert_up[0], "dp", axis=0, tiled=True),
        lax.all_gather(expert_down[0], "dp", axis=1, tiled=True),
    )
    count_of_rows, model_width = tokens.shape
    top_count = routes.shape[1]
    experts = full_router.shape[1]
    owners = lax.axis_size("expert")
    capacity = 9 * count_of_rows * top_count // (8 * experts)
    head_count = full_query.shape[1] // HEAD_DIM
    groups = gathered_key.shape[1] // HEAD_DIM
    head_ratio = head_count // groups
    scale_attn = gain_attn.astype(jnp.float32)
    scale_ffn = gain_ffn.astype(jnp.float32)
    score_scale = HEAD_DIM ** (-0.5)
    group_places = deal[:, 0, :].reshape(-1)
    group_docs, group_offsets = doc_layout(doc_lengths[0], group_places)
    shard_start = lax.axis_index("dp") * count_of_rows
    places = lax.dynamic_slice_in_dim(group_places, shard_start, count_of_rows)
    doc_ids = lax.dynamic_slice_in_dim(group_docs, shard_start, count_of_rows)
    offsets = lax.dynamic_slice_in_dim(group_offsets, shard_start, count_of_rows)
    cosine_lookup, sine_lookup = rope_tables(offsets, HEAD_DIM)
    inputs = tokens.astype(jnp.float32)
    inverse_one = lax.rsqrt(jnp.mean(inputs * inputs, axis=1, keepdims=True) + NORM_EPS)
    normed_one = inputs * inverse_one
    attention_input = (normed_one * scale_attn).astype(jnp.bfloat16)
    query_rows = apply_rotation(
        dot_plain(attention_input, full_query).reshape(count_of_rows, head_count, HEAD_DIM),
        cosine_lookup,
        sine_lookup,
    ).astype(jnp.bfloat16)
    key_matrix_rows = apply_rotation(
        dot_plain(attention_input, gathered_key).reshape(count_of_rows, groups, HEAD_DIM),
        cosine_lookup,
        sine_lookup,
    ).astype(jnp.bfloat16)
    value_matrix_rows = dot_plain(attention_input, gathered_value).astype(jnp.bfloat16)
    all_keys, all_values = (
        lax.all_gather(key_matrix_rows.reshape(count_of_rows, -1), "dp", axis=0, tiled=True),
        lax.all_gather(value_matrix_rows, "dp", axis=0, tiled=True),
    )
    group_rows = all_keys.shape[0]
    key_span = math.gcd(group_rows, 512)
    span_count = group_rows // key_span
    key_spans = (
        all_keys.reshape(span_count, key_span, groups, HEAD_DIM),
        all_values.reshape(span_count, key_span, groups, HEAD_DIM),
        group_places.reshape(span_count, key_span),
        group_docs.reshape(span_count, key_span),
    )
    grouped_q = query_rows.reshape(count_of_rows, groups, head_ratio, HEAD_DIM)

    def span_scores(key_block, key_place, key_doc):
        visible = (doc_ids[:, None] == key_doc[None, :]) & (places[:, None] >= key_place[None, :])
        scores = (
            jnp.einsum("qgrd,kgd->grqk", grouped_q, key_block, preferred_element_type=jnp.float32)
            * score_scale
        )
        return jnp.where(visible[None, None], scores, MASK_FILL)

    def extent(carry, operands):
        run_max, run_sum = carry
        key_block, value_block, key_place, key_doc = operands
        scores = span_scores(key_block, key_place, key_doc)
        new_max = jnp.maximum(run_max, jnp.max(scores, axis=-1, keepdims=True))
        run_sum = run_sum * jnp.exp(run_max - new_max) + jnp.sum(
            jnp.exp(scores - new_max), axis=-1, keepdims=True
        )
        return ((new_max, run_sum), None)

    stat_shape = (groups, head_ratio, count_of_rows, 1)
    (row_max, row_sum), _ = lax.scan(
        extent,
        (jnp.full(stat_shape, MASK_FILL, jnp.float32), jnp.zeros(stat_shape, jnp.float32)),
        key_spans,
    )
    log_total = row_max + jnp.log(row_sum)

    def weigh_values(running, operands):
        key_block, value_block, key_place, key_doc = operands
        weights = jnp.exp(span_scores(key_block, key_place, key_doc) - log_total).astype(
            jnp.bfloat16
        )
        return (
            running
            + jnp.einsum(
                "grqk,kgd->qgrd", weights, value_block, preferred_element_type=jnp.float32
            ),
            None,
        )

    attended, _ = lax.scan(
        weigh_values,
        jnp.zeros((count_of_rows, groups, head_ratio, HEAD_DIM), jnp.float32),
        key_spans,
    )
    attended = attended.reshape(count_of_rows, head_count * HEAD_DIM).astype(jnp.bfloat16)
    hidden_state = inputs + dot_plain(attended, full_out)
    inverse_two = lax.rsqrt(jnp.mean(hidden_state * hidden_state, axis=1, keepdims=True) + NORM_EPS)
    normed_two = hidden_state * inverse_two
    ffn_in = (normed_two * scale_ffn).astype(jnp.bfloat16)
    logits = dot_plain(ffn_in, full_router)
    route_hits = (routes[:, :, None] == jnp.arange(experts, dtype=jnp.int32)[None, None, :]).astype(
        jnp.float32
    )
    chosen = jnp.sum(route_hits * logits[:, None, :], axis=-1)
    gate_values = jax.nn.softmax(chosen, axis=-1)
    pair_slot, slot_token = assign_slots(routes, slot_order[0], experts, capacity)
    padded_in = jnp.concatenate([ffn_in, jnp.zeros((1, model_width), jnp.bfloat16)], axis=0)
    outgoing = padded_in[slot_token].reshape(owners, capacity, model_width)
    arrived = lax.all_to_all(outgoing, "expert", split_axis=0, concat_axis=0, tiled=True)
    flat_rows = arrived.reshape(-1, model_width)
    gate_pre = dot_plain(flat_rows, full_gate)
    up_pre = dot_plain(flat_rows, full_up)
    hidden = (jax.nn.silu(gate_pre) * up_pre).astype(jnp.bfloat16)
    result = dot_plain(hidden, full_down).astype(jnp.bfloat16).reshape(arrived.shape)
    sent_back = lax.all_to_all(result, "expert", split_axis=0, concat_axis=0, tiled=True)
    exchanged = (
        sent_back,
        arrived,
        gate_pre.reshape(arrived.shape[0], arrived.shape[1], -1),
        up_pre.reshape(arrived.shape[0], arrived.shape[1], -1),
    )
    returned = exchanged[0]
    expert_rows = exchanged[1].reshape(-1, model_width)
    gate_pre = exchanged[2].reshape(expert_rows.shape[0], -1)
    up_pre = exchanged[3].reshape(expert_rows.shape[0], -1)
    out_grad = cotangent.astype(jnp.float32)
    padded_back = jnp.concatenate(
        [returned.reshape(-1, model_width), jnp.zeros((1, model_width), jnp.bfloat16)], axis=0
    )
    slot_grid = pair_slot.reshape(count_of_rows, top_count)
    mixture = jnp.zeros((count_of_rows, model_width), jnp.float32)
    gate_parts = []
    for column in range(top_count):
        picked = padded_back[slot_grid[:, column]].astype(jnp.float32)
        mixture = mixture + gate_values[:, column : column + 1] * picked
        gate_parts.append(jnp.sum(out_grad * picked, axis=1))
    output = (hidden_state + mixture).astype(jnp.bfloat16)
    gate_grad = jnp.stack(gate_parts, axis=1)
    slot_gate = (
        jnp.zeros((experts * capacity + 1,), jnp.float32)
        .at[pair_slot]
        .set(gate_values.reshape(-1))[: experts * capacity]
    )
    padded_grad = jnp.concatenate([out_grad, jnp.zeros((1, model_width), jnp.float32)], axis=0)
    slot_grad = (
        (slot_gate[:, None] * padded_grad[slot_token])
        .astype(jnp.bfloat16)
        .reshape(owners, capacity, model_width)
    )
    arrived_grad = lax.all_to_all(
        slot_grad, "expert", split_axis=0, concat_axis=0, tiled=True
    ).reshape(-1, model_width)
    sigmoid_gate = jax.nn.sigmoid(gate_pre)
    silu_gate = gate_pre * sigmoid_gate
    hidden = (silu_gate * up_pre).astype(jnp.bfloat16)
    hidden_grad = dot_last(arrived_grad, full_down)
    gate_pre_grad = (
        hidden_grad * up_pre * sigmoid_gate * (1.0 + gate_pre * (1.0 - sigmoid_gate))
    ).astype(jnp.bfloat16)
    up_pre_grad = (hidden_grad * silu_gate).astype(jnp.bfloat16)
    down_weight_grad = dot_first(hidden, arrived_grad)
    gate_weight_grad = dot_first(expert_rows, gate_pre_grad)
    up_weight_grad = dot_first(expert_rows, up_pre_grad)
    row_grad = (dot_last(gate_pre_grad, full_gate) + dot_last(up_pre_grad, full_up)).astype(
        jnp.bfloat16
    )
    token_rows_grad = lax.all_to_all(
        row_grad.reshape(owners, capacity, model_width),
        "expert",
        split_axis=0,
        concat_axis=0,
        tiled=True,
    )
    gate_summed, up_summed, down_summed = (
        lax.psum_scatter(
            gate_weight_grad.astype(jnp.bfloat16), "dp", scatter_dimension=0, tiled=True
        ).astype(jnp.float32),
        lax.psum_scatter(
            up_weight_grad.astype(jnp.bfloat16), "dp", scatter_dimension=0, tiled=True
        ).astype(jnp.float32),
        lax.psum_scatter(
            down_weight_grad.astype(jnp.bfloat16), "dp", scatter_dimension=1, tiled=True
        ).astype(jnp.float32),
    )
    dispatch_grad = jax.ops.segment_sum(
        token_rows_grad.reshape(-1, model_width).astype(jnp.float32),
        slot_token,
        num_segments=count_of_rows + 1,
    )[:count_of_rows]
    chosen_grad = gate_values * (
        gate_grad - jnp.sum(gate_values * gate_grad, axis=1, keepdims=True)
    )
    logit_grad = jnp.sum(route_hits * chosen_grad[:, :, None], axis=1).astype(jnp.bfloat16)
    router_grad = dot_first(ffn_in, logit_grad)
    ffn_grad = dispatch_grad + dot_last(logit_grad, full_router)
    ffn_gain_grad = jnp.sum(ffn_grad * normed_two, axis=0)
    scaled_two = ffn_grad * scale_ffn
    state_grad = out_grad + inverse_two * (
        scaled_two - normed_two * jnp.mean(scaled_two * normed_two, axis=1, keepdims=True)
    )
    branch_grad = state_grad.astype(jnp.bfloat16)
    out_weight_grad = dot_first(attended, branch_grad)
    attended_grad = (
        dot_last(branch_grad, full_out)
        .astype(jnp.bfloat16)
        .reshape(count_of_rows, groups, head_ratio, HEAD_DIM)
    )

    def spread_sum(running, operands):
        key_block, value_block, key_place, key_doc = operands
        probs = jnp.exp(span_scores(key_block, key_place, key_doc) - log_total)
        prob_grad = jnp.einsum(
            "qgrd,kgd->grqk", attended_grad, value_block, preferred_element_type=jnp.float32
        )
        return (running + jnp.sum(probs * prob_grad, axis=-1, keepdims=True), None)

    score_shift, _ = lax.scan(spread_sum, jnp.zeros(stat_shape, jnp.float32), key_spans)

    def back_span(running, operands):
        key_block, value_block, key_place, key_doc = operands
        probs = jnp.exp(span_scores(key_block, key_place, key_doc) - log_total)
        prob_grad = jnp.einsum(
            "qgrd,kgd->grqk", attended_grad, value_block, preferred_element_type=jnp.float32
        )
        score_grad = (probs * (prob_grad - score_shift)).astype(jnp.bfloat16)
        running = running + jnp.einsum(
            "grqk,kgd->qgrd", score_grad, key_block, preferred_element_type=jnp.float32
        )
        key_part = (
            jnp.einsum("grqk,qgrd->kgd", score_grad, grouped_q, preferred_element_type=jnp.float32)
            * score_scale
        )
        value_part = jnp.einsum(
            "grqk,qgrd->kgd",
            probs.astype(jnp.bfloat16),
            attended_grad,
            preferred_element_type=jnp.float32,
        )
        return (running, (key_part.reshape(key_span, -1), value_part.reshape(key_span, -1)))

    query_sum, (key_parts, value_parts) = lax.scan(
        back_span, jnp.zeros((count_of_rows, groups, head_ratio, HEAD_DIM), jnp.float32), key_spans
    )
    key_grad, value_sum = (
        lax.psum_scatter(
            key_parts.reshape(group_rows, -1).astype(jnp.bfloat16),
            "dp",
            scatter_dimension=0,
            tiled=True,
        ).astype(jnp.float32),
        lax.psum_scatter(
            value_parts.reshape(group_rows, -1).astype(jnp.bfloat16),
            "dp",
            scatter_dimension=0,
            tiled=True,
        ).astype(jnp.float32),
    )
    query_grad = query_sum * score_scale
    query_lin_grad = unrotate(
        query_grad.reshape(count_of_rows, head_count, HEAD_DIM), cosine_lookup, sine_lookup
    )
    query_lin_grad = query_lin_grad.reshape(count_of_rows, -1).astype(jnp.bfloat16)
    key_lin_grad = (
        unrotate(key_grad.reshape(count_of_rows, groups, HEAD_DIM), cosine_lookup, sine_lookup)
        .reshape(count_of_rows, -1)
        .astype(jnp.bfloat16)
    )
    value_lin_grad = value_sum.astype(jnp.bfloat16)
    query_weight_grad = dot_first(attention_input, query_lin_grad)
    key_weight_grad = dot_first(attention_input, key_lin_grad)
    value_weight_grad = dot_first(attention_input, value_lin_grad)
    attn_grad = (
        dot_last(query_lin_grad, full_query)
        + dot_last(key_lin_grad, gathered_key)
        + dot_last(value_lin_grad, gathered_value)
    )
    attn_gain_grad = jnp.sum(attn_grad * normed_one, axis=0)
    scaled_one = attn_grad * scale_attn
    tokens_grad = (
        state_grad
        + inverse_one
        * (scaled_one - normed_one * jnp.mean(scaled_one * normed_one, axis=1, keepdims=True))
    ).astype(jnp.bfloat16)
    summed = (
        lax.psum_scatter(attn_gain_grad, ("dp", "expert"), scatter_dimension=0, tiled=True),
        lax.psum_scatter(query_weight_grad, ("dp", "expert"), scatter_dimension=0, tiled=True),
        lax.psum_scatter(key_weight_grad, ("dp", "expert"), scatter_dimension=0, tiled=True),
        lax.psum_scatter(value_weight_grad, ("dp", "expert"), scatter_dimension=0, tiled=True),
        lax.psum_scatter(out_weight_grad, ("dp", "expert"), scatter_dimension=0, tiled=True),
        lax.psum_scatter(ffn_gain_grad, ("dp", "expert"), scatter_dimension=0, tiled=True),
        lax.psum_scatter(router_grad, ("dp", "expert"), scatter_dimension=0, tiled=True),
    )
    return (
        output,
        tokens_grad,
        summed[0],
        summed[1],
        summed[2],
        summed[3],
        summed[4],
        summed[5],
        summed[6],
        gate_summed[None],
        up_summed[None],
        down_summed[None],
    )


def solution(mesh):
    in_specs = (
        P(("dp", "expert"), None),
        P(("dp", "expert"), None),
        P(("dp", "expert")),
        P(("dp", "expert"), None),
        P(("dp", "expert"), None),
        P(("dp", "expert"), None),
        P(("dp", "expert"), None),
        P(("dp", "expert")),
        P(("dp", "expert"), None),
        P("expert", "dp", None),
        P("expert", "dp", None),
        P("expert", None, "dp"),
        P(("dp", "expert"), None),
        P(("dp", "expert"), None),
        P("expert", None),
        P(None, "expert", None),
    )
    out_specs = (
        P(("dp", "expert"), None),
        P(("dp", "expert"), None),
        P(("dp", "expert")),
        P(("dp", "expert"), None),
        P(("dp", "expert"), None),
        P(("dp", "expert"), None),
        P(("dp", "expert"), None),
        P(("dp", "expert")),
        P(("dp", "expert"), None),
        P("expert", "dp", None),
        P("expert", "dp", None),
        P("expert", None, "dp"),
    )
    fast = mesh.shape["dp"] == 2 and mesh.shape["expert"] == 16
    body = paired_body if fast else general_body
    return jax.shard_map(body, mesh=mesh, in_specs=in_specs, out_specs=out_specs, check_vma=False)
```

```python
import functools
import math

import jax
import jax.numpy as jnp
from jax import lax
from jax.experimental import pallas as pl
from jax.experimental.pallas import tpu as pltpu
from jax.sharding import PartitionSpec as P

HEAD_DIM = 64


NORM_EPS = 1e-05
MASK_FILL = -1e30
ROPE_BASE = 10000.0


def dot_plain(left_side, right_side):
    return jnp.dot(left_side, right_side, preferred_element_type=jnp.float32)


def dot_last(left_side, right_side):
    return lax.dot_general(
        left_side, right_side, (((1,), (1,)), ((), ())), preferred_element_type=jnp.float32
    )


def dot_first(left_side, right_side):
    return lax.dot_general(
        left_side, right_side, (((0,), (0,)), ((), ())), preferred_element_type=jnp.float32
    )


def doc_layout(lengths, places):
    doc_ends = jnp.cumsum(lengths)
    doc_starts = doc_ends - lengths
    doc_ids = jnp.sum((places[:, None] >= doc_ends[None, :]).astype(jnp.int32), axis=1)
    member = doc_ids[:, None] == jnp.arange(lengths.shape[0], dtype=jnp.int32)[None, :]
    offsets = places - jnp.sum(jnp.where(member, doc_starts[None, :], 0), axis=1)
    return (doc_ids, offsets)


def rope_tables(offsets, head_size):
    half_size = head_size // 2
    frequency = ROPE_BASE ** (-2.0 * jnp.arange(half_size, dtype=jnp.float32) / head_size)
    angles = offsets.astype(jnp.float32)[:, None] * frequency[None, :]
    return (jnp.cos(angles), jnp.sin(angles))


def apply_rotation(values, cosine_lookup, sine_lookup):
    half_size = values.shape[-1] // 2
    first_half = values[..., :half_size]
    second = values[..., half_size:]
    cos_rows = cosine_lookup[:, None, :]
    sin_rows = sine_lookup[:, None, :]
    return jnp.concatenate(
        [first_half * cos_rows - second * sin_rows, second * cos_rows + first_half * sin_rows],
        axis=-1,
    )


def unrotate(gradient, cosine_lookup, sine_lookup):
    half_size = gradient.shape[-1] // 2
    first_half = gradient[..., :half_size]
    second = gradient[..., half_size:]
    cos_rows = cosine_lookup[:, None, :]
    sin_rows = sine_lookup[:, None, :]
    return jnp.concatenate(
        [first_half * cos_rows + second * sin_rows, second * cos_rows - first_half * sin_rows],
        axis=-1,
    )


def assign_slots(routes, take_order, experts, capacity):
    count_of_rows, top_count = routes.shape
    flat_routes = routes.reshape(-1)
    chosen = flat_routes[take_order]
    expert_hits = (chosen[:, None] == jnp.arange(experts, dtype=jnp.int32)[None, :]).astype(
        jnp.int32
    )
    slot_rank = jnp.sum(jnp.cumsum(expert_hits, axis=0) * expert_hits, axis=1) - 1
    slot_index = jnp.where(slot_rank < capacity, chosen * capacity + slot_rank, experts * capacity)
    pair_slot = jnp.zeros((flat_routes.shape[0],), jnp.int32).at[take_order].set(slot_index)
    slot_token = (
        jnp.full((experts * capacity + 1,), count_of_rows, jnp.int32)
        .at[slot_index]
        .set(take_order // top_count)
    )
    return (pair_slot, slot_token[: experts * capacity])


MESH = pl.DeviceIdType.MESH
BF16 = jnp.bfloat16
F32 = jnp.float32
NAR = 128


def remote(src, dst, send_sem, recv_sem, device):
    return pltpu.make_async_remote_copy(
        src_ref=src,
        dst_ref=dst,
        send_sem=send_sem,
        recv_sem=recv_sem,
        device_id=device,
        device_id_type=MESH,
    )


class Place:
    def __init__(self):
        self.i = lax.axis_index("dp")
        self.e = lax.axis_index("expert")
        self.a = self.e // 4
        self.bc = self.e % 4
        self.y = self.bc // 2
        self.c = self.bc % 2

    def over_x(self):
        return (1 - self.i, self.e)

    def over_y(self):
        return (self.i, self.e + 2 - 4 * self.y)

    def over_core(self):
        return (self.i, self.e + 1 - 2 * self.c)

    def order(self, k):
        turn = (1 - 2 * k) * (1 - k // 2)
        inner = (self.a * (3 - self.a)) // 2
        half = self.a // 2
        step = k + inner * turn
        return step + half * (3 - 2 * step)

    def barrier(self):
        sem = pltpu.get_barrier_semaphore()
        peers = [self.over_x(), self.over_y(), self.over_core()]
        for shift in range(1, 4):
            peers.append((self.i, ((self.a + shift) % 4) * 4 + self.bc))
        for peer in peers:
            pl.semaphore_signal(sem, inc=1, device_id=peer, device_id_type=MESH)
        pl.semaphore_wait(sem, len(peers))


class Gather:
    SENDS = 20
    RECVS = 16

    def __init__(self, place, view, sends, recvs):
        self.p, self.view, self.sends, self.recvs = place, view, sends, recvs

    def copy(self, block, slot, device):
        ref = self.view(block)
        return remote(ref, ref, self.sends.at[slot], self.recvs.at[block], device)

    def right(self, a1):
        return self.copy(a1 * 4 + self.p.bc, a1, (self.p.i, self.p.e + 4))

    def left(self, a1):
        return self.copy(a1 * 4 + self.p.bc, 4 + a1, (self.p.i, self.p.e - 4))

    def across(self, a1):
        return self.copy(a1 * 4 + self.p.bc, 8 + a1, self.p.over_y())

    def core(self, a1, y1):
        return self.copy(a1 * 4 + y1 * 2 + self.p.c, 12 + a1 * 2 + y1, self.p.over_core())

    def landed(self, block):
        self.copy(block, 0, self.p.over_core()).wait_recv()

    def begin(self):
        p = self.p
        self.across(p.a).start()

        @pl.when(p.a < 3)
        def _():
            self.right(p.a).start()

        @pl.when(p.a > 0)
        def _():
            self.left(p.a).start()

        self.core(p.a, p.y).start()

    def phase(self, s):
        p = self.p
        inner = (p.a * (3 - p.a)) // 2
        if s == 1:
            self.along(1)

        @pl.when(inner == 1)
        def _():
            if s < 3:
                self.along(s + 1)

        if s > 1:

            @pl.when(inner == 0)
            def _():
                self.along(s)

    def along(self, k):
        p = self.p
        a1 = p.order(k)
        self.landed(a1 * 4 + p.bc)

        @pl.when((a1 < p.a) & (p.a < 3))
        def _():
            self.right(a1).start()

        @pl.when((a1 > p.a) & (p.a > 0))
        def _():
            self.left(a1).start()

        self.across(a1).start()
        self.core(a1, p.y).start()

    def cross(self, k):
        p = self.p
        a1 = p.order(k)
        self.landed(a1 * 4 + (1 - p.y) * 2 + p.c)
        self.core(a1, 1 - p.y).start()

    def join(self, k):
        p = self.p
        a1 = p.order(k)
        self.landed(a1 * 4 + (1 - p.c))
        self.landed(a1 * 4 + 2 + (1 - p.c))

    def drain(self):
        p = self.p
        for a1 in range(4):

            @pl.when((a1 <= p.a) & (p.a < 3))
            def _():
                self.right(a1).wait_send()

            @pl.when((a1 >= p.a) & (p.a > 0))
            def _():
                self.left(a1).wait_send()

            self.across(a1).wait_send()
            self.core(a1, 0).wait_send()
            self.core(a1, 1).wait_send()


class Scatter:
    SENDS = 16
    RECVS = 16

    def __init__(self, place, part, core_in, y_in, a_in, sends, recvs):
        self.p, self.part = place, part
        self.core_in, self.y_in, self.a_in = core_in, y_in, a_in
        self.sends, self.recvs = sends, recvs

    def to_core(self, a1, y1):
        p = self.p
        slot = a1 * 2 + y1
        return remote(
            self.part(a1, y1 * 2 + 1 - p.c),
            self.core_in.at[a1, y1],
            self.sends.at[slot],
            self.recvs.at[slot],
            p.over_core(),
        )

    def to_y(self, a1):
        p = self.p
        return remote(
            self.part(a1, (1 - p.y) * 2 + p.c),
            self.y_in.at[a1],
            self.sends.at[8 + a1],
            self.recvs.at[8 + a1],
            p.over_y(),
        )

    def to_a(self, a1):
        p = self.p
        return remote(
            self.part(a1, p.bc),
            self.a_in.at[p.a],
            self.sends.at[12 + a1],
            self.recvs.at[12 + p.a],
            (p.i, a1 * 4 + p.bc),
        )

    def from_a(self, a1):
        p = self.p
        return remote(
            self.a_in.at[a1],
            self.a_in.at[a1],
            self.sends.at[12 + a1],
            self.recvs.at[12 + a1],
            (p.i, a1 * 4 + p.bc),
        )

    def start(self, a1):
        self.to_core(a1, 0).start()
        self.to_core(a1, 1).start()

    def add(self, ref, other):
        ref[...] = (ref[...].astype(F32) + other[...].astype(F32)).astype(ref.dtype)

    def core(self, a1):
        p = self.p
        for y1 in range(2):
            self.to_core(a1, y1).wait_recv()
        self.add(self.part(a1, (1 - p.y) * 2 + p.c), self.core_in.at[a1, 1 - p.y])
        self.to_y(a1).start()
        self.add(self.part(a1, p.bc), self.core_in.at[a1, p.y])

    def cross(self, a1):
        p = self.p
        self.to_y(a1).wait_recv()
        self.add(self.part(a1, p.bc), self.y_in.at[a1])

        @pl.when(a1 != p.a)
        def _():
            self.to_a(a1).start()

        @pl.when(a1 == p.a)
        def _():
            self.a_in[a1] = self.part(a1, p.bc)[...]

    def finish(self):
        p = self.p
        for k in range(1, 4):
            self.from_a(p.order(k)).wait_recv()

    def total(self):
        return (
            self.a_in[0].astype(F32)
            + self.a_in[1].astype(F32)
            + self.a_in[2].astype(F32)
            + self.a_in[3].astype(F32)
        )

    def drain(self):
        p = self.p
        for k in range(4):
            a1 = p.order(k)
            self.to_core(a1, 0).wait_send()
            self.to_core(a1, 1).wait_send()
            self.to_y(a1).wait_send()
            if k:
                self.to_a(a1).wait_send()


def lane_iota(shape):
    return lax.broadcasted_iota(jnp.int32, shape, len(shape) - 1)


def swap_halves(values):
    lane = lane_iota(values.shape) % HEAD_DIM
    half = HEAD_DIM // 2
    return jnp.where(
        lane < half,
        pltpu.roll(values, values.shape[-1] - half, 1),
        pltpu.roll(values, half, 1),
    )


def split_heads(tile):
    low = lane_iota(tile.shape) < HEAD_DIM
    turned = pltpu.roll(tile, HEAD_DIM, 1)
    zero = jnp.zeros_like(tile)
    return (
        (jnp.where(low, tile, zero), jnp.where(low, zero, turned)),
        (jnp.where(low, turned, zero), jnp.where(low, zero, tile)),
    )


def inverse_rms(values):
    return lax.rsqrt(jnp.mean(values * values, axis=1, keepdims=True) + NORM_EPS)


def gain_rows(narrow, experts):
    shape = (16, narrow.shape[1])
    row = lax.broadcasted_iota(jnp.int32, shape, 0)
    pick = jnp.where(lane_iota(shape) == row + experts, 1.0, 0.0).astype(BF16)
    return dot_last(pick, narrow)


def column_of(row):
    n = row.shape[1]
    shape = (n, n)
    same = lane_iota(shape) == lax.broadcasted_iota(jnp.int32, shape, 0)
    return jnp.sum(jnp.where(same, row, 0.0), axis=1, keepdims=True)


def documents(places, ends):
    doc = jnp.zeros_like(places)
    start = jnp.zeros_like(places)
    for end in ends:
        past = places >= end
        doc = doc + jnp.where(past, 1.0, 0.0)
        start = jnp.where(past, end, start)
    return doc, start


def turned(values):
    m, n = values.shape
    if n < NAR:
        values = jnp.concatenate([values, jnp.zeros((m, NAR - n), F32)], axis=1)
    if m < NAR:
        values = jnp.concatenate([values, jnp.zeros((NAR - m, NAR), F32)], axis=0)
    return jnp.transpose(values)[:n, :m]


def kept_pairs(routes_by_rank, take_order, experts, capacity):
    top_count, rows = routes_by_rank.shape
    routes = turned(routes_by_rank.astype(F32)).astype(jnp.int32)
    lane = lane_iota((rows, NAR))
    token = lax.broadcasted_iota(jnp.int32, (rows, 1), 0)
    number = lane_iota((rows, take_order.shape[1])).astype(F32)
    hit = jnp.zeros((rows, NAR), jnp.bool_)
    taken = jnp.zeros((rows, NAR), F32)
    for j in range(top_count):
        at = jnp.sum(jnp.where(take_order == token * top_count + j, number, 0.0), axis=1, keepdims=True)
        mine = lane == routes[:, j : j + 1]
        hit = hit | mine
        taken = jnp.where(mine, at, taken)
    taken = jnp.where(hit, taken, 1e9)
    across = jnp.transpose(taken)
    rank = jnp.zeros((rows, NAR), F32)
    for name in range(experts):
        before = jnp.where(across[name : name + 1, :] < taken[:, name : name + 1], 1.0, 0.0)
        rank = jnp.where(lane == name, jnp.sum(before, axis=1, keepdims=True), rank)
    one, zero = jnp.ones((rows, NAR), F32), jnp.zeros((rows, NAR), F32)
    hits = jnp.where(hit, one, zero)
    return hits, jnp.where(rank < capacity, hits, zero)


def front_kernel(
    tok, wq, wk, wv, wr, na, nf, wo, cot, eg, eu, ed, routes, slots, lengths, places,
    w_out_all, wo_out_all, x_all, cot_all, egp, eup, edp, att_in, q_out, k_out, v_out, pr_out, att, hid, fe, gates,
    cs, sn, kept,
    w_all, wo_all, pr, vis, hit, klo, khi, vlo, vhi, opart, orecv,
    ga_s, ga_r, gb_s, gb_r, gw_s, gw_r, gc_s, gc_r, xs, xr, loc, pr_sem,
):
    p = Place()
    i, e = p.i, p.e
    rows, width = tok.shape
    depth = wo.shape[0]
    plane = 16 * depth
    q_width = q_out.shape[1]
    k_width = k_out.shape[1]
    experts = 16
    wide = q_width + 2 * k_width
    capacity = 9 * rows * routes.shape[0] // (8 * experts)

    def w_row(ip, block):
        return pl.ds(pl.multiple_of(ip * plane + block * depth, 16), depth)

    def row_block(ip):
        return pl.ds(pl.multiple_of(ip * rows, rows), rows)

    def half_lanes(ip, n):
        return pl.ds(pl.multiple_of(ip * n, 128), n)

    lane = lane_iota((depth, NAR))
    gain_cols = [column_of(r[...].astype(F32)) for r in (na, nf)]
    narrow_own = jnp.concatenate([turned(wr[...].astype(F32)), jnp.zeros((depth, NAR - experts), F32)], axis=1)
    narrow_own = jnp.where(lane == experts, gain_cols[0], jnp.where(lane == experts + 1, gain_cols[1], narrow_own))
    w_all[w_row(i, e), wide:] = narrow_own.astype(BF16)
    w_all[w_row(i, e), :q_width] = wq[:, half_lanes(i, q_width)]
    w_all[w_row(i, e), q_width : q_width + k_width] = wk[:, half_lanes(i, k_width)]
    w_all[w_row(i, e), q_width + k_width : wide] = wv[:, half_lanes(i, k_width)]
    p.barrier()
    own = w_row(i, e)
    give_w = [
        remote(src, w_all.at[own, pl.ds(first, size)], xs.at[6 + n], xr.at[6 + n], p.over_x())
        for n, (src, first, size) in enumerate(
            (
                (wq.at[:, half_lanes(1 - i, q_width)], 0, q_width),
                (wk.at[:, half_lanes(1 - i, k_width)], q_width, k_width),
                (wv.at[:, half_lanes(1 - i, k_width)], q_width + k_width, k_width),
                (w_all.at[own, pl.ds(wide, NAR)], wide, NAR),
            )
        )
    ]
    for one in give_w:
        one.start()
    give_x = remote(tok, x_all.at[i], xs.at[1], xr.at[1], p.over_x())
    take_x = remote(x_all.at[1 - i], x_all.at[1 - i], xs.at[1], xr.at[1], p.over_x())
    give_x.start()

    ga = Gather(p, lambda block: w_all.at[w_row(i, block)], ga_s, ga_r)
    gb = Gather(p, lambda block: w_all.at[w_row(1 - i, block)], gb_s, gb_r)
    gw = Gather(p, lambda block: wo_all.at[w_row(0, block)], gw_s, gw_r)
    gc = Gather(
        p, lambda block: cot_all.at[block // 4, pl.ds(pl.multiple_of((block % 4) * rows, rows), rows)], gc_s, gc_r
    )

    ga.begin()
    own_cot = pltpu.make_async_copy(cot, gc.view(e), loc.at[0])
    own_cot.start()
    wo_all[w_row(0, e), :] = wo[...]
    x_all[i] = tok[...]
    for n, one in enumerate(give_w):
        first, size = ((0, q_width), (q_width, k_width), (q_width + k_width, k_width), (wide, NAR))[n]
        there = w_all.at[w_row(1 - i, e), pl.ds(first, size)]
        remote(there, there, xs.at[6 + n], xr.at[6 + n], p.over_x()).wait_recv()
    gb.begin()
    experts_out = [
        remote(src, dst, xs.at[2 + n], xr.at[2 + n], p.over_x())
        for n, (src, dst) in enumerate(((eg, egp), (eu, eup), (ed, edp)))
    ]
    experts_out[0].start()
    experts_out[1].start()

    ends = [lengths[0, 0].astype(F32)]
    for n in range(1, lengths.shape[1]):
        ends.append(ends[-1] + lengths[0, n].astype(F32))
    place_row = places[...].astype(F32)
    place_col = column_of(place_row)
    doc_row, _ = documents(place_row, ends[:-1])
    doc_col, start_col = documents(place_col, ends[:-1])
    vis[...] = jnp.where((doc_row == doc_col) & (place_col >= place_row), 1.0, 0.0)
    lane = lane_iota((1, 128))
    half = HEAD_DIM // 2
    freq = jnp.exp((lane % half).astype(F32) * (-2.0 / HEAD_DIM * math.log(ROPE_BASE)))
    angle = (place_col - start_col) * freq
    cs[...] = jnp.cos(angle)
    sine = jnp.sin(angle)
    sn[...] = jnp.where(lane % HEAD_DIM < half, -sine, sine)

    both = (ga, gb)
    for g in both:
        g.phase(1)
    hits, keeps = kept_pairs(routes[...], slots[...], experts, capacity)
    hit[...] = hits
    kept[...] = keeps
    for k in range(3):
        for g in both:
            g.cross(k)
        if k < 2:
            for g in both:
                g.phase(k + 2)
        if k == 1:
            gw.begin()
    gw.phase(1)
    own_cot.wait()
    gc.begin()
    for g in both:
        g.cross(3)
    for k in range(4):
        for g in both:
            g.join(k)

    events = [
        functools.partial(gw.phase, 2),
        functools.partial(gw.cross, 0),
        functools.partial(gw.phase, 3),
        functools.partial(gw.cross, 1),
        functools.partial(gw.cross, 2),
        functools.partial(gw.cross, 3),
        functools.partial(gc.phase, 1),
        functools.partial(gc.cross, 0),
        functools.partial(gc.phase, 2),
        functools.partial(gc.cross, 1),
        functools.partial(gc.phase, 3),
        functools.partial(gc.cross, 2),
        functools.partial(gc.cross, 3),
    ]

    def serve(upto=99):
        if events and len(events) > 13 - upto:
            events.pop(0)()

    w_save = pltpu.make_async_copy(w_all, w_out_all, loc.at[1])
    w_save.start()
    take_x.wait_recv()
    narrow = w_all[:, wide:]
    gains = gain_rows(narrow, experts)
    for ip in range(2):
        x = x_all[ip].astype(F32)
        att_in[ip * rows : (ip + 1) * rows, :] = (x * inverse_rms(x) * gains[0:1]).astype(BF16)
    serve()
    cos, sin = cs[...], sn[...]

    def rope(values):
        return values * cos + swap_halves(values) * sin

    for tile in range(wide // 256):
        lin = dot_plain(att_in[...], w_all[:, tile * 256 : (tile + 1) * 256])
        for h in range(2):
            col = tile * 256 + h * 128
            part = lin[:, h * 128 : (h + 1) * 128]
            if col < q_width:
                q_out[:, col : col + 128] = rope(part).astype(BF16)
            elif col < q_width + k_width:
                rotated = rope(part)
                n = (col - q_width) // 128
                k_out[:, n * 128 : (n + 1) * 128] = rotated.astype(BF16)
                for g, (low, high) in enumerate(split_heads(rotated)):
                    klo[2 * n + g] = low.astype(BF16)
                    khi[2 * n + g] = high.astype(BF16)
            else:
                n = (col - q_width - k_width) // 128
                v_out[:, n * 128 : (n + 1) * 128] = part.astype(BF16)
                for g, (low, high) in enumerate(split_heads(part)):
                    vlo[2 * n + g] = low.astype(BF16)
                    vhi[2 * n + g] = high.astype(BF16)
    serve()
    ratio = q_width // k_width
    scale = HEAD_DIM**-0.5
    heads = q_width // HEAD_DIM

    def save_probs(head):
        return pltpu.make_async_copy(pr.at[head], pr_out.at[head], pr_sem.at[head])

    for pair in range(heads // 2):
        lanes = slice(pair * 128, (pair + 1) * 128)
        out = None
        for side, (keys, vals) in enumerate(((klo, vlo), (khi, vhi))):
            head = 2 * pair + side
            g = head // ratio
            scores = dot_last(q_out[:, lanes], keys[g]) * scale
            scores = jnp.where(vis[...] > 0, scores, MASK_FILL)
            top = jnp.max(scores, axis=1, keepdims=True)
            grown = jnp.exp(scores - top)
            probs = grown / jnp.sum(grown, axis=1, keepdims=True)
            pr[head] = probs
            save_probs(head).start()
            term = dot_plain(probs.astype(BF16), vals[g])
            out = term if out is None else out + term
        att[:, lanes] = out.astype(BF16)
        serve(upto=7)
    while len(events) > 7:
        serve()
    for k in range(4):
        gw.join(k)
    wo_save = pltpu.make_async_copy(wo_all, wo_out_all, loc.at[2])
    wo_save.start()
    opart[...] = dot_plain(att[row_block(1 - i), :], wo_all[...]).astype(BF16)
    give_o = remote(opart, orecv, xs.at[5], xr.at[5], p.over_x())
    give_o.start()
    experts_out[2].start()
    hid[...] = tok[...].astype(F32) + dot_plain(att[row_block(i), :], wo_all[...])
    serve()
    serve()
    give_o.wait_recv()
    state = hid[...] + orecv[...].astype(F32)
    hid[...] = state
    ffn_in = (state * inverse_rms(state) * gains[1:2]).astype(BF16)
    fe[:, :width] = ffn_in
    logits = dot_plain(ffn_in, narrow)
    chosen = hit[...] > 0
    logits = jnp.where(chosen, logits, MASK_FILL)
    grown = jnp.where(chosen, jnp.exp(logits - jnp.max(logits, axis=1, keepdims=True)), 0.0)
    gate = grown / jnp.sum(grown, axis=1, keepdims=True)
    gates[...] = gate
    gate = gate * kept[...]
    gate_high = gate.astype(BF16).astype(F32)
    fe[:, width:] = (gate_high + pltpu.roll(gate - gate_high, experts, 1)).astype(BF16)
    while events:
        serve()
    for k in range(4):
        gc.join(k)
    for one in experts_out:
        one.wait()
    for one in give_w + [give_x, give_o]:
        one.wait_send()
    for g in (ga, gb, gw, gc):
        g.drain()
    w_save.wait()
    wo_save.wait()
    for head in range(heads):
        save_probs(head).wait()


def middle_kernel(
    fe, cot_all, eg, eu, ed, egp, eup, edp,
    total, mixp, og_own, ou_own, od_own, egr, eur, od_peer,
    f_all, part, core_in, y_in, a_in, wg, wu, wd, cot, og, h1, h2, hidden, gp, up, mix, sg, su, sd, tg, tu,
    ga_s, ga_r, sc_s, sc_r, loc, cot_sem, mix_sem, xs, xr,
):
    p = Place()
    i, e = p.i, p.e
    rows = fe.shape[0]
    group = 4 * rows
    width = og.shape[1]
    half = width // 2
    experts = 16

    def block_rows(block):
        return pl.ds(pl.multiple_of(block * rows, rows), rows)

    def group_rows(a1):
        return pl.ds(pl.multiple_of(a1 * group, group), group)

    def half_rows(ip):
        return pl.ds(pl.multiple_of(ip * half, half), half)

    f_all[block_rows(e), :] = fe[...]
    p.barrier()
    g = Gather(p, lambda block: f_all.at[block_rows(block)], ga_s, ga_r)
    g.begin()

    loads = []
    for ip, (a1, a2, a3) in ((i, (eg, eu, ed)), (1 - i, (egp, eup, edp))):
        loads.append((a1, wg.at[half_rows(ip)]))
        loads.append((a2, wu.at[half_rows(ip)]))
        loads.append((a3, wd.at[:, half_rows(ip)]))
    loads = [pltpu.make_async_copy(src, dst, loc.at[n]) for n, (src, dst) in enumerate(loads)]
    for one in loads:
        one.start()

    def fetch(k):
        return pltpu.make_async_copy(cot_all.at[p.order(k)], cot.at[k % 2], cot_sem.at[k % 2])

    def store_mix(a1):
        return pltpu.make_async_copy(mix, mixp.at[a1], mix_sem)

    fetch(0).start()
    sc = Scatter(p, lambda a1, b1: part.at[block_rows(a1 * 4 + b1)], core_in, y_in, a_in, sc_s, sc_r)
    lane = lane_iota((group, NAR))

    def first(k):
        here = group_rows(p.order(k))
        if k < 3:
            fetch(k + 1).start()
        h1[...] = dot_plain(f_all[here, :width], wg[...])
        h2[...] = dot_plain(f_all[here, :width], wu[...])

    def gate_of(k):
        meta = f_all[group_rows(p.order(k)), width:].astype(F32)
        return jnp.sum(jnp.where((lane == e) | (lane == e + experts), meta, 0.0), axis=1, keepdims=True)

    def second(k):
        here = group_rows(p.order(k))
        fetch(k).wait()
        og[here, :] = (gate_of(k) * cot[k % 2].astype(F32)).astype(BF16)
        hg = dot_last(og[here, :], wd[...])
        s = jax.nn.sigmoid(h1[...])
        gp[here, :] = (hg * h2[...] * s * (1.0 + h1[...] * (1.0 - s))).astype(BF16)
        up[here, :] = (hg * (h1[...] * s)).astype(BF16)
        hidden[here, :] = (h1[...] * s * h2[...]).astype(BF16)

    def third(k):
        here = group_rows(p.order(k))

        @pl.loop(0, 3)
        def _(n):
            cols = pl.ds(pl.multiple_of(n * 512, 512), 512)
            part[here, cols] = (dot_last(gp[here, :], wg[cols, :]) + dot_last(up[here, :], wu[cols, :])).astype(BF16)

    def fourth(k):
        a1 = p.order(k)
        here = group_rows(a1)
        if k > 0:
            store_mix(p.order(k - 1)).wait()
        gate = gate_of(k)

        def project(n, gate_grad):
            cols = pl.ds(pl.multiple_of(n * 512, 512), 512)
            out = dot_plain(hidden[here, :], wd[:, cols]).astype(BF16).astype(F32)
            mix[:, cols] = (gate * out).astype(BF16)
            return gate_grad + jnp.sum(out * cot[k % 2, :, cols].astype(F32), axis=1, keepdims=True)

        gate_grad = lax.fori_loop(0, 3, project, jnp.zeros((group, 1), F32))
        store_mix(a1).start()
        high = gate_grad.astype(BF16).astype(F32)
        part[here, width:] = jnp.where(
            lane == e, high, jnp.where(lane == e + experts, gate_grad - high, 0.0)
        ).astype(BF16)
        sc.start(a1)

    g.cross(0)
    g.phase(1)
    g.join(0)
    for one in loads:
        one.wait()
    first(0)
    second(0)
    g.phase(2)
    g.cross(1)
    third(0)
    fourth(0)
    g.join(1)
    first(1)
    second(1)
    g.phase(3)
    g.cross(2)
    sc.core(p.order(0))
    third(1)
    fourth(1)
    g.join(2)
    first(2)
    sc.core(p.order(1))
    second(2)
    g.cross(3)
    third(2)
    fourth(2)
    g.join(3)
    first(3)
    sc.core(p.order(2))
    second(3)
    third(3)
    sc.cross(p.order(0))
    fourth(3)

    tile = 256
    tiles = half // tile

    def rows_of(ip, n):
        return pl.ds(pl.multiple_of(ip * half + n * tile, tile), tile)

    def grads(ip, rhs, dst):
        @pl.loop(0, tiles)
        def _(n):
            dst[pl.ds(pl.multiple_of(n * tile, tile), tile), :] = dot_first(f_all[:, rows_of(ip, n)], rhs[...]).astype(
                dst.dtype
            )

    def down_grads(ip, dst):
        @pl.loop(0, tiles)
        def _(n):
            dst[:, pl.ds(pl.multiple_of(n * tile, tile), tile)] = dot_first(hidden[...], og[:, rows_of(ip, n)]).astype(
                dst.dtype
            )

    give_g = remote(tg, egr, xs.at[0], xr.at[0], p.over_x())
    give_u = remote(tu, eur, xs.at[1], xr.at[1], p.over_x())
    grads(1 - i, gp, tg)
    give_g.start()
    sc.core(p.order(3))
    grads(1 - i, up, tu)
    give_u.start()
    grads(i, gp, sg)
    outs = [
        pltpu.make_async_copy(src, dst, loc.at[n]) for n, (src, dst) in enumerate(((sg, og_own), (su, ou_own), (sd, od_own)))
    ]
    outs[0].start()
    sc.cross(p.order(1))
    grads(i, up, su)
    outs[1].start()
    down_grads(i, sd)
    outs[2].start()
    sc.cross(p.order(2))
    down_grads(1 - i, od_peer)
    sc.cross(p.order(3))
    sc.finish()
    total[...] = sc.total()
    store_mix(p.order(3)).wait()
    for one in outs:
        one.wait()
    give_g.wait()
    give_u.wait()
    g.drain()
    sc.drain()


def back_kernel(
    total, hid, gates, kept, cot, cs, sn, kk, vv,
    mixp, od_peer, w_in, wo_in, x_in, att_in_in, q_in, pr_in, att_in2,
    out, tok_grad, dq_out, dk_out, dv_out, dwo_out, gains_out, edr,
    w_all, wo_all, x_all, att_in, q, pr, att, klo, khi, vlo, vhi, bg, ag, dq, dk, dv, small_ref, asend, arecv, state,
    mpart, m_core, m_y, m_a, opart, o_core, o_y, o_a, wpart, w_core, w_y, w_a, wsend, wrecv,
    sm_s, sm_r, so_s, so_r, sw_s, sw_r, xs, xr, loc,
):
    p = Place()
    i, e = p.i, p.e
    rows, width = cot.shape
    q_width, k_width = q.shape[1], kk.shape[1]
    wide = q_width + 2 * k_width
    depth = dq_out.shape[0]
    plane = 16 * depth
    experts = 16
    ratio = q_width // k_width
    scale = HEAD_DIM**-0.5

    def row_block(ip):
        return pl.ds(pl.multiple_of(ip * rows, rows), rows)

    load_mix = [pltpu.make_async_copy(mixp.at[a1], mpart.at[a1], loc.at[7 + a1]) for a1 in range(4)]
    pairs = ((w_in, w_all), (wo_in, wo_all), (x_in, x_all), (att_in_in, att_in), (q_in, q), (pr_in, pr), (att_in2, att))
    load_w, load_wo, load_x, load_ai, load_q, load_pr, load_att = [
        pltpu.make_async_copy(src, dst, loc.at[n]) for n, (src, dst) in enumerate(pairs)
    ]
    load_w.start()
    for one in load_mix:
        one.start()
    for one in (load_wo, load_att, load_q, load_pr, load_x, load_ai):
        one.start()
    p.barrier()
    sm = Scatter(p, lambda a1, b1: mpart.at[a1, row_block(b1)], m_core, m_y, m_a, sm_s, sm_r)
    so = Scatter(
        p,
        lambda a1, b1: opart.at[pl.ds(pl.multiple_of((a1 * 4 + b1) * depth, 16), depth)],
        o_core, o_y, o_a, so_s, so_r,
    )
    sw = Scatter(
        p,
        lambda a1, b1: wpart.at[:, pl.ds(pl.multiple_of((a1 * 4 + b1) * depth, 16), depth)],
        w_core, w_y, w_a, sw_s, sw_r,
    )
    near = [p.order(k) for k in range(4)]
    for a1 in range(4):
        load_mix[a1].wait()
        sm.start(a1)

    load_w.wait()
    narrow = w_all[:, wide:]
    gains = gain_rows(narrow, experts)
    lane = lane_iota((rows, NAR))
    meta = total[:, width:]
    gate_grad = (meta + pltpu.roll(meta, NAR - experts, 1)) * kept[...]
    gate = gates[...]
    logit_grad = (gate * (gate_grad - jnp.sum(gate * gate_grad, axis=1, keepdims=True))).astype(BF16)
    ffn_grad = total[:, :width] + dot_last(logit_grad, narrow)
    hidden = hid[...]
    r2 = inverse_rms(hidden)
    n2 = hidden * r2
    d2 = ffn_grad * gains[1:2]
    state[...] = cot[...].astype(F32) + r2 * (d2 - n2 * jnp.mean(d2 * n2, axis=1, keepdims=True))
    bg[row_block(i), :] = state[...].astype(BF16)
    give_b = remote(bg.at[row_block(i)], bg.at[row_block(i)], xs.at[0], xr.at[0], p.over_x())
    take_b = remote(bg.at[row_block(1 - i)], bg.at[row_block(1 - i)], xs.at[0], xr.at[0], p.over_x())
    give_b.start()
    give_d = remote(od_peer, edr, xs.at[2], xr.at[2], p.over_x())
    give_d.start()
    for k in (3, 2, 1):
        sm.core(near[k])
    ones = jnp.where(lane == experts + 1, 1.0, 0.0).astype(BF16)
    gain_term = ffn_grad * n2
    gain_high = gain_term.astype(BF16)
    gain_low = (gain_term - gain_high.astype(F32)).astype(BF16)
    ffn_in = (n2 * gains[1:2]).astype(BF16)
    small_ref[...] = dot_first(ffn_in, logit_grad) + dot_first(gain_high, ones) + dot_first(gain_low, ones)

    for n in range(k_width // 128):
        for tile, los, his in ((kk, klo, khi), (vv, vlo, vhi)):
            for g, (low, high) in enumerate(split_heads(tile[:, n * 128 : (n + 1) * 128].astype(F32))):
                los[2 * n + g] = low.astype(BF16)
                his[2 * n + g] = high.astype(BF16)
    dk[...] = jnp.zeros_like(dk)
    dv[...] = jnp.zeros_like(dv)
    cos, sin = cs[...], sn[...]
    low_lane = lane_iota((2 * rows, 128)) < HEAD_DIM

    def unrope(values):
        return values * cos - swap_halves(values) * sin

    for one in (load_wo, load_att, load_q, load_pr, load_x, load_ai):
        one.wait()
    take_b.wait_recv()
    for n in range(q_width // 256):
        lanes = slice(n * 256, (n + 1) * 256)
        ag[:, lanes] = dot_last(bg[...], wo_all[lanes, :]).astype(BF16)
    for pair in range(q_width // 128):
        lanes = slice(pair * 128, (pair + 1) * 128)
        grad_in = ag[:, lanes]
        q_pair = q[:, lanes]
        q_grad = None
        for side, (keys, vals) in enumerate(((klo, vlo), (khi, vhi))):
            head = 2 * pair + side
            g = head // ratio
            probs = pr[head]
            prob_grad = dot_last(grad_in, vals[g])
            shift = jnp.sum(probs * prob_grad, axis=1, keepdims=True)
            score_grad = (probs * (prob_grad - shift)).astype(BF16)
            term = dot_plain(score_grad, keys[g])
            q_grad = term if q_grad is None else q_grad + term
            mine = low_lane if side == 0 else jnp.logical_not(low_lane)
            k_term = jnp.where(mine, dot_first(score_grad, q_pair), 0.0)
            v_term = jnp.where(mine, dot_first(probs.astype(BF16), grad_in), 0.0)
            if g % 2 != side:
                k_term = pltpu.roll(k_term, HEAD_DIM, 1)
                v_term = pltpu.roll(v_term, HEAD_DIM, 1)
            tile = slice((g // 2) * 128, (g // 2 + 1) * 128)
            dk[:, tile] += k_term
            dv[:, tile] += v_term
        dq[:, lanes] = unrope(scale * q_grad).astype(BF16)
        if pair in (2, 4):
            sm.cross(near[4 - pair // 2])
    for n in range(k_width // 128):
        lanes = slice(n * 128, (n + 1) * 128)
        dq[:, q_width + n * 128 : q_width + (n + 1) * 128] = unrope(scale * dk[:, lanes]).astype(BF16)
        dq[:, q_width + k_width + n * 128 : q_width + k_width + (n + 1) * 128] = dv[:, lanes].astype(BF16)

    pick = jnp.where(lane == experts, 1.0, 0.0).astype(BF16)
    for first in range(2):
        ip = 1 - i if first == 0 else i
        part = dot_last(dq[row_block(ip), :], w_all[:, :wide])
        x = x_all[ip].astype(F32)
        term = part * (x * inverse_rms(x))
        high = term.astype(BF16)
        low = (term - high.astype(F32)).astype(BF16)
        small_ref[...] += dot_first(high, pick) + dot_first(low, pick)
        if first == 0:
            asend[...] = part.astype(BF16)
            give_a = remote(asend, arecv, xs.at[1], xr.at[1], p.over_x())
            give_a.start()
    back = part
    for ip in range(2):
        wpart[ip, :, wide:] = small_ref[ip * plane : (ip + 1) * plane, :].astype(BF16)
    step = plane // 2
    for turn in range(2):
        n = near[3 - 3 * turn] // 2
        for ip in range(2):
            block = pl.ds(pl.multiple_of(n * step, 128), step)
            lanes = pl.ds(pl.multiple_of(ip * plane + n * step, 128), step)
            wpart[ip, block, :wide] = dot_first(att_in[:, lanes], dq[...]).astype(BF16)
        sw.start(near[3 - 2 * turn])
        sw.start(near[2 - 2 * turn])
    for k in (3, 2, 1, 0):
        sw.core(near[k])
    sm.cross(near[1])
    sm.core(near[0])
    for n in range(q_width // 256):
        lanes = slice(n * 256, (n + 1) * 256)
        opart[lanes, :] = dot_first(att[:, lanes], bg[...]).astype(BF16)
    for k in (3, 2, 1, 0):
        so.start(near[k])
    sw.cross(near[3])
    for k in (3, 2, 1, 0):
        so.core(near[k])
    give_a.wait_recv()
    attn_grad = back + arecv[...].astype(F32)
    x = x_all[i].astype(F32)
    r1 = inverse_rms(x)
    n1 = x * r1
    d1 = attn_grad * gains[0:1]
    tok_grad[...] = (state[...] + r1 * (d1 - n1 * jnp.mean(d1 * n1, axis=1, keepdims=True))).astype(BF16)
    for k in (2, 1, 0):
        sw.cross(near[k])
    sw.finish()
    wsend[...] = sw.total()
    give_s = remote(wsend.at[1 - i], wrecv, xs.at[3], xr.at[3], p.over_x())
    give_s.start()

    def place_half(ip, values):
        dq_out[:, pl.ds(pl.multiple_of(ip * q_width, 128), q_width)] = values[:, :q_width]
        dk_out[:, pl.ds(pl.multiple_of(ip * k_width, 128), k_width)] = values[:, q_width : q_width + k_width]
        dv_out[:, pl.ds(pl.multiple_of(ip * k_width, 128), k_width)] = values[:, q_width + k_width : wide]

    mine = wsend[i]
    place_half(i, mine)
    sm.cross(near[0])
    sm.finish()
    out[...] = (hid[...] + sm.total()).astype(BF16)
    for k in (3, 2, 1, 0):
        so.cross(near[k])
    so.finish()
    dwo_out[...] = so.total()
    give_s.wait_recv()
    theirs = wrecv[...]
    place_half(1 - i, theirs)
    gains_out[...] = mine[:, wide:] + theirs[:, wide:]
    give_d.wait()
    for one in (give_b, give_a, give_s):
        one.wait_send()
    for s in (sm, so, sw):
        s.drain()


def finish_kernel(
    og_own, ou_own, od_own, egr, eur, edr, out, tok, dq, dk, dv, dwo, gains,
    out_o, tok_o, dq_o, dk_o, dv_o, dwo_o, ga_o, gf_o, gr_o, eg_o, eu_o, ed_o,
):
    eg_o[0] = og_own[...] + egr[...].astype(F32)
    eu_o[0] = ou_own[...] + eur[...].astype(F32)
    ed_o[0] = od_own[...] + edr[...].astype(F32)

    @pl.when(pl.program_id(0) == 0)
    def _():
        for src, dst in ((out, out_o), (tok, tok_o), (dq, dq_o), (dk, dk_o), (dv, dv_o), (dwo, dwo_o)):
            dst[...] = src[...]
        experts = gr_o.shape[0]
        rows = turned(gains[...])
        ga_o[...] = rows[experts : experts + 1]
        gf_o[...] = rows[experts + 1 : experts + 2]
        gr_o[...] = rows[:experts]


def paired_body(
    tokens, cotangent, norm_attn, w_query, key_projection, value_projection, w_out, norm_ffn, w_router,
    expert_gate, expert_up, expert_down, routes, slot_order, doc_lengths, deal,
):
    rows, width = tokens.shape
    depth = w_query.shape[0]
    experts = 16
    q_width = w_query.shape[1] // 2
    k_width = key_projection.shape[1] // 2
    wide = q_width + 2 * k_width
    ff = expert_gate.shape[2]
    half = width // 2
    vm = pl.BlockSpec(memory_space=pltpu.VMEM)
    hb = pl.BlockSpec(memory_space=pl.ANY)
    sm = pl.BlockSpec(memory_space=pltpu.SMEM)

    def shaped(*dims, dtype=BF16):
        return jax.ShapeDtypeStruct(dims, dtype)

    def sems(n):
        return pltpu.SemaphoreType.DMA((n,))

    heads = q_width // HEAD_DIM
    groups = k_width // HEAD_DIM
    group_rows = 2 * rows
    by_group = [pltpu.VMEM((groups, group_rows, 128), BF16)] * 4
    (
        w_all, wo_all, x_all, cot_all, egp, eup, edp, att_in, q, kk, vv, pr, att, hid, fe, gates, cs, sn, kept,
    ) = pl.pallas_call(
        front_kernel,
        name="front",
        out_shape=(
            shaped(2 * 16 * depth, wide + NAR),
            shaped(16 * depth, width),
            shaped(2, rows, width),
            shaped(4, 4 * rows, width),
            shaped(half, ff),
            shaped(half, ff),
            shaped(ff, half),
            shaped(group_rows, width),
            shaped(group_rows, q_width),
            shaped(group_rows, k_width),
            shaped(group_rows, k_width),
            shaped(heads, group_rows, group_rows, dtype=F32),
            shaped(group_rows, q_width),
            shaped(rows, width, dtype=F32),
            shaped(rows, width + NAR),
            shaped(rows, NAR, dtype=F32),
            shaped(group_rows, 128, dtype=F32),
            shaped(group_rows, 128, dtype=F32),
            shaped(rows, NAR, dtype=F32),
        ),
        in_specs=[vm] * 8 + [hb] * 4 + [vm, vm, sm, vm],
        out_specs=(hb, hb, vm, hb, hb, hb, hb, vm, vm, vm, vm, hb) + (vm,) * 7,
        scratch_shapes=[
            pltpu.VMEM((2 * 16 * depth, wide + NAR), BF16),
            pltpu.VMEM((16 * depth, width), BF16),
            pltpu.VMEM((heads, group_rows, group_rows), F32),
            pltpu.VMEM((group_rows, group_rows), F32),
            pltpu.VMEM((rows, NAR), F32),
        ]
        + by_group
        + [pltpu.VMEM((rows, width), BF16)] * 2
        + [sems(Gather.SENDS), sems(Gather.RECVS)] * 4
        + [sems(10), sems(10), sems(3), sems(heads)],
        compiler_params=pltpu.CompilerParams(collective_id=1, has_side_effects=True, vmem_limit_bytes=56 << 20),
    )(
        tokens, w_query, key_projection, value_projection, w_router.T, norm_attn[None], norm_ffn[None], w_out,
        cotangent, expert_gate[0], expert_up[0], expert_down[0], routes.T, slot_order, doc_lengths,
        deal.reshape(1, -1),
    )

    part = [pltpu.VMEM((16 * rows, width + NAR), BF16)]
    (total, mixp, og_own, ou_own, od_own, egr, eur, od_peer) = pl.pallas_call(
        middle_kernel,
        name="middle",
        out_shape=(
            shaped(rows, width + NAR, dtype=F32),
            shaped(4, 4 * rows, width),
            shaped(half, ff, dtype=F32),
            shaped(half, ff, dtype=F32),
            shaped(ff, half, dtype=F32),
            shaped(half, ff),
            shaped(half, ff),
            shaped(ff, half),
        ),
        in_specs=[vm] + [hb] * 7,
        out_specs=(vm, hb, hb, hb, hb, hb, hb, vm),
        scratch_shapes=part
        + part
        + [
            pltpu.VMEM((4, 2, rows, width + NAR), BF16),
            pltpu.VMEM((4, rows, width + NAR), BF16),
            pltpu.VMEM((4, rows, width + NAR), BF16),
            pltpu.VMEM((width, ff), BF16),
            pltpu.VMEM((width, ff), BF16),
            pltpu.VMEM((ff, width), BF16),
            pltpu.VMEM((2, 4 * rows, width), BF16),
            pltpu.VMEM((16 * rows, width), BF16),
            pltpu.VMEM((4 * rows, ff), F32),
            pltpu.VMEM((4 * rows, ff), F32),
            pltpu.VMEM((16 * rows, ff), BF16),
            pltpu.VMEM((16 * rows, ff), BF16),
            pltpu.VMEM((16 * rows, ff), BF16),
            pltpu.VMEM((4 * rows, width), BF16),
            pltpu.VMEM((half, ff), F32),
            pltpu.VMEM((half, ff), F32),
            pltpu.VMEM((ff, half), F32),
            pltpu.VMEM((half, ff), BF16),
            pltpu.VMEM((half, ff), BF16),
            sems(Gather.SENDS),
            sems(Gather.RECVS),
            sems(Scatter.SENDS),
            sems(Scatter.RECVS),
            sems(6),
            sems(2),
            pltpu.SemaphoreType.DMA(()),
            sems(2),
            sems(2),
        ],
        compiler_params=pltpu.CompilerParams(collective_id=2, has_side_effects=True, vmem_limit_bytes=62 << 20),
    )(fe, cot_all, expert_gate[0], expert_up[0], expert_down[0], egp, eup, edp)

    def landing(block):
        return [
            pltpu.VMEM((4, 2) + block, BF16),
            pltpu.VMEM((4,) + block, BF16),
            pltpu.VMEM((4,) + block, BF16),
        ]

    (out, tok_grad, dq, dk, dv, dwo, gains, edr) = pl.pallas_call(
        back_kernel,
        name="back",
        out_shape=(
            shaped(rows, width),
            shaped(rows, width),
            shaped(depth, 2 * q_width, dtype=F32),
            shaped(depth, 2 * k_width, dtype=F32),
            shaped(depth, 2 * k_width, dtype=F32),
            shaped(depth, width, dtype=F32),
            shaped(depth, NAR, dtype=F32),
            shaped(ff, half),
        ),
        in_specs=[vm] * 9 + [hb] * 9,
        out_specs=(vm, vm, vm, vm, vm, vm, vm, hb),
        scratch_shapes=[
            pltpu.VMEM((2 * 16 * depth, wide + NAR), BF16),
            pltpu.VMEM((16 * depth, width), BF16),
            pltpu.VMEM((2, rows, width), BF16),
            pltpu.VMEM((group_rows, width), BF16),
            pltpu.VMEM((group_rows, q_width), BF16),
            pltpu.VMEM((heads, group_rows, group_rows), F32),
            pltpu.VMEM((group_rows, q_width), BF16),
        ]
        + by_group
        + [
            pltpu.VMEM((group_rows, width), BF16),
            pltpu.VMEM((group_rows, q_width), BF16),
            pltpu.VMEM((group_rows, wide), BF16),
            pltpu.VMEM((group_rows, k_width), F32),
            pltpu.VMEM((group_rows, k_width), F32),
            pltpu.VMEM((2 * 16 * depth, NAR), F32),
            pltpu.VMEM((rows, width), BF16),
            pltpu.VMEM((rows, width), BF16),
            pltpu.VMEM((rows, width), F32),
            pltpu.VMEM((4, 4 * rows, width), BF16),
        ]
        + landing((rows, width))
        + [pltpu.VMEM((16 * depth, width), BF16)]
        + landing((depth, width))
        + [pltpu.VMEM((2, 16 * depth, wide + NAR), BF16)]
        + landing((2, depth, wide + NAR))
        + [
            pltpu.VMEM((2, depth, wide + NAR), F32),
            pltpu.VMEM((depth, wide + NAR), F32),
        ]
        + [sems(Scatter.SENDS), sems(Scatter.RECVS)] * 3
        + [sems(4), sems(4), sems(11)],
        compiler_params=pltpu.CompilerParams(collective_id=3, has_side_effects=True, vmem_limit_bytes=62 << 20),
    )(
        total, hid, gates, kept, cotangent, cs, sn, kk, vv,
        mixp, od_peer, w_all, wo_all, x_all, att_in, q, pr, att,
    )

    steps = 4

    def cut(*dims):
        return pl.BlockSpec((dims[0] // steps,) + dims[1:], lambda n: (n,) + (0,) * (len(dims) - 1))

    def cut_out(*dims):
        return pl.BlockSpec((1, dims[0] // steps) + dims[1:], lambda n: (0, n) + (0,) * (len(dims) - 1))

    def whole(*dims):
        return pl.BlockSpec(dims, lambda n: (0,) * len(dims))

    mats = ((half, ff), (half, ff), (ff, half))
    rest = (out, tok_grad, dq, dk, dv, dwo, gains)
    res = pl.pallas_call(
        finish_kernel,
        name="finish",
        grid=(steps,),
        out_shape=tuple(jax.ShapeDtypeStruct(r.shape, r.dtype) for r in rest[:6])
        + (shaped(1, depth, dtype=F32), shaped(1, depth, dtype=F32), shaped(experts, depth, dtype=F32))
        + tuple(shaped(1, *m, dtype=F32) for m in mats),
        in_specs=[cut(*m) for m in mats] * 2 + [whole(*r.shape) for r in rest],
        out_specs=tuple(whole(*r.shape) for r in rest[:6])
        + (whole(1, depth), whole(1, depth), whole(experts, depth))
        + tuple(cut_out(*m) for m in mats),
        compiler_params=pltpu.CompilerParams(vmem_limit_bytes=62 << 20),
    )(og_own, ou_own, od_own, egr, eur, edr, *rest)
    out, tok_grad, dq, dk, dv, dwo, g_attn, g_ffn, g_router, eg, eu, ed = res
    return (
        out, tok_grad, g_attn.reshape(-1), dq, dk, dv, dwo, g_ffn.reshape(-1), g_router.T, eg, eu, ed,
    )


def general_body(
    tokens,
    cotangent,
    norm_attn,
    w_query,
    key_projection,
    value_projection,
    w_out,
    norm_ffn,
    w_router,
    expert_gate,
    expert_up,
    expert_down,
    routes,
    slot_order,
    doc_lengths,
    deal,
):
    gain_attn, full_query, gathered_key, gathered_value, full_out, gain_ffn, full_router = (
        lax.all_gather(norm_attn, ("dp", "expert"), axis=0, tiled=True),
        lax.all_gather(w_query, ("dp", "expert"), axis=0, tiled=True),
        lax.all_gather(key_projection, ("dp", "expert"), axis=0, tiled=True),
        lax.all_gather(value_projection, ("dp", "expert"), axis=0, tiled=True),
        lax.all_gather(w_out, ("dp", "expert"), axis=0, tiled=True),
        lax.all_gather(norm_ffn, ("dp", "expert"), axis=0, tiled=True),
        lax.all_gather(w_router, ("dp", "expert"), axis=0, tiled=True),
    )
    full_gate, full_up, full_down = (
        lax.all_gather(expert_gate[0], "dp", axis=0, tiled=True),
        lax.all_gather(expert_up[0], "dp", axis=0, tiled=True),
        lax.all_gather(expert_down[0], "dp", axis=1, tiled=True),
    )
    count_of_rows, model_width = tokens.shape
    top_count = routes.shape[1]
    experts = full_router.shape[1]
    owners = lax.axis_size("expert")
    capacity = 9 * count_of_rows * top_count // (8 * experts)
    head_count = full_query.shape[1] // HEAD_DIM
    groups = gathered_key.shape[1] // HEAD_DIM
    head_ratio = head_count // groups
    scale_attn = gain_attn.astype(jnp.float32)
    scale_ffn = gain_ffn.astype(jnp.float32)
    score_scale = HEAD_DIM ** (-0.5)
    group_places = deal[:, 0, :].reshape(-1)
    group_docs, group_offsets = doc_layout(doc_lengths[0], group_places)
    shard_start = lax.axis_index("dp") * count_of_rows
    places = lax.dynamic_slice_in_dim(group_places, shard_start, count_of_rows)
    doc_ids = lax.dynamic_slice_in_dim(group_docs, shard_start, count_of_rows)
    offsets = lax.dynamic_slice_in_dim(group_offsets, shard_start, count_of_rows)
    cosine_lookup, sine_lookup = rope_tables(offsets, HEAD_DIM)
    inputs = tokens.astype(jnp.float32)
    inverse_one = lax.rsqrt(jnp.mean(inputs * inputs, axis=1, keepdims=True) + NORM_EPS)
    normed_one = inputs * inverse_one
    attention_input = (normed_one * scale_attn).astype(jnp.bfloat16)
    query_rows = apply_rotation(
        dot_plain(attention_input, full_query).reshape(count_of_rows, head_count, HEAD_DIM),
        cosine_lookup,
        sine_lookup,
    ).astype(jnp.bfloat16)
    key_matrix_rows = apply_rotation(
        dot_plain(attention_input, gathered_key).reshape(count_of_rows, groups, HEAD_DIM),
        cosine_lookup,
        sine_lookup,
    ).astype(jnp.bfloat16)
    value_matrix_rows = dot_plain(attention_input, gathered_value).astype(jnp.bfloat16)
    all_keys, all_values = (
        lax.all_gather(key_matrix_rows.reshape(count_of_rows, -1), "dp", axis=0, tiled=True),
        lax.all_gather(value_matrix_rows, "dp", axis=0, tiled=True),
    )
    group_rows = all_keys.shape[0]
    key_span = math.gcd(group_rows, 512)
    span_count = group_rows // key_span
    key_spans = (
        all_keys.reshape(span_count, key_span, groups, HEAD_DIM),
        all_values.reshape(span_count, key_span, groups, HEAD_DIM),
        group_places.reshape(span_count, key_span),
        group_docs.reshape(span_count, key_span),
    )
    grouped_q = query_rows.reshape(count_of_rows, groups, head_ratio, HEAD_DIM)

    def span_scores(key_block, key_place, key_doc):
        visible = (doc_ids[:, None] == key_doc[None, :]) & (places[:, None] >= key_place[None, :])
        scores = (
            jnp.einsum("qgrd,kgd->grqk", grouped_q, key_block, preferred_element_type=jnp.float32)
            * score_scale
        )
        return jnp.where(visible[None, None], scores, MASK_FILL)

    def extent(carry, operands):
        run_max, run_sum = carry
        key_block, value_block, key_place, key_doc = operands
        scores = span_scores(key_block, key_place, key_doc)
        new_max = jnp.maximum(run_max, jnp.max(scores, axis=-1, keepdims=True))
        run_sum = run_sum * jnp.exp(run_max - new_max) + jnp.sum(
            jnp.exp(scores - new_max), axis=-1, keepdims=True
        )
        return ((new_max, run_sum), None)

    stat_shape = (groups, head_ratio, count_of_rows, 1)
    (row_max, row_sum), _ = lax.scan(
        extent,
        (jnp.full(stat_shape, MASK_FILL, jnp.float32), jnp.zeros(stat_shape, jnp.float32)),
        key_spans,
    )
    log_total = row_max + jnp.log(row_sum)

    def weigh_values(running, operands):
        key_block, value_block, key_place, key_doc = operands
        weights = jnp.exp(span_scores(key_block, key_place, key_doc) - log_total).astype(
            jnp.bfloat16
        )
        return (
            running
            + jnp.einsum(
                "grqk,kgd->qgrd", weights, value_block, preferred_element_type=jnp.float32
            ),
            None,
        )

    attended, _ = lax.scan(
        weigh_values,
        jnp.zeros((count_of_rows, groups, head_ratio, HEAD_DIM), jnp.float32),
        key_spans,
    )
    attended = attended.reshape(count_of_rows, head_count * HEAD_DIM).astype(jnp.bfloat16)
    hidden_state = inputs + dot_plain(attended, full_out)
    inverse_two = lax.rsqrt(jnp.mean(hidden_state * hidden_state, axis=1, keepdims=True) + NORM_EPS)
    normed_two = hidden_state * inverse_two
    ffn_in = (normed_two * scale_ffn).astype(jnp.bfloat16)
    logits = dot_plain(ffn_in, full_router)
    route_hits = (routes[:, :, None] == jnp.arange(experts, dtype=jnp.int32)[None, None, :]).astype(
        jnp.float32
    )
    chosen = jnp.sum(route_hits * logits[:, None, :], axis=-1)
    gate_values = jax.nn.softmax(chosen, axis=-1)
    pair_slot, slot_token = assign_slots(routes, slot_order[0], experts, capacity)
    padded_in = jnp.concatenate([ffn_in, jnp.zeros((1, model_width), jnp.bfloat16)], axis=0)
    outgoing = padded_in[slot_token].reshape(owners, capacity, model_width)
    arrived = lax.all_to_all(outgoing, "expert", split_axis=0, concat_axis=0, tiled=True)
    flat_rows = arrived.reshape(-1, model_width)
    gate_pre = dot_plain(flat_rows, full_gate)
    up_pre = dot_plain(flat_rows, full_up)
    hidden = (jax.nn.silu(gate_pre) * up_pre).astype(jnp.bfloat16)
    result = dot_plain(hidden, full_down).astype(jnp.bfloat16).reshape(arrived.shape)
    sent_back = lax.all_to_all(result, "expert", split_axis=0, concat_axis=0, tiled=True)
    exchanged = (
        sent_back,
        arrived,
        gate_pre.reshape(arrived.shape[0], arrived.shape[1], -1),
        up_pre.reshape(arrived.shape[0], arrived.shape[1], -1),
    )
    returned = exchanged[0]
    expert_rows = exchanged[1].reshape(-1, model_width)
    gate_pre = exchanged[2].reshape(expert_rows.shape[0], -1)
    up_pre = exchanged[3].reshape(expert_rows.shape[0], -1)
    out_grad = cotangent.astype(jnp.float32)
    padded_back = jnp.concatenate(
        [returned.reshape(-1, model_width), jnp.zeros((1, model_width), jnp.bfloat16)], axis=0
    )
    slot_grid = pair_slot.reshape(count_of_rows, top_count)
    mixture = jnp.zeros((count_of_rows, model_width), jnp.float32)
    gate_parts = []
    for column in range(top_count):
        picked = padded_back[slot_grid[:, column]].astype(jnp.float32)
        mixture = mixture + gate_values[:, column : column + 1] * picked
        gate_parts.append(jnp.sum(out_grad * picked, axis=1))
    output = (hidden_state + mixture).astype(jnp.bfloat16)
    gate_grad = jnp.stack(gate_parts, axis=1)
    slot_gate = (
        jnp.zeros((experts * capacity + 1,), jnp.float32)
        .at[pair_slot]
        .set(gate_values.reshape(-1))[: experts * capacity]
    )
    padded_grad = jnp.concatenate([out_grad, jnp.zeros((1, model_width), jnp.float32)], axis=0)
    slot_grad = (
        (slot_gate[:, None] * padded_grad[slot_token])
        .astype(jnp.bfloat16)
        .reshape(owners, capacity, model_width)
    )
    arrived_grad = lax.all_to_all(
        slot_grad, "expert", split_axis=0, concat_axis=0, tiled=True
    ).reshape(-1, model_width)
    sigmoid_gate = jax.nn.sigmoid(gate_pre)
    silu_gate = gate_pre * sigmoid_gate
    hidden = (silu_gate * up_pre).astype(jnp.bfloat16)
    hidden_grad = dot_last(arrived_grad, full_down)
    gate_pre_grad = (
        hidden_grad * up_pre * sigmoid_gate * (1.0 + gate_pre * (1.0 - sigmoid_gate))
    ).astype(jnp.bfloat16)
    up_pre_grad = (hidden_grad * silu_gate).astype(jnp.bfloat16)
    down_weight_grad = dot_first(hidden, arrived_grad)
    gate_weight_grad = dot_first(expert_rows, gate_pre_grad)
    up_weight_grad = dot_first(expert_rows, up_pre_grad)
    row_grad = (dot_last(gate_pre_grad, full_gate) + dot_last(up_pre_grad, full_up)).astype(
        jnp.bfloat16
    )
    token_rows_grad = lax.all_to_all(
        row_grad.reshape(owners, capacity, model_width),
        "expert",
        split_axis=0,
        concat_axis=0,
        tiled=True,
    )
    gate_summed, up_summed, down_summed = (
        lax.psum_scatter(
            gate_weight_grad.astype(jnp.bfloat16), "dp", scatter_dimension=0, tiled=True
        ).astype(jnp.float32),
        lax.psum_scatter(
            up_weight_grad.astype(jnp.bfloat16), "dp", scatter_dimension=0, tiled=True
        ).astype(jnp.float32),
        lax.psum_scatter(
            down_weight_grad.astype(jnp.bfloat16), "dp", scatter_dimension=1, tiled=True
        ).astype(jnp.float32),
    )
    dispatch_grad = jax.ops.segment_sum(
        token_rows_grad.reshape(-1, model_width).astype(jnp.float32),
        slot_token,
        num_segments=count_of_rows + 1,
    )[:count_of_rows]
    chosen_grad = gate_values * (
        gate_grad - jnp.sum(gate_values * gate_grad, axis=1, keepdims=True)
    )
    logit_grad = jnp.sum(route_hits * chosen_grad[:, :, None], axis=1).astype(jnp.bfloat16)
    router_grad = dot_first(ffn_in, logit_grad)
    ffn_grad = dispatch_grad + dot_last(logit_grad, full_router)
    ffn_gain_grad = jnp.sum(ffn_grad * normed_two, axis=0)
    scaled_two = ffn_grad * scale_ffn
    state_grad = out_grad + inverse_two * (
        scaled_two - normed_two * jnp.mean(scaled_two * normed_two, axis=1, keepdims=True)
    )
    branch_grad = state_grad.astype(jnp.bfloat16)
    out_weight_grad = dot_first(attended, branch_grad)
    attended_grad = (
        dot_last(branch_grad, full_out)
        .astype(jnp.bfloat16)
        .reshape(count_of_rows, groups, head_ratio, HEAD_DIM)
    )

    def spread_sum(running, operands):
        key_block, value_block, key_place, key_doc = operands
        probs = jnp.exp(span_scores(key_block, key_place, key_doc) - log_total)
        prob_grad = jnp.einsum(
            "qgrd,kgd->grqk", attended_grad, value_block, preferred_element_type=jnp.float32
        )
        return (running + jnp.sum(probs * prob_grad, axis=-1, keepdims=True), None)

    score_shift, _ = lax.scan(spread_sum, jnp.zeros(stat_shape, jnp.float32), key_spans)

    def back_span(running, operands):
        key_block, value_block, key_place, key_doc = operands
        probs = jnp.exp(span_scores(key_block, key_place, key_doc) - log_total)
        prob_grad = jnp.einsum(
            "qgrd,kgd->grqk", attended_grad, value_block, preferred_element_type=jnp.float32
        )
        score_grad = (probs * (prob_grad - score_shift)).astype(jnp.bfloat16)
        running = running + jnp.einsum(
            "grqk,kgd->qgrd", score_grad, key_block, preferred_element_type=jnp.float32
        )
        key_part = (
            jnp.einsum("grqk,qgrd->kgd", score_grad, grouped_q, preferred_element_type=jnp.float32)
            * score_scale
        )
        value_part = jnp.einsum(
            "grqk,qgrd->kgd",
            probs.astype(jnp.bfloat16),
            attended_grad,
            preferred_element_type=jnp.float32,
        )
        return (running, (key_part.reshape(key_span, -1), value_part.reshape(key_span, -1)))

    query_sum, (key_parts, value_parts) = lax.scan(
        back_span, jnp.zeros((count_of_rows, groups, head_ratio, HEAD_DIM), jnp.float32), key_spans
    )
    key_grad, value_sum = (
        lax.psum_scatter(
            key_parts.reshape(group_rows, -1).astype(jnp.bfloat16),
            "dp",
            scatter_dimension=0,
            tiled=True,
        ).astype(jnp.float32),
        lax.psum_scatter(
            value_parts.reshape(group_rows, -1).astype(jnp.bfloat16),
            "dp",
            scatter_dimension=0,
            tiled=True,
        ).astype(jnp.float32),
    )
    query_grad = query_sum * score_scale
    query_lin_grad = unrotate(
        query_grad.reshape(count_of_rows, head_count, HEAD_DIM), cosine_lookup, sine_lookup
    )
    query_lin_grad = query_lin_grad.reshape(count_of_rows, -1).astype(jnp.bfloat16)
    key_lin_grad = (
        unrotate(key_grad.reshape(count_of_rows, groups, HEAD_DIM), cosine_lookup, sine_lookup)
        .reshape(count_of_rows, -1)
        .astype(jnp.bfloat16)
    )
    value_lin_grad = value_sum.astype(jnp.bfloat16)
    query_weight_grad = dot_first(attention_input, query_lin_grad)
    key_weight_grad = dot_first(attention_input, key_lin_grad)
    value_weight_grad = dot_first(attention_input, value_lin_grad)
    attn_grad = (
        dot_last(query_lin_grad, full_query)
        + dot_last(key_lin_grad, gathered_key)
        + dot_last(value_lin_grad, gathered_value)
    )
    attn_gain_grad = jnp.sum(attn_grad * normed_one, axis=0)
    scaled_one = attn_grad * scale_attn
    tokens_grad = (
        state_grad
        + inverse_one
        * (scaled_one - normed_one * jnp.mean(scaled_one * normed_one, axis=1, keepdims=True))
    ).astype(jnp.bfloat16)
    summed = (
        lax.psum_scatter(attn_gain_grad, ("dp", "expert"), scatter_dimension=0, tiled=True),
        lax.psum_scatter(query_weight_grad, ("dp", "expert"), scatter_dimension=0, tiled=True),
        lax.psum_scatter(key_weight_grad, ("dp", "expert"), scatter_dimension=0, tiled=True),
        lax.psum_scatter(value_weight_grad, ("dp", "expert"), scatter_dimension=0, tiled=True),
        lax.psum_scatter(out_weight_grad, ("dp", "expert"), scatter_dimension=0, tiled=True),
        lax.psum_scatter(ffn_gain_grad, ("dp", "expert"), scatter_dimension=0, tiled=True),
        lax.psum_scatter(router_grad, ("dp", "expert"), scatter_dimension=0, tiled=True),
    )
    return (
        output,
        tokens_grad,
        summed[0],
        summed[1],
        summed[2],
        summed[3],
        summed[4],
        summed[5],
        summed[6],
        gate_summed[None],
        up_summed[None],
        down_summed[None],
    )


def solution(mesh):
    in_specs = (
        P(("dp", "expert"), None),
        P(("dp", "expert"), None),
        P(("dp", "expert")),
        P(("dp", "expert"), None),
        P(("dp", "expert"), None),
        P(("dp", "expert"), None),
        P(("dp", "expert"), None),
        P(("dp", "expert")),
        P(("dp", "expert"), None),
        P("expert", "dp", None),
        P("expert", "dp", None),
        P("expert", None, "dp"),
        P(("dp", "expert"), None),
        P(("dp", "expert"), None),
        P("expert", None),
        P(None, "expert", None),
    )
    out_specs = (
        P(("dp", "expert"), None),
        P(("dp", "expert"), None),
        P(("dp", "expert")),
        P(("dp", "expert"), None),
        P(("dp", "expert"), None),
        P(("dp", "expert"), None),
        P(("dp", "expert"), None),
        P(("dp", "expert")),
        P(("dp", "expert"), None),
        P("expert", "dp", None),
        P("expert", "dp", None),
        P("expert", None, "dp"),
    )
    fast = mesh.shape["dp"] == 2 and mesh.shape["expert"] == 16
    body = paired_body if fast else general_body
    return jax.shard_map(body, mesh=mesh, in_specs=in_specs, out_specs=out_specs, check_vma=False)
```

```python
import functools
import math

import jax
import jax.numpy as jnp
from jax import lax
from jax.experimental import pallas as pl
from jax.experimental.pallas import tpu as pltpu
from jax.sharding import PartitionSpec as P

HEAD_DIM = 64


NORM_EPS = 1e-05
MASK_FILL = -1e30
ROPE_BASE = 10000.0


def dot_plain(left_side, right_side):
    return jnp.dot(left_side, right_side, preferred_element_type=jnp.float32)


def dot_last(left_side, right_side):
    return lax.dot_general(
        left_side, right_side, (((1,), (1,)), ((), ())), preferred_element_type=jnp.float32
    )


def dot_first(left_side, right_side):
    return lax.dot_general(
        left_side, right_side, (((0,), (0,)), ((), ())), preferred_element_type=jnp.float32
    )


def doc_layout(lengths, places):
    doc_ends = jnp.cumsum(lengths)
    doc_starts = doc_ends - lengths
    doc_ids = jnp.sum((places[:, None] >= doc_ends[None, :]).astype(jnp.int32), axis=1)
    member = doc_ids[:, None] == jnp.arange(lengths.shape[0], dtype=jnp.int32)[None, :]
    offsets = places - jnp.sum(jnp.where(member, doc_starts[None, :], 0), axis=1)
    return (doc_ids, offsets)


def rope_tables(offsets, head_size):
    half_size = head_size // 2
    frequency = ROPE_BASE ** (-2.0 * jnp.arange(half_size, dtype=jnp.float32) / head_size)
    angles = offsets.astype(jnp.float32)[:, None] * frequency[None, :]
    return (jnp.cos(angles), jnp.sin(angles))


def apply_rotation(values, cosine_lookup, sine_lookup):
    half_size = values.shape[-1] // 2
    first_half = values[..., :half_size]
    second = values[..., half_size:]
    cos_rows = cosine_lookup[:, None, :]
    sin_rows = sine_lookup[:, None, :]
    return jnp.concatenate(
        [first_half * cos_rows - second * sin_rows, second * cos_rows + first_half * sin_rows],
        axis=-1,
    )


def unrotate(gradient, cosine_lookup, sine_lookup):
    half_size = gradient.shape[-1] // 2
    first_half = gradient[..., :half_size]
    second = gradient[..., half_size:]
    cos_rows = cosine_lookup[:, None, :]
    sin_rows = sine_lookup[:, None, :]
    return jnp.concatenate(
        [first_half * cos_rows + second * sin_rows, second * cos_rows - first_half * sin_rows],
        axis=-1,
    )


def assign_slots(routes, take_order, experts, capacity):
    count_of_rows, top_count = routes.shape
    flat_routes = routes.reshape(-1)
    chosen = flat_routes[take_order]
    expert_hits = (chosen[:, None] == jnp.arange(experts, dtype=jnp.int32)[None, :]).astype(
        jnp.int32
    )
    slot_rank = jnp.sum(jnp.cumsum(expert_hits, axis=0) * expert_hits, axis=1) - 1
    slot_index = jnp.where(slot_rank < capacity, chosen * capacity + slot_rank, experts * capacity)
    pair_slot = jnp.zeros((flat_routes.shape[0],), jnp.int32).at[take_order].set(slot_index)
    slot_token = (
        jnp.full((experts * capacity + 1,), count_of_rows, jnp.int32)
        .at[slot_index]
        .set(take_order // top_count)
    )
    return (pair_slot, slot_token[: experts * capacity])


MESH = pl.DeviceIdType.MESH
BF16 = jnp.bfloat16
F32 = jnp.float32
NAR = 128


def remote(src, dst, send_sem, recv_sem, device):
    return pltpu.make_async_remote_copy(
        src_ref=src,
        dst_ref=dst,
        send_sem=send_sem,
        recv_sem=recv_sem,
        device_id=device,
        device_id_type=MESH,
    )


class Place:
    def __init__(self):
        self.i = lax.axis_index("dp")
        self.e = lax.axis_index("expert")
        self.a = self.e // 4
        self.bc = self.e % 4
        self.y = self.bc // 2
        self.c = self.bc % 2

    def over_x(self):
        return (1 - self.i, self.e)

    def over_y(self):
        return (self.i, self.e + 2 - 4 * self.y)

    def over_core(self):
        return (self.i, self.e + 1 - 2 * self.c)

    def order(self, k):
        turn = (1 - 2 * k) * (1 - k // 2)
        inner = self.inner()
        half = self.a // 2
        step = k + inner * turn
        return step + half * (3 - 2 * step)

    def inner(self):
        return (self.a * (3 - self.a)) // 2

    def partner(self):
        return self.a + 1 - 2 * (self.a % 2)

    def barrier(self, whole_plane=False):
        sem = pltpu.get_barrier_semaphore()
        if whole_plane:
            peers = [(self.i, (self.e + shift) % 16) for shift in range(1, 16)]
        else:
            peers = [self.over_y(), self.over_core()]
            for shift in range(1, 4):
                peers.append((self.i, ((self.a + shift) % 4) * 4 + self.bc))
        peers.append(self.over_x())
        for peer in peers:
            pl.semaphore_signal(sem, inc=1, device_id=peer, device_id_type=MESH)
        pl.semaphore_wait(sem, len(peers))


class Gather:
    SENDS = 20
    RECVS = 16

    def __init__(self, place, view, sends, recvs):
        self.p, self.view, self.sends, self.recvs = place, view, sends, recvs

    def copy(self, block, slot, device):
        ref = self.view(block)
        return remote(ref, ref, self.sends.at[slot], self.recvs.at[block], device)

    def right(self, a1):
        return self.copy(a1 * 4 + self.p.bc, a1, (self.p.i, self.p.e + 4))

    def left(self, a1):
        return self.copy(a1 * 4 + self.p.bc, 4 + a1, (self.p.i, self.p.e - 4))

    def across(self, a1):
        return self.copy(a1 * 4 + self.p.bc, 8 + a1, self.p.over_y())

    def core(self, a1, y1):
        return self.copy(a1 * 4 + y1 * 2 + self.p.c, 12 + a1 * 2 + y1, self.p.over_core())

    def landed(self, block):
        self.copy(block, 0, self.p.over_core()).wait_recv()

    def begin(self):
        p = self.p
        self.across(p.a).start()

        @pl.when(p.a < 3)
        def _():
            self.right(p.a).start()

        @pl.when(p.a > 0)
        def _():
            self.left(p.a).start()

        self.core(p.a, p.y).start()

    def phase(self, s):
        p = self.p
        inner = p.inner()
        if s == 1:
            self.along(1)

        @pl.when(inner == 1)
        def _():
            if s < 3:
                self.along(s + 1)

        if s > 1:

            @pl.when(inner == 0)
            def _():
                self.along(s)

    def along(self, k):
        p = self.p
        a1 = p.order(k)
        self.landed(a1 * 4 + p.bc)

        @pl.when((a1 < p.a) & (p.a < 3))
        def _():
            self.right(a1).start()

        @pl.when((a1 > p.a) & (p.a > 0))
        def _():
            self.left(a1).start()

        self.across(a1).start()
        self.core(a1, p.y).start()

    def cross(self, k):
        p = self.p
        a1 = p.order(k)
        self.landed(a1 * 4 + (1 - p.y) * 2 + p.c)
        self.core(a1, 1 - p.y).start()

    def join(self, k):
        p = self.p
        a1 = p.order(k)
        self.landed(a1 * 4 + (1 - p.c))
        self.landed(a1 * 4 + 2 + (1 - p.c))

    def sent(self, k):
        p = self.p
        a1 = p.order(k)

        @pl.when((a1 <= p.a) & (p.a < 3))
        def _():
            self.right(a1).wait_send()

        @pl.when((a1 >= p.a) & (p.a > 0))
        def _():
            self.left(a1).wait_send()

        self.across(a1).wait_send()
        self.core(a1, 0).wait_send()
        self.core(a1, 1).wait_send()

    def drain(self):
        for k in range(4):
            self.sent(k)


class Scatter:
    SENDS = 16
    RECVS = 17

    def __init__(self, place, part, core_in, y_in, a_in, pass_in, sends, recvs):
        self.p, self.part = place, part
        self.core_in, self.y_in, self.a_in, self.pass_in = core_in, y_in, a_in, pass_in
        self.sends, self.recvs = sends, recvs

    def to_core(self, a1, y1):
        p = self.p
        slot = a1 * 2 + y1
        return remote(
            self.part(a1, y1 * 2 + 1 - p.c),
            self.core_in(a1, y1),
            self.sends.at[slot],
            self.recvs.at[slot],
            p.over_core(),
        )

    def to_y(self, a1):
        p = self.p
        return remote(
            self.part(a1, (1 - p.y) * 2 + p.c),
            self.y_in(a1),
            self.sends.at[8 + a1],
            self.recvs.at[8 + a1],
            p.over_y(),
        )

    def to_a(self, a1, slot):
        p = self.p
        return remote(
            self.part(a1, p.bc),
            self.a_in(slot),
            self.sends.at[12 + a1],
            self.recvs.at[12 + slot],
            (p.i, a1 * 4 + p.bc),
        )

    def to_inner(self, a1):
        p = self.p
        return remote(
            self.part(a1, p.bc),
            self.pass_in(a1 % 2),
            self.sends.at[12 + a1],
            self.recvs.at[15 + a1 % 2],
            (p.i, p.partner() * 4 + p.bc),
        )

    def start(self, a1):
        self.to_core(a1, 0).start()
        self.to_core(a1, 1).start()

    def add(self, ref, other):
        ref[...] = (ref[...].astype(F32) + other[...].astype(F32)).astype(ref.dtype)

    def core(self, a1):
        p = self.p
        for y1 in range(2):
            self.to_core(a1, y1).wait_recv()
        self.add(self.part(a1, (1 - p.y) * 2 + p.c), self.core_in(a1, 1 - p.y))
        self.to_y(a1).start()
        self.add(self.part(a1, p.bc), self.core_in(a1, p.y))

    def cross(self, a1):
        p = self.p
        self.to_y(a1).wait_recv()
        self.add(self.part(a1, p.bc), self.y_in(a1))

        @pl.when(a1 == p.partner())
        def _():
            self.to_a(a1, 1).start()

        @pl.when((a1 // 2 != p.a // 2) & (p.inner() == 0))
        def _():
            self.to_inner(a1).start()

    def relay(self, a1):
        p = self.p

        @pl.when((a1 // 2 != p.a // 2) & (p.inner() == 1))
        def _():
            self.to_inner(a1).wait_recv()
            self.add(self.part(a1, p.bc), self.pass_in(a1 % 2))
            self.to_a(a1, 2).start()

    def finish(self):
        for slot in (1, 2):
            self.to_a(self.p.a, slot).wait_recv()

    def total(self):
        own = self.part(self.p.a, self.p.bc)[...].astype(F32)
        return own + self.a_in(1)[...].astype(F32) + self.a_in(2)[...].astype(F32)

    def drain(self):
        p = self.p
        for k in range(4):
            a1 = p.order(k)
            self.to_core(a1, 0).wait_send()
            self.to_core(a1, 1).wait_send()
            self.to_y(a1).wait_send()
            if k:
                self.to_a(a1, 1).wait_send()


class Exchange:
    def __init__(self, place, source, target, sends, recvs):
        self.p, self.source, self.target, self.sends, self.recvs = place, source, target, sends, recvs

    def copy(self, there):
        p = self.p
        return remote(
            self.source.at[there], self.target.at[p.e], self.sends.at[there], self.recvs.at[p.e], (p.i, there)
        )

    def give(self, there):
        @pl.when(there != self.p.e)
        def _():
            self.copy(there).start()

        @pl.when(there == self.p.e)
        def _():
            self.target[there] = self.source[there]

    def take(self, there):
        p = self.p

        @pl.when(there != p.e)
        def _():
            remote(
                self.target.at[there], self.target.at[there], self.sends.at[there], self.recvs.at[there], (p.i, there)
            ).wait_recv()

    def drain(self):
        @pl.loop(0, 16)
        def _(there):
            @pl.when(there != self.p.e)
            def _():
                self.copy(there).wait_send()


def lane_iota(shape):
    return lax.broadcasted_iota(jnp.int32, shape, len(shape) - 1)


def swap_halves(values):
    lane = lane_iota(values.shape) % HEAD_DIM
    half = HEAD_DIM // 2
    return jnp.where(
        lane < half,
        pltpu.roll(values, values.shape[-1] - half, 1),
        pltpu.roll(values, half, 1),
    )


def split_heads(tile):
    low = lane_iota(tile.shape) < HEAD_DIM
    turned = pltpu.roll(tile, HEAD_DIM, 1)
    zero = jnp.zeros_like(tile)
    return (
        (jnp.where(low, tile, zero), jnp.where(low, zero, turned)),
        (jnp.where(low, turned, zero), jnp.where(low, zero, tile)),
    )


def inverse_rms(values):
    return lax.rsqrt(jnp.mean(values * values, axis=1, keepdims=True) + NORM_EPS)


def gain_rows(narrow, experts):
    shape = (16, narrow.shape[1])
    row = lax.broadcasted_iota(jnp.int32, shape, 0)
    pick = jnp.where(lane_iota(shape) == row + experts, 1.0, 0.0).astype(BF16)
    return dot_last(pick, narrow)


def column_of(row):
    n = row.shape[1]
    shape = (n, n)
    same = lane_iota(shape) == lax.broadcasted_iota(jnp.int32, shape, 0)
    return jnp.sum(jnp.where(same, row, 0.0), axis=1, keepdims=True)


def row_of(column):
    n = column.shape[0]
    shape = (n, n)
    same = lane_iota(shape) == lax.broadcasted_iota(jnp.int32, shape, 0)
    return jnp.sum(jnp.where(same, column, 0.0), axis=0, keepdims=True)


def documents(places, ends):
    doc = jnp.zeros_like(places)
    start = jnp.zeros_like(places)
    for end in ends:
        past = places >= end
        doc = doc + jnp.where(past, 1.0, 0.0)
        start = jnp.where(past, end, start)
    return doc, start


def turned(values):
    m, n = values.shape
    if n < NAR:
        values = jnp.concatenate([values, jnp.zeros((m, NAR - n), F32)], axis=1)
    if m < NAR:
        values = jnp.concatenate([values, jnp.zeros((NAR - m, NAR), F32)], axis=0)
    return jnp.transpose(values)[:n, :m]


def kept_pairs(routes_by_rank, take_order, experts, capacity):
    top_count, rows = routes_by_rank.shape
    routes = turned(routes_by_rank.astype(F32)).astype(jnp.int32)
    lane = lane_iota((rows, NAR))
    token = lax.broadcasted_iota(jnp.int32, (rows, 1), 0)
    number = lane_iota((rows, take_order.shape[1])).astype(F32)
    hit = jnp.zeros((rows, NAR), jnp.bool_)
    taken = jnp.zeros((rows, NAR), F32)
    for j in range(top_count):
        at = jnp.sum(jnp.where(take_order == token * top_count + j, number, 0.0), axis=1, keepdims=True)
        mine = lane == routes[:, j : j + 1]
        hit = hit | mine
        taken = jnp.where(mine, at, taken)
    taken = jnp.where(hit, taken, 1e9)
    across = jnp.transpose(taken)
    rank = jnp.zeros((rows, NAR), F32)
    for name in range(experts):
        before = jnp.where(across[name : name + 1, :] < taken[:, name : name + 1], 1.0, 0.0)
        rank = jnp.where(lane == name, jnp.sum(before, axis=1, keepdims=True), rank)
    one, zero = jnp.ones((rows, NAR), F32), jnp.zeros((rows, NAR), F32)
    hits = jnp.where(hit, one, zero)
    return hits, jnp.where(rank < capacity, hits, zero)


def layer_kernel(
    tok, wq, wk, wv, wr, na, nf, wo, cot, eg, eu, ed, routes, slots, lengths, places,
    out, tok_grad, dq_out, dk_out, dv_out, dwo_out, gains_out, og_own, ou_own, od_own, egr, eur, edr, mixp,
    w_all, wo_all, x_all, q, klo, khi, vlo, vhi, pr, att, hid, vis, cs, sn, hit, kept, gates, opart, orecv,
    f_all, part, og, hgu, core_in, y_in, a_in, pass_in, gate_out, gate_in, grad_out, grad_in, wg, wu, wd, h1, h2, mix,
    dk, dv, small, state, wsend, wrecv,
    ga_s, ga_r, gb_s, gb_r, gw_s, gw_r, gc_s, gc_r, gf_s, gf_r, sc_s, sc_r, sm_s, sm_r, so_s, so_r, sw_s, sw_r,
    gs_s, gs_r, gg_s, gg_r, xs, xr, loc, mix_sem, ready,
):
    p = Place()
    i, e = p.i, p.e
    rows, width = tok.shape
    depth = wo.shape[0]
    plane = 16 * depth
    group = 4 * rows
    group_rows_count = 2 * rows
    half = width // 2
    ff = wd.shape[0]
    q_width = q.shape[1]
    k_width = dk.shape[1]
    experts = 16
    wide = q_width + 2 * k_width
    capacity = 9 * rows * routes.shape[0] // (8 * experts)
    ratio = q_width // k_width
    scale = HEAD_DIM**-0.5
    heads = q_width // HEAD_DIM
    near = [p.order(k) for k in range(4)]

    def w_row(ip, block):
        return pl.ds(pl.multiple_of(ip * plane + block * depth, 16), depth)

    def row_block(ip):
        return pl.ds(pl.multiple_of(ip * rows, rows), rows)

    def half_lanes(ip, n):
        return pl.ds(pl.multiple_of(ip * n, 128), n)

    def half_rows(ip):
        return pl.ds(pl.multiple_of(ip * half, half), half)

    def group_rows(a1):
        return pl.ds(pl.multiple_of(a1 * group, group), group)

    lane = lane_iota((depth, NAR))
    gain_cols = [column_of(r[...].astype(F32)) for r in (na, nf)]
    narrow_own = jnp.concatenate([turned(wr[...].astype(F32)), jnp.zeros((depth, NAR - experts), F32)], axis=1)
    narrow_own = jnp.where(lane == experts, gain_cols[0], jnp.where(lane == experts + 1, gain_cols[1], narrow_own))
    own = w_row(i, e)
    w_all[own, wide:] = narrow_own.astype(BF16)
    w_all[own, :q_width] = wq[:, half_lanes(i, q_width)]
    w_all[own, q_width : q_width + k_width] = wk[:, half_lanes(i, k_width)]
    w_all[own, q_width + k_width : wide] = wv[:, half_lanes(i, k_width)]
    p.barrier(whole_plane=True)
    cuts = (
        (wq.at[:, half_lanes(1 - i, q_width)], 0, q_width),
        (wk.at[:, half_lanes(1 - i, k_width)], q_width, k_width),
        (wv.at[:, half_lanes(1 - i, k_width)], q_width + k_width, k_width),
        (w_all.at[own, pl.ds(wide, NAR)], wide, NAR),
    )
    give_w = [
        remote(src, w_all.at[own, pl.ds(first, size)], xs.at[n], xr.at[n], p.over_x())
        for n, (src, first, size) in enumerate(cuts)
    ]
    for one in give_w:
        one.start()
    give_x = remote(tok, x_all.at[i], xs.at[4], xr.at[4], p.over_x())
    take_x = remote(x_all.at[1 - i], x_all.at[1 - i], xs.at[4], xr.at[4], p.over_x())
    give_x.start()

    ga = Gather(p, lambda block: w_all.at[w_row(i, block)], ga_s, ga_r)
    gb = Gather(p, lambda block: w_all.at[w_row(1 - i, block)], gb_s, gb_r)
    gw = Gather(p, lambda block: wo_all.at[w_row(0, block)], gw_s, gw_r)
    gc = Gather(p, lambda block: og.at[row_block(block)], gc_s, gc_r)
    gf = Gather(p, lambda block: f_all.at[row_block(block)], gf_s, gf_r)

    ga.begin()
    own_cot = pltpu.make_async_copy(cot, og.at[row_block(e)], loc.at[0])
    own_cot.start()
    loads = [
        pltpu.make_async_copy(src, dst, loc.at[1 + n])
        for n, (src, dst) in enumerate(((eg, wg.at[half_rows(i)]), (eu, wu.at[half_rows(i)]), (ed, wd.at[:, half_rows(i)])))
    ]
    for one in loads:
        one.start()
    wo_all[w_row(0, e), :] = wo[...]
    x_all[i] = tok[...]
    for n, (_, first, size) in enumerate(cuts):
        there = w_all.at[w_row(1 - i, e), pl.ds(first, size)]
        remote(there, there, xs.at[n], xr.at[n], p.over_x()).wait_recv()
    gb.begin()
    ff_half = ff // 2
    weight_moves = (
        (eg, lambda ip: wg.at[half_rows(ip)]),
        (eu, lambda ip: wu.at[half_rows(ip)]),
        (ed.at[pl.ds(0, ff_half)], lambda ip: wd.at[pl.ds(0, ff_half), half_rows(ip)]),
        (ed.at[pl.ds(ff_half, ff_half)], lambda ip: wd.at[pl.ds(ff_half, ff_half), half_rows(ip)]),
    )
    give_e = [
        remote(src, dst(i), xs.at[5 + n], xr.at[5 + n], p.over_x()) for n, (src, dst) in enumerate(weight_moves)
    ]
    take_e = [
        remote(dst(1 - i), dst(1 - i), xs.at[5 + n], xr.at[5 + n], p.over_x())
        for n, (src, dst) in enumerate(weight_moves)
    ]
    for one in give_e[:3]:
        one.start()

    ends = [lengths[0, 0].astype(F32)]
    for n in range(1, lengths.shape[1]):
        ends.append(ends[-1] + lengths[0, n].astype(F32))
    place_row = places[...].astype(F32)
    place_col = column_of(place_row)
    doc_row, _ = documents(place_row, ends[:-1])
    doc_col, start_col = documents(place_col, ends[:-1])
    vis[...] = jnp.where((doc_row == doc_col) & (place_col >= place_row), 1.0, 0.0)
    lane = lane_iota((1, 128))
    quarter = HEAD_DIM // 2
    freq = jnp.exp((lane % quarter).astype(F32) * (-2.0 / HEAD_DIM * math.log(ROPE_BASE)))
    angle = (place_col - start_col) * freq
    cs[...] = jnp.cos(angle)
    sine = jnp.sin(angle)
    sn[...] = jnp.where(lane % HEAD_DIM < quarter, -sine, sine)

    both = (ga, gb)
    for g in both:
        g.phase(1)
    hits, keeps = kept_pairs(routes[...], slots[...], experts, capacity)
    hit[...] = hits
    kept[...] = keeps
    for k in range(3):
        for g in both:
            g.cross(k)
        if k < 2:
            for g in both:
                g.phase(k + 2)
        if k == 1:
            gw.begin()
    gw.phase(1)
    own_cot.wait()
    gc.begin()
    for g in both:
        g.cross(3)
    for k in range(4):
        for g in both:
            g.join(k)

    events = [
        functools.partial(gw.phase, 2),
        functools.partial(gw.cross, 0),
        functools.partial(gw.phase, 3),
        functools.partial(gw.cross, 1),
        functools.partial(gw.cross, 2),
        functools.partial(gw.cross, 3),
    ]

    def serve():
        if events:
            events.pop(0)()

    take_x.wait_recv()
    narrow = w_all[:, wide:]
    gains = gain_rows(narrow, experts)
    att_in = mix.at[pl.ds(2 * rows, 2 * rows)]

    def fill_att_in():
        for ip in range(2):
            x = x_all[ip].astype(F32)
            att_in[ip * rows : (ip + 1) * rows, :] = (x * inverse_rms(x) * gains[0:1]).astype(BF16)

    fill_att_in()
    serve()
    cos, sin = cs[...], sn[...]

    def rope(values):
        return values * cos + swap_halves(values) * sin

    def unrope(values):
        return values * cos - swap_halves(values) * sin

    for tile in range(wide // 256):
        lin = dot_plain(att_in[...], w_all[:, tile * 256 : (tile + 1) * 256])
        for h in range(2):
            col = tile * 256 + h * 128
            piece = lin[:, h * 128 : (h + 1) * 128]
            if col < q_width:
                q[:, col : col + 128] = rope(piece).astype(BF16)
                continue
            is_key = col < q_width + k_width
            n = (col - q_width - (0 if is_key else k_width)) // 128
            lows, highs = (klo, khi) if is_key else (vlo, vhi)
            for g, (low, high) in enumerate(split_heads(rope(piece) if is_key else piece)):
                lows[2 * n + g] = low.astype(BF16)
                highs[2 * n + g] = high.astype(BF16)
    serve()
    sides = ((klo, vlo), (khi, vhi))
    for pair in range(heads // 2):
        lanes = slice(pair * 128, (pair + 1) * 128)
        total = None
        for side, (keys, vals) in enumerate(sides):
            head = 2 * pair + side
            g = head // ratio
            scores = dot_last(q[:, lanes], keys[g]) * scale
            scores = jnp.where(vis[...] > 0, scores, MASK_FILL)
            grown = jnp.exp(scores - jnp.max(scores, axis=1, keepdims=True))
            probs = (grown / jnp.sum(grown, axis=1, keepdims=True)).astype(BF16)
            pr[head] = probs
            term = dot_plain(probs, vals[g])
            total = term if total is None else total + term
        att[:, lanes] = total.astype(BF16)
        serve()
    while events:
        serve()
    for k in range(4):
        gw.join(k)
    gc.phase(1)
    opart[...] = dot_plain(att[row_block(1 - i), :], wo_all[...]).astype(BF16)
    give_o = remote(opart, orecv, xs.at[9], xr.at[9], p.over_x())
    give_o.start()
    give_e[3].start()
    hid[...] = tok[...].astype(F32) + dot_plain(att[row_block(i), :], wo_all[...])
    gc.cross(0)
    gc.phase(2)
    for one in loads:
        one.wait()
    give_o.wait()
    hidden = hid[...] + orecv[...].astype(F32)
    hid[...] = hidden
    ffn_in = (hidden * inverse_rms(hidden) * gains[1:2]).astype(BF16)
    f_all[row_block(e), :] = ffn_in
    gf.begin()
    logits = dot_plain(ffn_in, narrow)
    chosen = hit[...] > 0
    logits = jnp.where(chosen, logits, MASK_FILL)
    grown = jnp.where(chosen, jnp.exp(logits - jnp.max(logits, axis=1, keepdims=True)), 0.0)
    gate = grown / jnp.sum(grown, axis=1, keepdims=True)
    gates[...] = gate
    gate_rows = jnp.transpose(gate * kept[...])
    for name in range(experts):
        gate_out[name] = jnp.broadcast_to(gate_rows[name : name + 1, :], (8, rows))
    gates_in = Exchange(p, gate_out, gate_in, gs_s, gs_r)
    grads_in = Exchange(p, grad_out, grad_in, gg_s, gg_r)

    @pl.loop(0, experts)
    def _(there):
        gates_in.give(there)

    gc.phase(3)
    gc.cross(1)
    gc.cross(2)
    sc = Scatter(
        p,
        lambda a1, b1: part.at[row_block(a1 * 4 + b1)],
        lambda a1, y1: core_in.at[a1 * 2 + y1],
        lambda a1: y_in.at[a1],
        lambda slot: a_in.at[slot - 1],
        lambda j: pass_in.at[j],
        sc_s, sc_r,
    )

    def store_mix(a1):
        return pltpu.make_async_copy(mix, mixp.at[a1], mix_sem)

    def gate_of(k):
        return jnp.concatenate([column_of(gate_in[near[k] * 4 + b1, 0:1, :]) for b1 in range(4)], axis=0)

    def inward(k):
        here = group_rows(near[k])
        h1[...] = dot_plain(f_all[here, :], wg[...])
        h2[...] = dot_plain(f_all[here, :], wu[...])
        pre = h1[...]
        hgu[here, 0:ff] = (pre * jax.nn.sigmoid(pre) * h2[...]).astype(BF16)

    def outward(k):
        a1 = near[k]
        here = group_rows(a1)
        if k > 0:
            store_mix(near[k - 1]).wait()
        gate = gate_of(k)

        def project(n, gate_grad):
            cols = pl.ds(pl.multiple_of(n * 512, 512), 512)
            res = dot_plain(hgu[here, 0:ff], wd[:, cols]).astype(BF16).astype(F32)
            mix[:, cols] = (gate * res).astype(BF16)
            c = og[here, cols].astype(F32)
            og[here, cols] = (gate * c).astype(BF16)
            return gate_grad + jnp.sum(res * c, axis=1, keepdims=True)

        gc.sent(k)
        gate_grad = lax.fori_loop(0, width // 512, project, jnp.zeros((group, 1), F32))
        store_mix(a1).start()
        for b1 in range(4):
            row = row_of(gate_grad[b1 * rows : (b1 + 1) * rows])
            grad_out[a1 * 4 + b1] = jnp.broadcast_to(row, (8, rows))
            grads_in.give(a1 * 4 + b1)

    def backward(k):
        here = group_rows(near[k])
        hg = dot_last(og[here, :], wd[...])
        s = jax.nn.sigmoid(h1[...])
        hgu[here, ff : 2 * ff] = (hg * h2[...] * s * (1.0 + h1[...] * (1.0 - s))).astype(BF16)
        hgu[here, 2 * ff :] = (hg * (h1[...] * s)).astype(BF16)

    def send_rows(k):
        here = group_rows(near[k])

        @pl.loop(0, width // 512)
        def _(n):
            cols = pl.ds(pl.multiple_of(n * 512, 512), 512)
            part[here, cols] = (
                dot_last(hgu[here, ff : 2 * ff], wg[cols, :]) + dot_last(hgu[here, 2 * ff :], wu[cols, :])
            ).astype(BF16)

        sc.start(near[k])

    for one in take_e:
        one.wait_recv()

    @pl.loop(0, experts)
    def _(there):
        gates_in.take(there)

    gf.cross(0)
    gf.phase(1)
    gc.join(0)
    gf.join(0)
    inward(0)
    outward(0)
    gc.cross(3)
    gf.phase(2)
    backward(0)
    send_rows(0)
    gf.cross(1)
    gf.phase(3)
    gc.join(1)
    gf.join(1)
    inward(1)
    outward(1)
    backward(1)
    gf.cross(2)
    send_rows(1)
    gc.join(2)
    gf.join(2)
    inward(2)
    sc.core(near[1])
    outward(2)
    backward(2)
    gf.cross(3)
    send_rows(2)
    gc.join(3)
    gf.join(3)
    inward(3)
    sc.core(near[2])
    outward(3)
    sc.cross(near[1])
    backward(3)
    send_rows(3)

    tile = 256
    tiles = half // tile

    def rows_of(ip, n):
        return pl.ds(pl.multiple_of(ip * half + n * tile, tile), tile)

    def in_grad(ip, n, first):
        return dot_first(f_all[:, rows_of(ip, n)], hgu[:, first : first + ff])

    def down_grad(ip, n):
        return dot_first(hgu[:, 0:ff], og[:, rows_of(ip, n)])

    give_g = remote(wg.at[half_rows(1 - i)], egr, xs.at[10], xr.at[10], p.over_x())
    give_u = remote(wu.at[half_rows(1 - i)], eur, xs.at[11], xr.at[11], p.over_x())
    give_d = remote(wd.at[:, half_rows(1 - i)], edr, xs.at[12], xr.at[12], p.over_x())

    @pl.loop(0, tiles)
    def _(n):
        wg[rows_of(1 - i, n), :] = in_grad(1 - i, n, ff).astype(BF16)

    give_g.start()
    sc.core(near[3])
    sc.core(near[0])

    @pl.loop(0, tiles)
    def _(n):
        wu[rows_of(1 - i, n), :] = in_grad(1 - i, n, 2 * ff).astype(BF16)

    sc.cross(near[2])

    @pl.loop(0, tiles)
    def _(n):
        wd[:, rows_of(1 - i, n)] = down_grad(1 - i, n).astype(BF16)

    def save(n, src, dst):
        return pltpu.make_async_copy(src, dst, loc.at[n % 4])

    spots = [h1.at[pl.ds(0, tile)], h1.at[pl.ds(tile, tile)], h2.at[pl.ds(0, tile)], h2.at[pl.ds(tile, tile)]]
    saves = []
    for n in range(2 * tiles):
        if n >= 4:
            saves[n - 4].wait()
        spots[n % 4][...] = in_grad(i, n % tiles, ff * (1 + n // tiles))
        target = (og_own, ou_own)[n // tiles].at[pl.ds((n % tiles) * tile, tile)]
        saves.append(save(n, spots[n % 4], target))
        saves[n].start()
        if n == 2:
            sc.cross(near[3])
            sc.relay(near[2])
    for n in range(2 * tiles - 4, 2 * tiles):
        saves[n].wait()
    spots = [h1.at[:, pl.ds(0, tile)], h1.at[:, pl.ds(tile, tile)], h2.at[:, pl.ds(0, tile)]]
    saves = []
    for n in range(tiles):
        spots[n][...] = down_grad(i, n)
        saves.append(save(n, spots[n], od_own.at[:, pl.ds(n * tile, tile)]))
        saves[n].start()
    sc.relay(near[3])
    store_mix(near[3]).wait()
    gf.drain()

    spare = 16 * rows - 2 * group_rows_count
    dq = hgu.at[pl.ds(spare, group_rows_count), pl.ds(0, wide)]
    bg = hgu.at[pl.ds(spare + group_rows_count, group_rows_count)]
    ag = mix.at[pl.ds(0, group_rows_count), pl.ds(0, q_width)]
    friends = [p.over_x(), p.over_core(), p.over_y()] + [(i, ((p.a + shift) % 4) * 4 + p.bc) for shift in range(1, 4)]
    for friend in friends:
        pl.semaphore_signal(ready.at[0], inc=1, device_id=friend, device_id_type=MESH)
    load_mix = [pltpu.make_async_copy(mixp.at[a1], f_all.at[group_rows(a1)], loc.at[4 + k]) for k, a1 in enumerate(near)]
    for one in load_mix:
        one.start()
    sm = Scatter(
        p,
        lambda a1, b1: f_all.at[row_block(a1 * 4 + b1)],
        lambda a1, y1: og.at[row_block(a1 * 2 + y1)],
        lambda a1: og.at[row_block(8 + a1)],
        lambda slot: og.at[row_block(11 + slot)],
        lambda j: og.at[row_block(14 + j)],
        sm_s, sm_r,
    )

    def piece_of(n):
        return hgu.at[pl.ds(pl.multiple_of(n * depth, 16), depth)]

    so = Scatter(
        p,
        lambda a1, b1: piece_of(a1 * 4 + b1),
        lambda a1, y1: piece_of(16 + a1 * 2 + y1),
        lambda a1: piece_of(24 + a1),
        lambda slot: piece_of(27 + slot),
        lambda j: piece_of(30 + j),
        so_s, so_r,
    )
    both_rows = 2 * depth
    flat = (pl.ds(0, both_rows), pl.ds(0, wide + NAR))
    sw = Scatter(
        p,
        lambda a1, b1: part.at[pl.ds(pl.multiple_of((a1 * 4 + b1) * both_rows, 32), both_rows), pl.ds(0, wide + NAR)],
        lambda a1, y1: core_in.at[(a1 * 2 + y1,) + flat],
        lambda a1: y_in.at[(a1,) + flat],
        lambda slot: a_in.at[(slot - 1,) + flat],
        lambda j: pass_in.at[(j,) + flat],
        sw_s, sw_r,
    )
    for one in load_mix:
        one.wait()
    pl.semaphore_wait(ready.at[0], len(friends))
    for k in (3, 2, 1, 0):
        sm.start(near[k])
    for k in (3, 2, 1):
        sm.core(near[k])
    sc.cross(near[0])

    @pl.loop(0, experts)
    def _(there):
        grads_in.take(there)

    by_expert = jnp.concatenate([grad_in[name, 0:1, :] for name in range(experts)], axis=0)
    lane = lane_iota((rows, NAR))
    gate_grad = jnp.concatenate([turned(by_expert), jnp.zeros((rows, NAR - experts), F32)], axis=1) * kept[...]
    gate = gates[...]
    logit_grad = (gate * (gate_grad - jnp.sum(gate * gate_grad, axis=1, keepdims=True))).astype(BF16)
    narrow = w_all[:, wide:]
    gains = gain_rows(narrow, experts)
    routed = dot_last(logit_grad, narrow)
    hidden = hid[...]
    r2 = inverse_rms(hidden)
    n2 = hidden * r2
    again = pltpu.make_async_copy(cot, opart, loc.at[8])
    again.start()
    again.wait()
    sc.finish()
    ffn_grad = sc.total() + routed
    d2 = ffn_grad * gains[1:2]
    state[...] = opart[...].astype(F32) + r2 * (d2 - n2 * jnp.mean(d2 * n2, axis=1, keepdims=True))
    bg[row_block(i), :] = state[...].astype(BF16)
    give_b = remote(bg.at[row_block(i)], bg.at[row_block(i)], xs.at[13], xr.at[13], p.over_x())
    take_b = remote(bg.at[row_block(1 - i)], bg.at[row_block(1 - i)], xs.at[13], xr.at[13], p.over_x())
    give_b.start()
    give_u.start()
    sc.drain()
    for friend in friends[1:]:
        pl.semaphore_signal(ready.at[1], inc=1, device_id=friend, device_id_type=MESH)
    ones = jnp.where(lane == experts + 1, 1.0, 0.0).astype(BF16)
    gain_term = ffn_grad * n2
    gain_high = gain_term.astype(BF16)
    gain_low = (gain_term - gain_high.astype(F32)).astype(BF16)
    ffn_in = (n2 * gains[1:2]).astype(BF16)
    small[...] = dot_first(ffn_in, logit_grad) + dot_first(gain_high, ones) + dot_first(gain_low, ones)
    fill_att_in()
    dk[...] = jnp.zeros_like(dk)
    dv[...] = jnp.zeros_like(dv)
    low_lane = lane_iota((2 * rows, 128)) < HEAD_DIM
    sm.cross(near[3])
    take_b.wait_recv()
    for n in range(q_width // 256):
        lanes = slice(n * 256, (n + 1) * 256)
        ag[:, lanes] = dot_last(bg[...], wo_all[lanes, :]).astype(BF16)
    for n in range(q_width // 256):
        lanes = slice(n * 256, (n + 1) * 256)
        hgu[lanes, :] = dot_first(att[:, lanes], bg[...]).astype(BF16)
    for k in (3, 2, 1, 0):
        so.start(near[k])
    for pair in range(heads // 2):
        lanes = slice(pair * 128, (pair + 1) * 128)
        grad_in_pair = ag[:, lanes]
        q_pair = q[:, lanes]
        q_grad = None
        for side, (keys, vals) in enumerate(sides):
            head = 2 * pair + side
            g = head // ratio
            probs = pr[head]
            prob_grad = dot_last(grad_in_pair, vals[g])
            wide_probs = probs.astype(F32)
            shift = jnp.sum(wide_probs * prob_grad, axis=1, keepdims=True)
            score_grad = (wide_probs * (prob_grad - shift)).astype(BF16)
            term = dot_plain(score_grad, keys[g])
            q_grad = term if q_grad is None else q_grad + term
            mine = low_lane if side == 0 else jnp.logical_not(low_lane)
            k_term = jnp.where(mine, dot_first(score_grad, q_pair), 0.0)
            v_term = jnp.where(mine, dot_first(probs, grad_in_pair), 0.0)
            if g % 2 != side:
                k_term = pltpu.roll(k_term, HEAD_DIM, 1)
                v_term = pltpu.roll(v_term, HEAD_DIM, 1)
            lot = slice((g // 2) * 128, (g // 2 + 1) * 128)
            dk[:, lot] += k_term
            dv[:, lot] += v_term
        dq[:, lanes] = unrope(scale * q_grad).astype(BF16)
        if pair == 1:
            sm.cross(near[2])
            sm.relay(near[3])
        if pair == 0:
            for k in (3, 2, 1, 0):
                so.core(near[k])
        if pair == 3:
            sm.cross(near[1])
            sm.relay(near[2])
    for n in range(k_width // 128):
        lanes = slice(n * 128, (n + 1) * 128)
        dq[:, q_width + n * 128 : q_width + (n + 1) * 128] = unrope(scale * dk[:, lanes]).astype(BF16)
        dq[:, q_width + k_width + n * 128 : q_width + k_width + (n + 1) * 128] = dv[:, lanes].astype(BF16)

    pick = jnp.where(lane == experts, 1.0, 0.0).astype(BF16)
    for first in range(2):
        ip = 1 - i if first == 0 else i
        back = dot_last(dq[row_block(ip), :], w_all[:, :wide])
        x = x_all[ip].astype(F32)
        term = back * (x * inverse_rms(x))
        high = term.astype(BF16)
        low = (term - high.astype(F32)).astype(BF16)
        small[...] += dot_first(high, pick) + dot_first(low, pick)
        if first == 0:
            opart[...] = back.astype(BF16)
            give_a = remote(opart, orecv, xs.at[14], xr.at[14], p.over_x())
            give_a.start()
            give_d.start()
    step = plane // 2
    count = step // depth
    for turn in range(2):
        n = near[3 - 3 * turn] // 2
        for ip in range(2):
            span = pl.ds(pl.multiple_of(ip * plane + n * step, 128), step)
            block = dot_first(att_in[:, span], dq[...]).astype(BF16)
            extra = small[span, :].astype(BF16)
            for m in range(count):
                at = pl.ds(pl.multiple_of((n * count + m) * both_rows + ip * depth, 16), depth)
                part[at, :wide] = block[m * depth : (m + 1) * depth]
                part[at, wide : wide + NAR] = extra[m * depth : (m + 1) * depth]
        if turn == 0:
            pl.semaphore_wait(ready.at[1], len(friends) - 1)
        sw.start(near[3 - 2 * turn])
        sw.start(near[2 - 2 * turn])
    for k in (3, 2, 1, 0):
        sw.core(near[k])
    sm.core(near[0])
    so.cross(near[3])
    so.cross(near[2])
    give_a.wait_recv()
    attn_grad = back + orecv[...].astype(F32)
    x = x_all[i].astype(F32)
    r1 = inverse_rms(x)
    n1 = x * r1
    d1 = attn_grad * gains[0:1]
    tok_grad[...] = (state[...] + r1 * (d1 - n1 * jnp.mean(d1 * n1, axis=1, keepdims=True))).astype(BF16)
    so.cross(near[1])
    so.relay(near[3])
    so.cross(near[0])
    so.relay(near[2])
    sw.cross(near[3])
    sw.cross(near[2])
    sw.relay(near[3])
    sw.cross(near[1])
    sw.relay(near[2])
    sw.cross(near[0])
    sw.finish()
    summed = sw.total()
    wsend[0] = summed[:depth]
    wsend[1] = summed[depth:]
    give_s = remote(wsend.at[1 - i], wrecv, xs.at[15], xr.at[15], p.over_x())
    give_s.start()

    def place_half(ip, values):
        dq_out[:, half_lanes(ip, q_width)] = values[:, :q_width]
        dk_out[:, half_lanes(ip, k_width)] = values[:, q_width : q_width + k_width]
        dv_out[:, half_lanes(ip, k_width)] = values[:, q_width + k_width : wide]

    mine = wsend[i]
    place_half(i, mine)
    so.finish()
    dwo_out[...] = so.total()
    sm.cross(near[0])
    sm.finish()
    out[...] = (hid[...] + sm.total()).astype(BF16)
    give_s.wait_recv()
    theirs = wrecv[...]
    place_half(1 - i, theirs)
    gains_out[...] = mine[:, wide:] + theirs[:, wide:]
    for one in give_w + [give_x] + give_e + [give_b, give_a, give_s]:
        one.wait_send()
    for one in (give_g, give_u, give_d):
        one.wait()
    for one in saves:
        one.wait()
    for g in (ga, gb, gw):
        g.drain()
    for s in (sm, so, sw):
        s.drain()
    gates_in.drain()
    grads_in.drain()


def finish_kernel(
    og_own, ou_own, od_own, egr, eur, edr, out, tok, dq, dk, dv, dwo, gains,
    out_o, tok_o, dq_o, dk_o, dv_o, dwo_o, ga_o, gf_o, gr_o, eg_o, eu_o, ed_o,
):
    eg_o[0] = og_own[...] + egr[...].astype(F32)
    eu_o[0] = ou_own[...] + eur[...].astype(F32)
    ed_o[0] = od_own[...] + edr[...].astype(F32)

    @pl.when(pl.program_id(0) == 0)
    def _():
        for src, dst in ((out, out_o), (tok, tok_o), (dq, dq_o), (dk, dk_o), (dv, dv_o), (dwo, dwo_o)):
            dst[...] = src[...]
        experts = gr_o.shape[0]
        rows = turned(gains[...])
        ga_o[...] = rows[experts : experts + 1]
        gf_o[...] = rows[experts + 1 : experts + 2]
        gr_o[...] = rows[:experts]


def paired_body(
    tokens, cotangent, norm_attn, w_query, key_projection, value_projection, w_out, norm_ffn, w_router,
    expert_gate, expert_up, expert_down, routes, slot_order, doc_lengths, deal,
):
    rows, width = tokens.shape
    depth = w_query.shape[0]
    experts = 16
    q_width = w_query.shape[1] // 2
    k_width = key_projection.shape[1] // 2
    wide = q_width + 2 * k_width
    ff = expert_gate.shape[2]
    half = width // 2
    vm = pl.BlockSpec(memory_space=pltpu.VMEM)
    hb = pl.BlockSpec(memory_space=pl.ANY)
    sm = pl.BlockSpec(memory_space=pltpu.SMEM)

    def shaped(*dims, dtype=BF16):
        return jax.ShapeDtypeStruct(dims, dtype)

    def sems(n):
        return pltpu.SemaphoreType.DMA((n,))

    heads = q_width // HEAD_DIM
    groups = k_width // HEAD_DIM
    group_rows = 2 * rows

    def room(*dims, dtype=BF16):
        return pltpu.VMEM(dims, dtype)

    def gather_sems(n):
        return [sems(Gather.SENDS), sems(Gather.RECVS)] * n

    def scatter_sems(n):
        return [sems(Scatter.SENDS), sems(Scatter.RECVS)] * n

    res = pl.pallas_call(
        layer_kernel,
        name="layer",
        out_shape=(
            shaped(rows, width),
            shaped(rows, width),
            shaped(depth, 2 * q_width, dtype=F32),
            shaped(depth, 2 * k_width, dtype=F32),
            shaped(depth, 2 * k_width, dtype=F32),
            shaped(depth, width, dtype=F32),
            shaped(depth, NAR, dtype=F32),
            shaped(half, ff, dtype=F32),
            shaped(half, ff, dtype=F32),
            shaped(ff, half, dtype=F32),
            shaped(half, ff),
            shaped(half, ff),
            shaped(ff, half),
            shaped(4, 4 * rows, width),
        ),
        in_specs=[vm] * 8 + [hb] * 4 + [vm, vm, sm, vm],
        out_specs=(vm,) * 7 + (hb,) * 7,
        scratch_shapes=[
            room(2 * 16 * depth, wide + NAR),
            room(16 * depth, width),
            room(2, rows, width),
            room(group_rows, q_width),
        ]
        + [room(groups, group_rows, 128)] * 4
        + [
            room(heads, group_rows, group_rows),
            room(group_rows, q_width),
            room(rows, width, dtype=F32),
            room(group_rows, group_rows, dtype=F32),
            room(group_rows, 128, dtype=F32),
            room(group_rows, 128, dtype=F32),
            room(rows, NAR, dtype=F32),
            room(rows, NAR, dtype=F32),
            room(rows, NAR, dtype=F32),
            room(rows, width),
            room(rows, width),
        ]
        + [room(16 * rows, width)] * 4
        + [room(8, rows, width), room(4, rows, width), room(2, rows, width), room(2, rows, width)]
        + [room(16, 8, rows, dtype=F32)] * 4
        + [
            room(width, ff),
            room(width, ff),
            room(ff, width),
            room(4 * rows, ff, dtype=F32),
            room(4 * rows, ff, dtype=F32),
            room(4 * rows, width),
            room(group_rows, k_width, dtype=F32),
            room(group_rows, k_width, dtype=F32),
            room(2 * 16 * depth, NAR, dtype=F32),
            room(rows, width, dtype=F32),
            room(2, depth, wide + NAR, dtype=F32),
            room(depth, wide + NAR, dtype=F32),
        ]
        + gather_sems(5)
        + scatter_sems(4)
        + [sems(16)] * 4
        + [sems(16), sems(16), sems(9), pltpu.SemaphoreType.DMA(()), pltpu.SemaphoreType.REGULAR((2,))],
        compiler_params=pltpu.CompilerParams(collective_id=1, has_side_effects=True, vmem_limit_bytes=64 << 20),
    )(
        tokens, w_query, key_projection, value_projection, w_router.T, norm_attn[None], norm_ffn[None], w_out,
        cotangent, expert_gate[0], expert_up[0], expert_down[0], routes.T, slot_order, doc_lengths,
        deal.reshape(1, -1),
    )
    out, tok_grad, dq, dk, dv, dwo, gains, og_own, ou_own, od_own, egr, eur, edr, _ = res

    steps = 4

    def cut(*dims):
        return pl.BlockSpec((dims[0] // steps,) + dims[1:], lambda n: (n,) + (0,) * (len(dims) - 1))

    def cut_out(*dims):
        return pl.BlockSpec((1, dims[0] // steps) + dims[1:], lambda n: (0, n) + (0,) * (len(dims) - 1))

    def entire(*dims):
        return pl.BlockSpec(dims, lambda n: (0,) * len(dims))

    mats = ((half, ff), (half, ff), (ff, half))
    rest = (out, tok_grad, dq, dk, dv, dwo, gains)
    res = pl.pallas_call(
        finish_kernel,
        name="finish",
        grid=(steps,),
        out_shape=tuple(jax.ShapeDtypeStruct(r.shape, r.dtype) for r in rest[:6])
        + (shaped(1, depth, dtype=F32), shaped(1, depth, dtype=F32), shaped(experts, depth, dtype=F32))
        + tuple(shaped(1, *m, dtype=F32) for m in mats),
        in_specs=[cut(*m) for m in mats] * 2 + [entire(*r.shape) for r in rest],
        out_specs=tuple(entire(*r.shape) for r in rest[:6])
        + (entire(1, depth), entire(1, depth), entire(experts, depth))
        + tuple(cut_out(*m) for m in mats),
        compiler_params=pltpu.CompilerParams(vmem_limit_bytes=62 << 20),
    )(og_own, ou_own, od_own, egr, eur, edr, *rest)
    out, tok_grad, dq, dk, dv, dwo, g_attn, g_ffn, g_router, eg, eu, ed = res
    return (
        out, tok_grad, g_attn.reshape(-1), dq, dk, dv, dwo, g_ffn.reshape(-1), g_router.T, eg, eu, ed,
    )


def general_body(
    tokens,
    cotangent,
    norm_attn,
    w_query,
    key_projection,
    value_projection,
    w_out,
    norm_ffn,
    w_router,
    expert_gate,
    expert_up,
    expert_down,
    routes,
    slot_order,
    doc_lengths,
    deal,
):
    gain_attn, full_query, gathered_key, gathered_value, full_out, gain_ffn, full_router = (
        lax.all_gather(norm_attn, ("dp", "expert"), axis=0, tiled=True),
        lax.all_gather(w_query, ("dp", "expert"), axis=0, tiled=True),
        lax.all_gather(key_projection, ("dp", "expert"), axis=0, tiled=True),
        lax.all_gather(value_projection, ("dp", "expert"), axis=0, tiled=True),
        lax.all_gather(w_out, ("dp", "expert"), axis=0, tiled=True),
        lax.all_gather(norm_ffn, ("dp", "expert"), axis=0, tiled=True),
        lax.all_gather(w_router, ("dp", "expert"), axis=0, tiled=True),
    )
    full_gate, full_up, full_down = (
        lax.all_gather(expert_gate[0], "dp", axis=0, tiled=True),
        lax.all_gather(expert_up[0], "dp", axis=0, tiled=True),
        lax.all_gather(expert_down[0], "dp", axis=1, tiled=True),
    )
    count_of_rows, model_width = tokens.shape
    top_count = routes.shape[1]
    experts = full_router.shape[1]
    owners = lax.axis_size("expert")
    capacity = 9 * count_of_rows * top_count // (8 * experts)
    head_count = full_query.shape[1] // HEAD_DIM
    groups = gathered_key.shape[1] // HEAD_DIM
    head_ratio = head_count // groups
    scale_attn = gain_attn.astype(jnp.float32)
    scale_ffn = gain_ffn.astype(jnp.float32)
    score_scale = HEAD_DIM ** (-0.5)
    group_places = deal[:, 0, :].reshape(-1)
    group_docs, group_offsets = doc_layout(doc_lengths[0], group_places)
    shard_start = lax.axis_index("dp") * count_of_rows
    places = lax.dynamic_slice_in_dim(group_places, shard_start, count_of_rows)
    doc_ids = lax.dynamic_slice_in_dim(group_docs, shard_start, count_of_rows)
    offsets = lax.dynamic_slice_in_dim(group_offsets, shard_start, count_of_rows)
    cosine_lookup, sine_lookup = rope_tables(offsets, HEAD_DIM)
    inputs = tokens.astype(jnp.float32)
    inverse_one = lax.rsqrt(jnp.mean(inputs * inputs, axis=1, keepdims=True) + NORM_EPS)
    normed_one = inputs * inverse_one
    attention_input = (normed_one * scale_attn).astype(jnp.bfloat16)
    query_rows = apply_rotation(
        dot_plain(attention_input, full_query).reshape(count_of_rows, head_count, HEAD_DIM),
        cosine_lookup,
        sine_lookup,
    ).astype(jnp.bfloat16)
    key_matrix_rows = apply_rotation(
        dot_plain(attention_input, gathered_key).reshape(count_of_rows, groups, HEAD_DIM),
        cosine_lookup,
        sine_lookup,
    ).astype(jnp.bfloat16)
    value_matrix_rows = dot_plain(attention_input, gathered_value).astype(jnp.bfloat16)
    all_keys, all_values = (
        lax.all_gather(key_matrix_rows.reshape(count_of_rows, -1), "dp", axis=0, tiled=True),
        lax.all_gather(value_matrix_rows, "dp", axis=0, tiled=True),
    )
    group_rows = all_keys.shape[0]
    key_span = math.gcd(group_rows, 512)
    span_count = group_rows // key_span
    key_spans = (
        all_keys.reshape(span_count, key_span, groups, HEAD_DIM),
        all_values.reshape(span_count, key_span, groups, HEAD_DIM),
        group_places.reshape(span_count, key_span),
        group_docs.reshape(span_count, key_span),
    )
    grouped_q = query_rows.reshape(count_of_rows, groups, head_ratio, HEAD_DIM)

    def span_scores(key_block, key_place, key_doc):
        visible = (doc_ids[:, None] == key_doc[None, :]) & (places[:, None] >= key_place[None, :])
        scores = (
            jnp.einsum("qgrd,kgd->grqk", grouped_q, key_block, preferred_element_type=jnp.float32)
            * score_scale
        )
        return jnp.where(visible[None, None], scores, MASK_FILL)

    def extent(carry, operands):
        run_max, run_sum = carry
        key_block, value_block, key_place, key_doc = operands
        scores = span_scores(key_block, key_place, key_doc)
        new_max = jnp.maximum(run_max, jnp.max(scores, axis=-1, keepdims=True))
        run_sum = run_sum * jnp.exp(run_max - new_max) + jnp.sum(
            jnp.exp(scores - new_max), axis=-1, keepdims=True
        )
        return ((new_max, run_sum), None)

    stat_shape = (groups, head_ratio, count_of_rows, 1)
    (row_max, row_sum), _ = lax.scan(
        extent,
        (jnp.full(stat_shape, MASK_FILL, jnp.float32), jnp.zeros(stat_shape, jnp.float32)),
        key_spans,
    )
    log_total = row_max + jnp.log(row_sum)

    def weigh_values(running, operands):
        key_block, value_block, key_place, key_doc = operands
        weights = jnp.exp(span_scores(key_block, key_place, key_doc) - log_total).astype(
            jnp.bfloat16
        )
        return (
            running
            + jnp.einsum(
                "grqk,kgd->qgrd", weights, value_block, preferred_element_type=jnp.float32
            ),
            None,
        )

    attended, _ = lax.scan(
        weigh_values,
        jnp.zeros((count_of_rows, groups, head_ratio, HEAD_DIM), jnp.float32),
        key_spans,
    )
    attended = attended.reshape(count_of_rows, head_count * HEAD_DIM).astype(jnp.bfloat16)
    hidden_state = inputs + dot_plain(attended, full_out)
    inverse_two = lax.rsqrt(jnp.mean(hidden_state * hidden_state, axis=1, keepdims=True) + NORM_EPS)
    normed_two = hidden_state * inverse_two
    ffn_in = (normed_two * scale_ffn).astype(jnp.bfloat16)
    logits = dot_plain(ffn_in, full_router)
    route_hits = (routes[:, :, None] == jnp.arange(experts, dtype=jnp.int32)[None, None, :]).astype(
        jnp.float32
    )
    chosen = jnp.sum(route_hits * logits[:, None, :], axis=-1)
    gate_values = jax.nn.softmax(chosen, axis=-1)
    pair_slot, slot_token = assign_slots(routes, slot_order[0], experts, capacity)
    padded_in = jnp.concatenate([ffn_in, jnp.zeros((1, model_width), jnp.bfloat16)], axis=0)
    outgoing = padded_in[slot_token].reshape(owners, capacity, model_width)
    arrived = lax.all_to_all(outgoing, "expert", split_axis=0, concat_axis=0, tiled=True)
    flat_rows = arrived.reshape(-1, model_width)
    gate_pre = dot_plain(flat_rows, full_gate)
    up_pre = dot_plain(flat_rows, full_up)
    hidden = (jax.nn.silu(gate_pre) * up_pre).astype(jnp.bfloat16)
    result = dot_plain(hidden, full_down).astype(jnp.bfloat16).reshape(arrived.shape)
    sent_back = lax.all_to_all(result, "expert", split_axis=0, concat_axis=0, tiled=True)
    exchanged = (
        sent_back,
        arrived,
        gate_pre.reshape(arrived.shape[0], arrived.shape[1], -1),
        up_pre.reshape(arrived.shape[0], arrived.shape[1], -1),
    )
    returned = exchanged[0]
    expert_rows = exchanged[1].reshape(-1, model_width)
    gate_pre = exchanged[2].reshape(expert_rows.shape[0], -1)
    up_pre = exchanged[3].reshape(expert_rows.shape[0], -1)
    out_grad = cotangent.astype(jnp.float32)
    padded_back = jnp.concatenate(
        [returned.reshape(-1, model_width), jnp.zeros((1, model_width), jnp.bfloat16)], axis=0
    )
    slot_grid = pair_slot.reshape(count_of_rows, top_count)
    mixture = jnp.zeros((count_of_rows, model_width), jnp.float32)
    gate_parts = []
    for column in range(top_count):
        picked = padded_back[slot_grid[:, column]].astype(jnp.float32)
        mixture = mixture + gate_values[:, column : column + 1] * picked
        gate_parts.append(jnp.sum(out_grad * picked, axis=1))
    output = (hidden_state + mixture).astype(jnp.bfloat16)
    gate_grad = jnp.stack(gate_parts, axis=1)
    slot_gate = (
        jnp.zeros((experts * capacity + 1,), jnp.float32)
        .at[pair_slot]
        .set(gate_values.reshape(-1))[: experts * capacity]
    )
    padded_grad = jnp.concatenate([out_grad, jnp.zeros((1, model_width), jnp.float32)], axis=0)
    slot_grad = (
        (slot_gate[:, None] * padded_grad[slot_token])
        .astype(jnp.bfloat16)
        .reshape(owners, capacity, model_width)
    )
    arrived_grad = lax.all_to_all(
        slot_grad, "expert", split_axis=0, concat_axis=0, tiled=True
    ).reshape(-1, model_width)
    sigmoid_gate = jax.nn.sigmoid(gate_pre)
    silu_gate = gate_pre * sigmoid_gate
    hidden = (silu_gate * up_pre).astype(jnp.bfloat16)
    hidden_grad = dot_last(arrived_grad, full_down)
    gate_pre_grad = (
        hidden_grad * up_pre * sigmoid_gate * (1.0 + gate_pre * (1.0 - sigmoid_gate))
    ).astype(jnp.bfloat16)
    up_pre_grad = (hidden_grad * silu_gate).astype(jnp.bfloat16)
    down_weight_grad = dot_first(hidden, arrived_grad)
    gate_weight_grad = dot_first(expert_rows, gate_pre_grad)
    up_weight_grad = dot_first(expert_rows, up_pre_grad)
    row_grad = (dot_last(gate_pre_grad, full_gate) + dot_last(up_pre_grad, full_up)).astype(
        jnp.bfloat16
    )
    token_rows_grad = lax.all_to_all(
        row_grad.reshape(owners, capacity, model_width),
        "expert",
        split_axis=0,
        concat_axis=0,
        tiled=True,
    )
    gate_summed, up_summed, down_summed = (
        lax.psum_scatter(
            gate_weight_grad.astype(jnp.bfloat16), "dp", scatter_dimension=0, tiled=True
        ).astype(jnp.float32),
        lax.psum_scatter(
            up_weight_grad.astype(jnp.bfloat16), "dp", scatter_dimension=0, tiled=True
        ).astype(jnp.float32),
        lax.psum_scatter(
            down_weight_grad.astype(jnp.bfloat16), "dp", scatter_dimension=1, tiled=True
        ).astype(jnp.float32),
    )
    dispatch_grad = jax.ops.segment_sum(
        token_rows_grad.reshape(-1, model_width).astype(jnp.float32),
        slot_token,
        num_segments=count_of_rows + 1,
    )[:count_of_rows]
    chosen_grad = gate_values * (
        gate_grad - jnp.sum(gate_values * gate_grad, axis=1, keepdims=True)
    )
    logit_grad = jnp.sum(route_hits * chosen_grad[:, :, None], axis=1).astype(jnp.bfloat16)
    router_grad = dot_first(ffn_in, logit_grad)
    ffn_grad = dispatch_grad + dot_last(logit_grad, full_router)
    ffn_gain_grad = jnp.sum(ffn_grad * normed_two, axis=0)
    scaled_two = ffn_grad * scale_ffn
    state_grad = out_grad + inverse_two * (
        scaled_two - normed_two * jnp.mean(scaled_two * normed_two, axis=1, keepdims=True)
    )
    branch_grad = state_grad.astype(jnp.bfloat16)
    out_weight_grad = dot_first(attended, branch_grad)
    attended_grad = (
        dot_last(branch_grad, full_out)
        .astype(jnp.bfloat16)
        .reshape(count_of_rows, groups, head_ratio, HEAD_DIM)
    )

    def spread_sum(running, operands):
        key_block, value_block, key_place, key_doc = operands
        probs = jnp.exp(span_scores(key_block, key_place, key_doc) - log_total)
        prob_grad = jnp.einsum(
            "qgrd,kgd->grqk", attended_grad, value_block, preferred_element_type=jnp.float32
        )
        return (running + jnp.sum(probs * prob_grad, axis=-1, keepdims=True), None)

    score_shift, _ = lax.scan(spread_sum, jnp.zeros(stat_shape, jnp.float32), key_spans)

    def back_span(running, operands):
        key_block, value_block, key_place, key_doc = operands
        probs = jnp.exp(span_scores(key_block, key_place, key_doc) - log_total)
        prob_grad = jnp.einsum(
            "qgrd,kgd->grqk", attended_grad, value_block, preferred_element_type=jnp.float32
        )
        score_grad = (probs * (prob_grad - score_shift)).astype(jnp.bfloat16)
        running = running + jnp.einsum(
            "grqk,kgd->qgrd", score_grad, key_block, preferred_element_type=jnp.float32
        )
        key_part = (
            jnp.einsum("grqk,qgrd->kgd", score_grad, grouped_q, preferred_element_type=jnp.float32)
            * score_scale
        )
        value_part = jnp.einsum(
            "grqk,qgrd->kgd",
            probs.astype(jnp.bfloat16),
            attended_grad,
            preferred_element_type=jnp.float32,
        )
        return (running, (key_part.reshape(key_span, -1), value_part.reshape(key_span, -1)))

    query_sum, (key_parts, value_parts) = lax.scan(
        back_span, jnp.zeros((count_of_rows, groups, head_ratio, HEAD_DIM), jnp.float32), key_spans
    )
    key_grad, value_sum = (
        lax.psum_scatter(
            key_parts.reshape(group_rows, -1).astype(jnp.bfloat16),
            "dp",
            scatter_dimension=0,
            tiled=True,
        ).astype(jnp.float32),
        lax.psum_scatter(
            value_parts.reshape(group_rows, -1).astype(jnp.bfloat16),
            "dp",
            scatter_dimension=0,
            tiled=True,
        ).astype(jnp.float32),
    )
    query_grad = query_sum * score_scale
    query_lin_grad = unrotate(
        query_grad.reshape(count_of_rows, head_count, HEAD_DIM), cosine_lookup, sine_lookup
    )
    query_lin_grad = query_lin_grad.reshape(count_of_rows, -1).astype(jnp.bfloat16)
    key_lin_grad = (
        unrotate(key_grad.reshape(count_of_rows, groups, HEAD_DIM), cosine_lookup, sine_lookup)
        .reshape(count_of_rows, -1)
        .astype(jnp.bfloat16)
    )
    value_lin_grad = value_sum.astype(jnp.bfloat16)
    query_weight_grad = dot_first(attention_input, query_lin_grad)
    key_weight_grad = dot_first(attention_input, key_lin_grad)
    value_weight_grad = dot_first(attention_input, value_lin_grad)
    attn_grad = (
        dot_last(query_lin_grad, full_query)
        + dot_last(key_lin_grad, gathered_key)
        + dot_last(value_lin_grad, gathered_value)
    )
    attn_gain_grad = jnp.sum(attn_grad * normed_one, axis=0)
    scaled_one = attn_grad * scale_attn
    tokens_grad = (
        state_grad
        + inverse_one
        * (scaled_one - normed_one * jnp.mean(scaled_one * normed_one, axis=1, keepdims=True))
    ).astype(jnp.bfloat16)
    summed = (
        lax.psum_scatter(attn_gain_grad, ("dp", "expert"), scatter_dimension=0, tiled=True),
        lax.psum_scatter(query_weight_grad, ("dp", "expert"), scatter_dimension=0, tiled=True),
        lax.psum_scatter(key_weight_grad, ("dp", "expert"), scatter_dimension=0, tiled=True),
        lax.psum_scatter(value_weight_grad, ("dp", "expert"), scatter_dimension=0, tiled=True),
        lax.psum_scatter(out_weight_grad, ("dp", "expert"), scatter_dimension=0, tiled=True),
        lax.psum_scatter(ffn_gain_grad, ("dp", "expert"), scatter_dimension=0, tiled=True),
        lax.psum_scatter(router_grad, ("dp", "expert"), scatter_dimension=0, tiled=True),
    )
    return (
        output,
        tokens_grad,
        summed[0],
        summed[1],
        summed[2],
        summed[3],
        summed[4],
        summed[5],
        summed[6],
        gate_summed[None],
        up_summed[None],
        down_summed[None],
    )


def solution(mesh):
    in_specs = (
        P(("dp", "expert"), None),
        P(("dp", "expert"), None),
        P(("dp", "expert")),
        P(("dp", "expert"), None),
        P(("dp", "expert"), None),
        P(("dp", "expert"), None),
        P(("dp", "expert"), None),
        P(("dp", "expert")),
        P(("dp", "expert"), None),
        P("expert", "dp", None),
        P("expert", "dp", None),
        P("expert", None, "dp"),
        P(("dp", "expert"), None),
        P(("dp", "expert"), None),
        P("expert", None),
        P(None, "expert", None),
    )
    out_specs = (
        P(("dp", "expert"), None),
        P(("dp", "expert"), None),
        P(("dp", "expert")),
        P(("dp", "expert"), None),
        P(("dp", "expert"), None),
        P(("dp", "expert"), None),
        P(("dp", "expert"), None),
        P(("dp", "expert")),
        P(("dp", "expert"), None),
        P("expert", "dp", None),
        P("expert", "dp", None),
        P("expert", None, "dp"),
    )
    fast = mesh.shape["dp"] == 2 and mesh.shape["expert"] == 16
    body = paired_body if fast else general_body
    return jax.shard_map(body, mesh=mesh, in_specs=in_specs, out_specs=out_specs, check_vma=False)
```

```python
import functools
import math

import jax
import jax.numpy as jnp
from jax import lax
from jax.experimental import pallas as pl
from jax.experimental.pallas import tpu as pltpu
from jax.sharding import PartitionSpec as P

HEAD_DIM = 64


NORM_EPS = 1e-05
MASK_FILL = -1e30
ROPE_BASE = 10000.0


def dot_plain(left_side, right_side):
    return jnp.dot(left_side, right_side, preferred_element_type=jnp.float32)


def dot_last(left_side, right_side):
    return lax.dot_general(
        left_side, right_side, (((1,), (1,)), ((), ())), preferred_element_type=jnp.float32
    )


def dot_first(left_side, right_side):
    return lax.dot_general(
        left_side, right_side, (((0,), (0,)), ((), ())), preferred_element_type=jnp.float32
    )


def doc_layout(lengths, places):
    doc_ends = jnp.cumsum(lengths)
    doc_starts = doc_ends - lengths
    doc_ids = jnp.sum((places[:, None] >= doc_ends[None, :]).astype(jnp.int32), axis=1)
    member = doc_ids[:, None] == jnp.arange(lengths.shape[0], dtype=jnp.int32)[None, :]
    offsets = places - jnp.sum(jnp.where(member, doc_starts[None, :], 0), axis=1)
    return (doc_ids, offsets)


def rope_tables(offsets, head_size):
    half_size = head_size // 2
    frequency = ROPE_BASE ** (-2.0 * jnp.arange(half_size, dtype=jnp.float32) / head_size)
    angles = offsets.astype(jnp.float32)[:, None] * frequency[None, :]
    return (jnp.cos(angles), jnp.sin(angles))


def apply_rotation(values, cosine_lookup, sine_lookup):
    half_size = values.shape[-1] // 2
    first_half = values[..., :half_size]
    second = values[..., half_size:]
    cos_rows = cosine_lookup[:, None, :]
    sin_rows = sine_lookup[:, None, :]
    return jnp.concatenate(
        [first_half * cos_rows - second * sin_rows, second * cos_rows + first_half * sin_rows],
        axis=-1,
    )


def unrotate(gradient, cosine_lookup, sine_lookup):
    half_size = gradient.shape[-1] // 2
    first_half = gradient[..., :half_size]
    second = gradient[..., half_size:]
    cos_rows = cosine_lookup[:, None, :]
    sin_rows = sine_lookup[:, None, :]
    return jnp.concatenate(
        [first_half * cos_rows + second * sin_rows, second * cos_rows - first_half * sin_rows],
        axis=-1,
    )


def assign_slots(routes, take_order, experts, capacity):
    count_of_rows, top_count = routes.shape
    flat_routes = routes.reshape(-1)
    chosen = flat_routes[take_order]
    expert_hits = (chosen[:, None] == jnp.arange(experts, dtype=jnp.int32)[None, :]).astype(
        jnp.int32
    )
    slot_rank = jnp.sum(jnp.cumsum(expert_hits, axis=0) * expert_hits, axis=1) - 1
    slot_index = jnp.where(slot_rank < capacity, chosen * capacity + slot_rank, experts * capacity)
    pair_slot = jnp.zeros((flat_routes.shape[0],), jnp.int32).at[take_order].set(slot_index)
    slot_token = (
        jnp.full((experts * capacity + 1,), count_of_rows, jnp.int32)
        .at[slot_index]
        .set(take_order // top_count)
    )
    return (pair_slot, slot_token[: experts * capacity])


MESH = pl.DeviceIdType.MESH
BF16 = jnp.bfloat16
F32 = jnp.float32
NAR = 128


def remote(src, dst, send_sem, recv_sem, device):
    return pltpu.make_async_remote_copy(
        src_ref=src,
        dst_ref=dst,
        send_sem=send_sem,
        recv_sem=recv_sem,
        device_id=device,
        device_id_type=MESH,
    )


class Place:
    def __init__(self):
        self.i = lax.axis_index("dp")
        self.e = lax.axis_index("expert")
        self.a = self.e // 4
        self.bc = self.e % 4
        self.y = self.bc // 2
        self.c = self.bc % 2

    def over_x(self):
        return (1 - self.i, self.e)

    def over_y(self):
        return (self.i, self.e + 2 - 4 * self.y)

    def over_core(self):
        return (self.i, self.e + 1 - 2 * self.c)

    def order(self, k):
        turn = (1 - 2 * k) * (1 - k // 2)
        inner = self.inner()
        half = self.a // 2
        step = k + inner * turn
        return step + half * (3 - 2 * step)

    def inner(self):
        return (self.a * (3 - self.a)) // 2

    def partner(self):
        return self.a + 1 - 2 * (self.a % 2)

    def barrier(self, whole_plane=False):
        sem = pltpu.get_barrier_semaphore()
        if whole_plane:
            peers = [(self.i, (self.e + shift) % 16) for shift in range(1, 16)]
        else:
            peers = [self.over_y(), self.over_core()]
            for shift in range(1, 4):
                peers.append((self.i, ((self.a + shift) % 4) * 4 + self.bc))
        peers.append(self.over_x())
        for peer in peers:
            pl.semaphore_signal(sem, inc=1, device_id=peer, device_id_type=MESH)
        pl.semaphore_wait(sem, len(peers))


class Gather:
    SENDS = 20
    RECVS = 16

    def __init__(self, place, view, sends, recvs, lean=False):
        self.p, self.view, self.sends, self.recvs = place, view, sends, recvs
        self.lean = lean

    def copy(self, block, slot, device):
        ref = self.view(block)
        return remote(ref, ref, self.sends.at[slot], self.recvs.at[block], device)

    def right(self, a1):
        return self.copy(a1 * 4 + self.p.bc, a1, (self.p.i, self.p.e + 4))

    def left(self, a1):
        return self.copy(a1 * 4 + self.p.bc, 4 + a1, (self.p.i, self.p.e - 4))

    def across(self, a1):
        return self.copy(a1 * 4 + self.p.bc, 8 + a1, self.p.over_y())

    def core(self, a1, y1):
        return self.copy(a1 * 4 + y1 * 2 + self.p.c, 12 + a1 * 2 + y1, self.p.over_core())

    def landed(self, block):
        self.copy(block, 0, self.p.over_core()).wait_recv()

    def handed(self):
        p = self.p
        device = (p.i, p.partner() * 4 + p.bc)
        return self.copy(p.a * 4 + (1 - p.y) * 2 + p.c, 8 + p.partner(), device)

    def hand(self):
        self.handed().start()

    def begin(self):
        p = self.p
        self.across(p.a).start()

        @pl.when(p.a < 3)
        def _():
            self.right(p.a).start()

        @pl.when(p.a > 0)
        def _():
            self.left(p.a).start()

        self.core(p.a, p.y).start()

    def phase(self, s):
        p = self.p
        inner = p.inner()
        if s == 1:
            self.along(1)

        @pl.when(inner == 1)
        def _():
            if s < 3:
                self.along(s + 1)

        if s > 1:

            @pl.when(inner == 0)
            def _():
                self.along(s)

    def along(self, k):
        p = self.p
        a1 = p.order(k)
        self.landed(a1 * 4 + p.bc)

        @pl.when((a1 < p.a) & (p.a < 3))
        def _():
            self.right(a1).start()

        @pl.when((a1 > p.a) & (p.a > 0))
        def _():
            self.left(a1).start()

        if k != 1 or not self.lean:
            self.across(a1).start()
        self.core(a1, p.y).start()

    def cross(self, k):
        p = self.p
        a1 = p.order(k)
        self.landed(a1 * 4 + (1 - p.y) * 2 + p.c)
        self.core(a1, 1 - p.y).start()

    def join(self, k):
        p = self.p
        a1 = p.order(k)
        self.landed(a1 * 4 + (1 - p.c))
        self.landed(a1 * 4 + 2 + (1 - p.c))

    def sent(self, k):
        p = self.p
        a1 = p.order(k)

        @pl.when((a1 <= p.a) & (p.a < 3))
        def _():
            self.right(a1).wait_send()

        @pl.when((a1 >= p.a) & (p.a > 0))
        def _():
            self.left(a1).wait_send()

        if k == 0 and self.lean:
            self.handed().wait_send()
        if k != 1 or not self.lean:
            self.across(a1).wait_send()
        self.core(a1, 0).wait_send()
        self.core(a1, 1).wait_send()

    def drain(self):
        for k in range(4):
            self.sent(k)


class Scatter:
    SENDS = 16
    RECVS = 17

    def __init__(self, place, part, core_in, y_in, a_in, pass_in, sends, recvs, lean=False):
        self.p, self.part, self.lean = place, part, lean
        self.core_in, self.y_in, self.a_in, self.pass_in = core_in, y_in, a_in, pass_in
        self.sends, self.recvs = sends, recvs

    def to_core(self, a1, y1):
        p = self.p
        slot = a1 * 2 + y1
        return remote(
            self.part(a1, y1 * 2 + 1 - p.c),
            self.core_in(a1, y1),
            self.sends.at[slot],
            self.recvs.at[slot],
            p.over_core(),
        )

    def to_y(self, a1):
        p = self.p
        return remote(
            self.part(a1, (1 - p.y) * 2 + p.c),
            self.y_in(a1),
            self.sends.at[8 + a1],
            self.recvs.at[8 + a1],
            p.over_y(),
        )

    def to_far(self, a1):
        p = self.p
        return remote(
            self.part(a1, p.bc),
            self.a_in(2),
            self.sends.at[12 + a1],
            self.recvs.at[14],
            (p.i, a1 * 4 + p.bc),
        )

    def to_inner(self, a1):
        p = self.p
        return remote(
            self.part(a1, p.bc),
            self.pass_in(a1 % 2),
            self.sends.at[12 + a1],
            self.recvs.at[15 + a1 % 2],
            (p.i, p.partner() * 4 + p.bc),
        )

    def to_partner(self, other):
        p = self.p
        a1 = p.partner()
        side = 1 - p.y if other else p.y
        return remote(
            self.part(a1, side * 2 + p.c),
            self.y_in(p.a) if other else self.a_in(1),
            self.sends.at[(8 if other else 12) + a1],
            self.recvs.at[8 + p.a if other else 13],
            (p.i, a1 * 4 + p.bc),
        )

    def from_partner(self, other):
        p = self.p
        spot = self.y_in(p.partner()) if other else self.a_in(1)
        slot = 8 + p.partner() if other else 13
        return remote(spot, spot, self.sends.at[0], self.recvs.at[slot], p.over_core())

    def start(self, k):
        a1 = self.p.order(k)
        self.to_core(a1, 0).start()
        self.to_core(a1, 1).start()

    def add(self, ref, other):
        ref[...] = (ref[...].astype(F32) + other[...].astype(F32)).astype(ref.dtype)

    def core(self, k):
        p = self.p
        a1 = p.order(k)
        for y1 in range(2):
            self.to_core(a1, y1).wait_recv()
        self.add(self.part(a1, (1 - p.y) * 2 + p.c), self.core_in(a1, 1 - p.y))
        if k > 1 or not self.lean:
            self.to_y(a1).start()
        elif k == 1:
            self.to_partner(True).start()
        self.add(self.part(a1, p.bc), self.core_in(a1, p.y))
        if k == 1 and self.lean:
            self.to_partner(False).start()

    def meet(self):
        p = self.p
        self.from_partner(True).wait_recv()
        self.add(self.part(p.a, (1 - p.y) * 2 + p.c), self.y_in(p.partner()))
        self.to_y(p.a).start()

    def cross(self, k):
        p = self.p
        a1 = p.order(k)
        self.to_y(a1).wait_recv()
        self.add(self.part(a1, p.bc), self.y_in(a1))
        if k == 1:
            self.to_partner(False).start()
        if k > 1:

            @pl.when(p.inner() == 0)
            def _():
                self.to_inner(a1).start()

    def relay(self, k):
        p = self.p
        a1 = p.order(k)

        @pl.when(p.inner() == 1)
        def _():
            self.to_inner(a1).wait_recv()
            self.add(self.part(a1, p.bc), self.pass_in(a1 % 2))
            self.to_far(a1).start()

    def finish(self):
        self.from_partner(False).wait_recv()
        self.to_far(self.p.a).wait_recv()

    def total(self):
        own = self.part(self.p.a, self.p.bc)[...].astype(F32)
        return own + self.a_in(1)[...].astype(F32) + self.a_in(2)[...].astype(F32)

    def drain(self):
        p = self.p
        for k in range(4):
            a1 = p.order(k)
            self.to_core(a1, 0).wait_send()
            self.to_core(a1, 1).wait_send()
            if k == 1:
                self.to_partner(False).wait_send()
            if k == 1 and self.lean:
                self.to_partner(True).wait_send()
            else:
                self.to_y(a1).wait_send()
            if k > 1:
                self.to_far(a1).wait_send()


class Exchange:
    def __init__(self, place, source, target, sends, recvs):
        self.p, self.source, self.target, self.sends, self.recvs = place, source, target, sends, recvs

    def copy(self, there):
        p = self.p
        return remote(
            self.source.at[there], self.target.at[p.e], self.sends.at[there], self.recvs.at[p.e], (p.i, there)
        )

    def give(self, there):
        @pl.when(there != self.p.e)
        def _():
            self.copy(there).start()

        @pl.when(there == self.p.e)
        def _():
            self.target[there] = self.source[there]

    def take(self, there):
        p = self.p

        @pl.when(there != p.e)
        def _():
            remote(
                self.target.at[there], self.target.at[there], self.sends.at[there], self.recvs.at[there], (p.i, there)
            ).wait_recv()

    def drain(self):
        @pl.loop(0, 16)
        def _(there):
            @pl.when(there != self.p.e)
            def _():
                self.copy(there).wait_send()


def lane_iota(shape):
    return lax.broadcasted_iota(jnp.int32, shape, len(shape) - 1)


def swap_halves(values):
    lane = lane_iota(values.shape) % HEAD_DIM
    half = HEAD_DIM // 2
    return jnp.where(
        lane < half,
        pltpu.roll(values, values.shape[-1] - half, 1),
        pltpu.roll(values, half, 1),
    )


def split_heads(tile):
    low = lane_iota(tile.shape) < HEAD_DIM
    turned = pltpu.roll(tile, HEAD_DIM, 1)
    zero = jnp.zeros_like(tile)
    return (
        (jnp.where(low, tile, zero), jnp.where(low, zero, turned)),
        (jnp.where(low, turned, zero), jnp.where(low, zero, tile)),
    )


def inverse_rms(values):
    return lax.rsqrt(jnp.mean(values * values, axis=1, keepdims=True) + NORM_EPS)


def gain_rows(narrow, experts):
    shape = (16, narrow.shape[1])
    row = lax.broadcasted_iota(jnp.int32, shape, 0)
    pick = jnp.where(lane_iota(shape) == row + experts, 1.0, 0.0).astype(BF16)
    return dot_last(pick, narrow)


def column_of(row):
    n = row.shape[1]
    shape = (n, n)
    same = lane_iota(shape) == lax.broadcasted_iota(jnp.int32, shape, 0)
    return jnp.sum(jnp.where(same, row, 0.0), axis=1, keepdims=True)


def row_of(column):
    n = column.shape[0]
    shape = (n, n)
    same = lane_iota(shape) == lax.broadcasted_iota(jnp.int32, shape, 0)
    return jnp.sum(jnp.where(same, column, 0.0), axis=0, keepdims=True)


def documents(places, ends):
    doc = jnp.zeros_like(places)
    start = jnp.zeros_like(places)
    for end in ends:
        past = places >= end
        doc = doc + jnp.where(past, 1.0, 0.0)
        start = jnp.where(past, end, start)
    return doc, start


def turned(values):
    m, n = values.shape
    if n < NAR:
        values = jnp.concatenate([values, jnp.zeros((m, NAR - n), F32)], axis=1)
    if m < NAR:
        values = jnp.concatenate([values, jnp.zeros((NAR - m, NAR), F32)], axis=0)
    return jnp.transpose(values)[:n, :m]


def kept_pairs(routes_by_rank, take_order, experts, capacity):
    top_count, rows = routes_by_rank.shape
    routes = turned(routes_by_rank.astype(F32)).astype(jnp.int32)
    lane = lane_iota((rows, NAR))
    token = lax.broadcasted_iota(jnp.int32, (rows, 1), 0)
    number = lane_iota((rows, take_order.shape[1])).astype(F32)
    hit = jnp.zeros((rows, NAR), jnp.bool_)
    taken = jnp.zeros((rows, NAR), F32)
    for j in range(top_count):
        at = jnp.sum(jnp.where(take_order == token * top_count + j, number, 0.0), axis=1, keepdims=True)
        mine = lane == routes[:, j : j + 1]
        hit = hit | mine
        taken = jnp.where(mine, at, taken)
    taken = jnp.where(hit, taken, 1e9)
    across = jnp.transpose(taken)
    rank = jnp.zeros((rows, NAR), F32)
    for name in range(experts):
        before = jnp.where(across[name : name + 1, :] < taken[:, name : name + 1], 1.0, 0.0)
        rank = jnp.where(lane == name, jnp.sum(before, axis=1, keepdims=True), rank)
    one, zero = jnp.ones((rows, NAR), F32), jnp.zeros((rows, NAR), F32)
    hits = jnp.where(hit, one, zero)
    return hits, jnp.where(rank < capacity, hits, zero)


def layer_kernel(
    tok, wq, wk, wv, wr, na, nf, wo, cot, eg, eu, ed, routes, slots, lengths, places,
    out, tok_grad, dq_out, dk_out, dv_out, dwo_out, gains_out, gu_own, od_own, gur, edr, mixp,
    w_all, wo_all, x_all, q, klo, khi, vlo, vhi, pr, att, hid, vis, cs, sn, hit, kept, gates, opart, orecv,
    f_all, part, og, hgu, core_in, y_in, a_in, pass_in, gate_out, gate_in, grad_out, grad_in, wgu, wd, h12, mix,
    dk, dv, small, state, wsend, wgive, wrecv,
    ga_s, ga_r, gb_s, gb_r, gw_s, gw_r, gc_s, gc_r, gf_s, gf_r, sc_s, sc_r, sm_s, sm_r, so_s, so_r, sw_s, sw_r,
    gs_s, gs_r, gg_s, gg_r, xs, xr, loc, mix_sem, ready,
):
    p = Place()
    i, e = p.i, p.e
    rows, width = tok.shape
    depth = wo.shape[0]
    plane = 16 * depth
    group = 4 * rows
    group_rows_count = 2 * rows
    half = width // 2
    ff = wd.shape[0]
    q_width = q.shape[1]
    k_width = dk.shape[1]
    experts = 16
    wide = q_width + 2 * k_width
    capacity = 9 * rows * routes.shape[0] // (8 * experts)
    ratio = q_width // k_width
    scale = HEAD_DIM**-0.5
    heads = q_width // HEAD_DIM
    near = [p.order(k) for k in range(4)]

    def w_row(ip, block):
        return pl.ds(pl.multiple_of(ip * plane + block * depth, 16), depth)

    def row_block(ip):
        return pl.ds(pl.multiple_of(ip * rows, rows), rows)

    def half_lanes(ip, n):
        return pl.ds(pl.multiple_of(ip * n, 128), n)

    def half_rows(ip):
        return pl.ds(pl.multiple_of(ip * half, half), half)

    def group_rows(a1):
        return pl.ds(pl.multiple_of(a1 * group, group), group)

    lane = lane_iota((depth, NAR))
    gain_cols = [column_of(r[...].astype(F32)) for r in (na, nf)]
    narrow_own = jnp.concatenate([turned(wr[...].astype(F32)), jnp.zeros((depth, NAR - experts), F32)], axis=1)
    narrow_own = jnp.where(lane == experts, gain_cols[0], jnp.where(lane == experts + 1, gain_cols[1], narrow_own))
    own = w_row(i, e)
    w_all[own, wide:] = narrow_own.astype(BF16)
    w_all[own, :q_width] = wq[:, half_lanes(i, q_width)]
    w_all[own, q_width : q_width + k_width] = wk[:, half_lanes(i, k_width)]
    w_all[own, q_width + k_width : wide] = wv[:, half_lanes(i, k_width)]
    p.barrier(whole_plane=True)
    cuts = (
        (wq.at[:, half_lanes(1 - i, q_width)], 0, q_width),
        (wk.at[:, half_lanes(1 - i, k_width)], q_width, k_width),
        (wv.at[:, half_lanes(1 - i, k_width)], q_width + k_width, k_width),
        (w_all.at[own, pl.ds(wide, NAR)], wide, NAR),
    )
    give_w = [
        remote(src, w_all.at[own, pl.ds(first, size)], xs.at[n], xr.at[n], p.over_x())
        for n, (src, first, size) in enumerate(cuts)
    ]
    for one in give_w:
        one.start()
    give_x = remote(tok, x_all.at[i], xs.at[4], xr.at[4], p.over_x())
    take_x = remote(x_all.at[1 - i], x_all.at[1 - i], xs.at[4], xr.at[4], p.over_x())
    give_x.start()

    ga = Gather(p, lambda block: w_all.at[w_row(i, block)], ga_s, ga_r)
    gb = Gather(p, lambda block: w_all.at[w_row(1 - i, block)], gb_s, gb_r)
    gw = Gather(p, lambda block: wo_all.at[w_row(0, block)], gw_s, gw_r)
    gc = Gather(p, lambda block: og.at[row_block(block)], gc_s, gc_r, lean=True)
    gf = Gather(p, lambda block: f_all.at[row_block(block)], gf_s, gf_r)

    ga.begin()
    own_cot = pltpu.make_async_copy(cot, og.at[row_block(e)], loc.at[0])
    own_cot.start()
    loads = [
        pltpu.make_async_copy(src, dst, loc.at[1 + n])
        for n, (src, dst) in enumerate(((eg, wgu.at[half_rows(i), pl.ds(0, ff)]), (eu, wgu.at[half_rows(i), pl.ds(ff, ff)]), (ed, wd.at[:, half_rows(i)])))
    ]
    for one in loads:
        one.start()
    wo_all[w_row(0, e), :] = wo[...]
    x_all[i] = tok[...]
    for n, (_, first, size) in enumerate(cuts):
        there = w_all.at[w_row(1 - i, e), pl.ds(first, size)]
        remote(there, there, xs.at[n], xr.at[n], p.over_x()).wait_recv()
    gb.begin()
    cut = ff // 48 * 16
    weight_moves = (
        (eg, lambda ip: wgu.at[half_rows(ip), pl.ds(0, ff)]),
        (eu, lambda ip: wgu.at[half_rows(ip), pl.ds(ff, ff)]),
        (ed.at[pl.ds(0, cut)], lambda ip: wd.at[pl.ds(0, cut), half_rows(ip)]),
        (ed.at[pl.ds(cut, ff - cut)], lambda ip: wd.at[pl.ds(cut, ff - cut), half_rows(ip)]),
    )
    give_e = [
        remote(src, dst(i), xs.at[5 + n], xr.at[5 + n], p.over_x()) for n, (src, dst) in enumerate(weight_moves)
    ]
    take_e = [
        remote(dst(1 - i), dst(1 - i), xs.at[5 + n], xr.at[5 + n], p.over_x())
        for n, (src, dst) in enumerate(weight_moves)
    ]
    for one in give_e[:3]:
        one.start()

    ends = [lengths[0, 0].astype(F32)]
    for n in range(1, lengths.shape[1]):
        ends.append(ends[-1] + lengths[0, n].astype(F32))
    place_row = places[...].astype(F32)
    place_col = column_of(place_row)
    doc_row, _ = documents(place_row, ends[:-1])
    doc_col, start_col = documents(place_col, ends[:-1])
    vis[...] = jnp.where((doc_row == doc_col) & (place_col >= place_row), 1.0, 0.0)
    lane = lane_iota((1, 128))
    quarter = HEAD_DIM // 2
    freq = jnp.exp((lane % quarter).astype(F32) * (-2.0 / HEAD_DIM * math.log(ROPE_BASE)))
    angle = (place_col - start_col) * freq
    cs[...] = jnp.cos(angle)
    sine = jnp.sin(angle)
    sn[...] = jnp.where(lane % HEAD_DIM < quarter, -sine, sine)

    both = (ga, gb)
    for g in both:
        g.phase(1)
    hits, keeps = kept_pairs(routes[...], slots[...], experts, capacity)
    hit[...] = hits
    kept[...] = keeps
    for k in range(3):
        for g in both:
            g.cross(k)
        if k < 2:
            for g in both:
                g.phase(k + 2)
        if k == 1:
            gw.begin()
    gw.phase(1)
    own_cot.wait()
    for g in both:
        g.cross(3)
    for k in range(4):
        for g in both:
            g.join(k)

    events = [
        functools.partial(gw.phase, 2),
        functools.partial(gw.cross, 0),
        functools.partial(gw.phase, 3),
        gc.begin,
        functools.partial(gw.cross, 1),
        functools.partial(gw.cross, 2),
        functools.partial(gw.cross, 3),
    ]

    def serve():
        if events:
            events.pop(0)()

    take_x.wait_recv()
    narrow = w_all[:, wide:]
    gains = gain_rows(narrow, experts)
    att_in = mix.at[pl.ds(2 * rows, 2 * rows)]

    def fill_att_in():
        for ip in range(2):
            x = x_all[ip].astype(F32)
            att_in[ip * rows : (ip + 1) * rows, :] = (x * inverse_rms(x) * gains[0:1]).astype(BF16)

    fill_att_in()
    serve()
    cos, sin = cs[...], sn[...]

    def rope(values):
        return values * cos + swap_halves(values) * sin

    def unrope(values):
        return values * cos - swap_halves(values) * sin

    for tile in range(wide // 256):
        lin = dot_plain(att_in[...], w_all[:, tile * 256 : (tile + 1) * 256])
        for h in range(2):
            col = tile * 256 + h * 128
            piece = lin[:, h * 128 : (h + 1) * 128]
            if col < q_width:
                q[:, col : col + 128] = rope(piece).astype(BF16)
                continue
            is_key = col < q_width + k_width
            n = (col - q_width - (0 if is_key else k_width)) // 128
            lows, highs = (klo, khi) if is_key else (vlo, vhi)
            for g, (low, high) in enumerate(split_heads(rope(piece) if is_key else piece)):
                lows[2 * n + g] = low.astype(BF16)
                highs[2 * n + g] = high.astype(BF16)
    serve()
    sides = ((klo, vlo), (khi, vhi))
    for pair in range(heads // 2):
        lanes = slice(pair * 128, (pair + 1) * 128)
        total = None
        for side, (keys, vals) in enumerate(sides):
            head = 2 * pair + side
            g = head // ratio
            scores = dot_last(q[:, lanes], keys[g]) * scale
            scores = jnp.where(vis[...] > 0, scores, MASK_FILL)
            grown = jnp.exp(scores - jnp.max(scores, axis=1, keepdims=True))
            probs = (grown / jnp.sum(grown, axis=1, keepdims=True)).astype(BF16)
            pr[head] = probs
            term = dot_plain(probs, vals[g])
            total = term if total is None else total + term
        att[:, lanes] = total.astype(BF16)
        serve()
    while events:
        serve()
    for k in range(4):
        gw.join(k)
    gc.phase(1)
    opart[...] = dot_plain(att[row_block(1 - i), :], wo_all[...]).astype(BF16)
    give_o = remote(opart, orecv, xs.at[9], xr.at[9], p.over_x())
    give_o.start()
    give_e[3].start()
    hid[...] = tok[...].astype(F32) + dot_plain(att[row_block(i), :], wo_all[...])
    gc.cross(0)
    gc.phase(2)
    for one in loads:
        one.wait()
    give_o.wait()
    hidden = hid[...] + orecv[...].astype(F32)
    hid[...] = hidden
    ffn_in = (hidden * inverse_rms(hidden) * gains[1:2]).astype(BF16)
    f_all[row_block(e), :] = ffn_in
    gf.begin()
    logits = dot_plain(ffn_in, narrow)
    chosen = hit[...] > 0
    logits = jnp.where(chosen, logits, MASK_FILL)
    grown = jnp.where(chosen, jnp.exp(logits - jnp.max(logits, axis=1, keepdims=True)), 0.0)
    gate = grown / jnp.sum(grown, axis=1, keepdims=True)
    gates[...] = gate
    gate_rows = jnp.transpose(gate * kept[...])
    for name in range(experts):
        gate_out[name] = jnp.broadcast_to(gate_rows[name : name + 1, :], (8, rows))
    gates_in = Exchange(p, gate_out, gate_in, gs_s, gs_r)
    grads_in = Exchange(p, grad_out, grad_in, gg_s, gg_r)

    @pl.loop(0, experts)
    def _(there):
        gates_in.give(there)

    gc.hand()
    gc.phase(3)
    sc = Scatter(
        p,
        lambda a1, b1: part.at[row_block(a1 * 4 + b1)],
        lambda a1, y1: core_in.at[a1 * 2 + y1],
        lambda a1: y_in.at[a1],
        lambda slot: a_in.at[slot - 1],
        lambda j: pass_in.at[j],
        sc_s, sc_r, lean=True,
    )

    def store_mix(a1):
        return pltpu.make_async_copy(mix, mixp.at[a1], mix_sem)

    def gate_of(k):
        return jnp.concatenate([column_of(gate_in[near[k] * 4 + b1, 0:1, :]) for b1 in range(4)], axis=0)

    def inward(k):
        here = group_rows(near[k])
        h12[...] = dot_plain(f_all[here, :], wgu[...])
        pre = h12[:, :ff]
        hgu[here, 0:ff] = (pre * jax.nn.sigmoid(pre) * h12[:, ff:]).astype(BF16)

    def outward(k):
        a1 = near[k]
        here = group_rows(a1)
        if k > 0:
            store_mix(near[k - 1]).wait()
        gate = gate_of(k)

        def project(n, gate_grad):
            cols = pl.ds(pl.multiple_of(n * 512, 512), 512)
            res = dot_plain(hgu[here, 0:ff], wd[:, cols]).astype(BF16).astype(F32)
            mix[:, cols] = (gate * res).astype(BF16)
            c = og[here, cols].astype(F32)
            og[here, cols] = (gate * c).astype(BF16)
            return gate_grad + jnp.sum(res * c, axis=1, keepdims=True)

        gc.sent(k)
        gate_grad = lax.fori_loop(0, width // 512, project, jnp.zeros((group, 1), F32))
        store_mix(a1).start()
        for b1 in range(4):
            row = row_of(gate_grad[b1 * rows : (b1 + 1) * rows])
            grad_out[a1 * 4 + b1] = jnp.broadcast_to(row, (8, rows))
            grads_in.give(a1 * 4 + b1)

    def backward(k):
        here = group_rows(near[k])
        hg = dot_last(og[here, :], wd[...])
        pre = h12[:, :ff]
        s = jax.nn.sigmoid(pre)
        hgu[here, ff : 2 * ff] = (hg * h12[:, ff:] * s * (1.0 + pre * (1.0 - s))).astype(BF16)
        hgu[here, 2 * ff :] = (hg * (pre * s)).astype(BF16)

    def send_rows(k):
        here = group_rows(near[k])

        @pl.loop(0, width // 512)
        def _(n):
            cols = pl.ds(pl.multiple_of(n * 512, 512), 512)
            part[here, cols] = dot_last(hgu[here, ff:], wgu[cols, :]).astype(BF16)

        sc.start(k)

    for one in take_e[:2]:
        one.wait_recv()

    @pl.loop(0, experts)
    def _(there):
        gates_in.take(there)

    gf.cross(0)
    gf.phase(1)
    gc.join(0)
    gf.join(0)
    inward(0)
    take_e[2].wait_recv()
    take_e[3].wait_recv()
    outward(0)
    gc.cross(1)
    gc.cross(2)
    gf.phase(2)
    backward(0)
    send_rows(0)
    gf.cross(1)
    gf.phase(3)
    gc.join(1)
    gf.join(1)
    inward(1)
    outward(1)
    gc.cross(3)
    backward(1)
    gf.cross(2)
    send_rows(1)
    gc.join(2)
    gf.join(2)
    inward(2)
    sc.core(1)
    outward(2)
    backward(2)
    gf.cross(3)
    send_rows(2)
    gc.join(3)
    gf.join(3)
    inward(3)
    sc.core(2)
    outward(3)
    backward(3)
    send_rows(3)
    sc.cross(2)

    tile = 256
    tiles = half // tile

    def rows_of(ip, n):
        return pl.ds(pl.multiple_of(ip * half + n * tile, tile), tile)

    def in_grad(ip, n):
        return dot_first(f_all[:, rows_of(ip, n)], hgu[:, ff:])

    def down_grad(ip, n):
        return dot_first(hgu[:, 0:ff], og[:, rows_of(ip, n)])

    def give_in(n):
        src, dst = wgu.at[half_rows(1 - i), pl.ds(n * ff, ff)], gur.at[:, pl.ds(n * ff, ff)]
        return remote(src, dst, xs.at[10 + n], xr.at[10 + n], p.over_x())

    give_g, give_u = give_in(0), give_in(1)
    give_d = remote(wd.at[:, half_rows(1 - i)], edr, xs.at[12], xr.at[12], p.over_x())

    for n in range(tiles):
        wgu[rows_of(1 - i, n), :] = in_grad(1 - i, n).astype(BF16)
        if n == 0:
            sc.core(3)
        if n == 1:
            sc.core(0)
            sc.meet()
    give_g.start()

    @pl.loop(0, tiles)
    def _(n):
        wd[:, rows_of(1 - i, n)] = down_grad(1 - i, n).astype(BF16)

    sc.relay(2)

    def save(n, src, dst):
        return pltpu.make_async_copy(src, dst, loc.at[n % 4])

    saves = []
    for n in range(tiles):
        spot = h12.at[pl.ds((n % 2) * tile, tile)]
        if n >= 2:
            saves[n - 2].wait()
        spot[...] = in_grad(i, n)
        saves.append(save(n, spot, gu_own.at[pl.ds(n * tile, tile)]))
        saves[n].start()
    for n in range(tiles - 2, tiles):
        saves[n].wait()
    sc.cross(3)
    saves = []
    for n in range(tiles):
        spot = h12.at[:, pl.ds(n * tile, tile)]
        spot[...] = down_grad(i, n)
        saves.append(save(n, spot, od_own.at[:, pl.ds(n * tile, tile)]))
        saves[n].start()
    store_mix(near[3]).wait()
    gf.drain()

    spare = 16 * rows - 2 * group_rows_count
    dq = hgu.at[pl.ds(spare, group_rows_count), pl.ds(0, wide)]
    bg = hgu.at[pl.ds(spare + group_rows_count, group_rows_count)]
    ag = mix.at[pl.ds(0, group_rows_count), pl.ds(0, q_width)]
    friends = [p.over_x(), p.over_core(), p.over_y()] + [(i, ((p.a + shift) % 4) * 4 + p.bc) for shift in range(1, 4)]
    for friend in friends:
        pl.semaphore_signal(ready.at[0], inc=1, device_id=friend, device_id_type=MESH)
    load_mix = [pltpu.make_async_copy(mixp.at[a1], f_all.at[group_rows(a1)], loc.at[4 + k]) for k, a1 in enumerate(near)]
    for one in load_mix:
        one.start()
    sm = Scatter(
        p,
        lambda a1, b1: f_all.at[row_block(a1 * 4 + b1)],
        lambda a1, y1: og.at[row_block(a1 * 2 + y1)],
        lambda a1: og.at[row_block(8 + a1)],
        lambda slot: og.at[row_block(11 + slot)],
        lambda j: og.at[row_block(14 + j)],
        sm_s, sm_r, lean=True,
    )

    def piece_of(n):
        return hgu.at[pl.ds(pl.multiple_of(n * depth, 16), depth)]

    so = Scatter(
        p,
        lambda a1, b1: piece_of(a1 * 4 + b1),
        lambda a1, y1: piece_of(16 + a1 * 2 + y1),
        lambda a1: piece_of(24 + a1),
        lambda slot: piece_of(27 + slot),
        lambda j: piece_of(30 + j),
        so_s, so_r,
    )
    both_rows = 2 * depth
    flat = (pl.ds(0, both_rows), pl.ds(0, wide + NAR))
    sw = Scatter(
        p,
        lambda a1, b1: part.at[pl.ds(pl.multiple_of((a1 * 4 + b1) * both_rows, 32), both_rows), pl.ds(0, wide + NAR)],
        lambda a1, y1: core_in.at[(a1 * 2 + y1,) + flat],
        lambda a1: y_in.at[(a1,) + flat],
        lambda slot: a_in.at[(slot - 1,) + flat],
        lambda j: pass_in.at[(j,) + flat],
        sw_s, sw_r,
    )
    for one in load_mix:
        one.wait()
    pl.semaphore_wait(ready.at[0], len(friends))
    for k in (3, 2, 1, 0):
        sm.start(k)
    sm.core(3)
    sm.core(2)
    sc.relay(3)
    sc.cross(0)
    sm.core(1)
    sm.core(0)

    @pl.loop(0, experts)
    def _(there):
        grads_in.take(there)

    by_expert = jnp.concatenate([grad_in[name, 0:1, :] for name in range(experts)], axis=0)
    lane = lane_iota((rows, NAR))
    gate_grad = jnp.concatenate([turned(by_expert), jnp.zeros((rows, NAR - experts), F32)], axis=1) * kept[...]
    gate = gates[...]
    logit_grad = (gate * (gate_grad - jnp.sum(gate * gate_grad, axis=1, keepdims=True))).astype(BF16)
    narrow = w_all[:, wide:]
    gains = gain_rows(narrow, experts)
    routed = dot_last(logit_grad, narrow)
    hidden = hid[...]
    r2 = inverse_rms(hidden)
    n2 = hidden * r2
    again = pltpu.make_async_copy(cot, opart, loc.at[8])
    again.start()
    again.wait()
    sc.finish()
    ffn_grad = sc.total() + routed
    d2 = ffn_grad * gains[1:2]
    state[...] = opart[...].astype(F32) + r2 * (d2 - n2 * jnp.mean(d2 * n2, axis=1, keepdims=True))
    bg[row_block(i), :] = state[...].astype(BF16)
    give_b = remote(bg.at[row_block(i)], bg.at[row_block(i)], xs.at[13], xr.at[13], p.over_x())
    take_b = remote(bg.at[row_block(1 - i)], bg.at[row_block(1 - i)], xs.at[13], xr.at[13], p.over_x())
    give_b.start()
    give_u.start()
    sc.drain()
    for friend in friends[1:]:
        pl.semaphore_signal(ready.at[1], inc=1, device_id=friend, device_id_type=MESH)
    gain_ffn = jnp.sum(ffn_grad * n2, axis=0, keepdims=True)
    ffn_in = (n2 * gains[1:2]).astype(BF16)
    small[...] = dot_first(ffn_in, logit_grad)
    for n in range(width // NAR):
        span = slice(n * NAR, (n + 1) * NAR)
        small[span, :] = jnp.where(lane == experts + 1, column_of(gain_ffn[:, span]), small[span, :])
    for one in saves:
        one.wait()
    for one in give_w + [give_x] + give_e:
        one.wait_send()
    for g in (ga, gb, gw):
        g.drain()
    gates_in.drain()
    grads_in.drain()
    fill_att_in()
    dk[...] = jnp.zeros_like(dk)
    dv[...] = jnp.zeros_like(dv)
    low_lane = lane_iota((2 * rows, 128)) < HEAD_DIM
    sm.cross(3)
    take_b.wait_recv()
    for n in range(q_width // 256):
        lanes = slice(n * 256, (n + 1) * 256)
        ag[:, lanes] = dot_last(bg[...], wo_all[lanes, :]).astype(BF16)
    for n in range(q_width // 256):
        lanes = slice(n * 256, (n + 1) * 256)
        hgu[lanes, :] = dot_first(att[:, lanes], bg[...]).astype(BF16)
    for k in (3, 2, 1, 0):
        so.start(k)
    for pair in range(heads // 2):
        lanes = slice(pair * 128, (pair + 1) * 128)
        grad_in_pair = ag[:, lanes]
        q_pair = q[:, lanes]
        q_grad = None
        for side, (keys, vals) in enumerate(sides):
            head = 2 * pair + side
            g = head // ratio
            probs = pr[head]
            prob_grad = dot_last(grad_in_pair, vals[g])
            wide_probs = probs.astype(F32)
            shift = jnp.sum(wide_probs * prob_grad, axis=1, keepdims=True)
            score_grad = (wide_probs * (prob_grad - shift)).astype(BF16)
            term = dot_plain(score_grad, keys[g])
            q_grad = term if q_grad is None else q_grad + term
            mine = low_lane if side == 0 else jnp.logical_not(low_lane)
            k_term = jnp.where(mine, dot_first(score_grad, q_pair), 0.0)
            v_term = jnp.where(mine, dot_first(probs, grad_in_pair), 0.0)
            if g % 2 != side:
                k_term = pltpu.roll(k_term, HEAD_DIM, 1)
                v_term = pltpu.roll(v_term, HEAD_DIM, 1)
            lot = slice((g // 2) * 128, (g // 2 + 1) * 128)
            dk[:, lot] += k_term
            dv[:, lot] += v_term
        dq[:, lanes] = unrope(scale * q_grad).astype(BF16)
        if pair == 0:
            for k in (3, 2, 1, 0):
                so.core(k)
            sm.cross(2)
        if pair == 1:
            sm.meet()
            sm.relay(3)
        if pair == 3:
            so.cross(3)
            sm.relay(2)
        if pair == 4:
            so.cross(2)
            so.cross(1)
        if pair == 5:
            so.relay(3)
    for n in range(k_width // 128):
        lanes = slice(n * 128, (n + 1) * 128)
        dq[:, q_width + n * 128 : q_width + (n + 1) * 128] = unrope(scale * dk[:, lanes]).astype(BF16)
        dq[:, q_width + k_width + n * 128 : q_width + k_width + (n + 1) * 128] = dv[:, lanes].astype(BF16)

    both_back = dot_last(dq[...], w_all[:, :wide])
    bg_terms = jnp.zeros((1, width), F32)
    for ip in range(2):
        x = x_all[ip].astype(F32)
        bg_terms = bg_terms + jnp.sum(both_back[ip * rows : (ip + 1) * rows] * (x * inverse_rms(x)), axis=0, keepdims=True)
    for n in range(width // NAR):
        span = slice(n * NAR, (n + 1) * NAR)
        small[span, :] = jnp.where(lane == experts, column_of(bg_terms[:, span]), small[span, :])
    h12[0 : 2 * rows, :] = both_back[:, : 2 * ff]
    h12[2 * rows :, 0 : width - 2 * ff] = both_back[:, 2 * ff :]

    def back_rows(ip):
        return jnp.concatenate([h12[row_block(ip), :], h12[row_block(2 + ip), 0 : width - 2 * ff]], axis=1)

    opart[...] = back_rows(1 - i).astype(BF16)
    give_a = remote(opart, orecv, xs.at[14], xr.at[14], p.over_x())
    give_a.start()
    give_d.start()
    step = plane // 2
    count = step // depth
    for turn in range(2):
        n = near[3 - 3 * turn] // 2
        for ip in range(2):
            span = pl.ds(pl.multiple_of(ip * plane + n * step, 128), step)
            block = dot_first(att_in[:, span], dq[...]).astype(BF16)
            extra = small[span, :].astype(BF16)
            for m in range(count):
                at = pl.ds(pl.multiple_of((n * count + m) * both_rows + ip * depth, 16), depth)
                part[at, :wide] = block[m * depth : (m + 1) * depth]
                part[at, wide : wide + NAR] = extra[m * depth : (m + 1) * depth]
        if turn == 0:
            pl.semaphore_wait(ready.at[1], len(friends) - 1)
        sw.start(3 - 2 * turn)
        sw.start(2 - 2 * turn)
    for k in (3, 2, 1, 0):
        sw.core(k)
    so.relay(2)
    so.cross(0)
    sw.cross(3)
    sw.cross(2)
    give_a.wait_recv()
    attn_grad = back_rows(i) + orecv[...].astype(F32)
    x = x_all[i].astype(F32)
    r1 = inverse_rms(x)
    n1 = x * r1
    d1 = attn_grad * gains[0:1]
    tok_grad[...] = (state[...] + r1 * (d1 - n1 * jnp.mean(d1 * n1, axis=1, keepdims=True))).astype(BF16)
    sw.relay(3)
    sw.cross(1)
    sw.relay(2)
    sw.cross(0)
    sw.finish()
    summed = sw.total()
    wsend[0] = summed[:depth]
    wsend[1] = summed[depth:]
    wgive[...] = wsend[1 - i].astype(BF16)
    give_s = remote(wgive, wrecv, xs.at[15], xr.at[15], p.over_x())
    give_s.start()

    def place_half(ip, values):
        dq_out[:, half_lanes(ip, q_width)] = values[:, :q_width]
        dk_out[:, half_lanes(ip, k_width)] = values[:, q_width : q_width + k_width]
        dv_out[:, half_lanes(ip, k_width)] = values[:, q_width + k_width : wide]

    mine = wsend[i]
    place_half(i, mine)
    sm.cross(0)
    sm.finish()
    out[...] = (hid[...] + sm.total()).astype(BF16)
    give_s.wait_recv()
    theirs = wrecv[...].astype(F32)
    place_half(1 - i, theirs)
    gains_out[...] = mine[:, wide:] + theirs[:, wide:]
    so.finish()
    dwo_out[...] = so.total()
    for one in (give_b, give_a, give_s):
        one.wait_send()
    for one in (give_g, give_u, give_d):
        one.wait()
    for s in (sm, so, sw):
        s.drain()


def finish_kernel(
    gu_own, od_own, gur, edr, out, tok, dq, dk, dv, dwo, gains,
    out_o, tok_o, dq_o, dk_o, dv_o, dwo_o, ga_o, gf_o, gr_o, eg_o, eu_o, ed_o,
):
    ff = eg_o.shape[2]
    eg_o[0] = gu_own[:, :ff] + gur[:, :ff].astype(F32)
    eu_o[0] = gu_own[:, ff:] + gur[:, ff:].astype(F32)
    ed_o[0] = od_own[...] + edr[...].astype(F32)

    @pl.when(pl.program_id(0) == 0)
    def _():
        for src, dst in ((out, out_o), (tok, tok_o), (dq, dq_o), (dk, dk_o), (dv, dv_o), (dwo, dwo_o)):
            dst[...] = src[...]
        experts = gr_o.shape[0]
        rows = turned(gains[...])
        ga_o[...] = rows[experts : experts + 1]
        gf_o[...] = rows[experts + 1 : experts + 2]
        gr_o[...] = rows[:experts]


def paired_body(
    tokens, cotangent, norm_attn, w_query, key_projection, value_projection, w_out, norm_ffn, w_router,
    expert_gate, expert_up, expert_down, routes, slot_order, doc_lengths, deal,
):
    rows, width = tokens.shape
    depth = w_query.shape[0]
    experts = 16
    q_width = w_query.shape[1] // 2
    k_width = key_projection.shape[1] // 2
    wide = q_width + 2 * k_width
    ff = expert_gate.shape[2]
    half = width // 2
    vm = pl.BlockSpec(memory_space=pltpu.VMEM)
    hb = pl.BlockSpec(memory_space=pl.ANY)
    sm = pl.BlockSpec(memory_space=pltpu.SMEM)

    def shaped(*dims, dtype=BF16):
        return jax.ShapeDtypeStruct(dims, dtype)

    def sems(n):
        return pltpu.SemaphoreType.DMA((n,))

    heads = q_width // HEAD_DIM
    groups = k_width // HEAD_DIM
    group_rows = 2 * rows

    def room(*dims, dtype=BF16):
        return pltpu.VMEM(dims, dtype)

    def gather_sems(n):
        return [sems(Gather.SENDS), sems(Gather.RECVS)] * n

    def scatter_sems(n):
        return [sems(Scatter.SENDS), sems(Scatter.RECVS)] * n

    res = pl.pallas_call(
        layer_kernel,
        name="layer",
        out_shape=(
            shaped(rows, width),
            shaped(rows, width),
            shaped(depth, 2 * q_width, dtype=F32),
            shaped(depth, 2 * k_width, dtype=F32),
            shaped(depth, 2 * k_width, dtype=F32),
            shaped(depth, width, dtype=F32),
            shaped(depth, NAR, dtype=F32),
            shaped(half, 2 * ff, dtype=F32),
            shaped(ff, half, dtype=F32),
            shaped(half, 2 * ff),
            shaped(ff, half),
            shaped(4, 4 * rows, width),
        ),
        in_specs=[vm] * 8 + [hb] * 4 + [vm, vm, sm, vm],
        out_specs=(vm,) * 7 + (hb,) * 5,
        scratch_shapes=[
            room(2 * 16 * depth, wide + NAR),
            room(16 * depth, width),
            room(2, rows, width),
            room(group_rows, q_width),
        ]
        + [room(groups, group_rows, 128)] * 4
        + [
            room(heads, group_rows, group_rows),
            room(group_rows, q_width),
            room(rows, width, dtype=F32),
            room(group_rows, group_rows, dtype=F32),
            room(group_rows, 128, dtype=F32),
            room(group_rows, 128, dtype=F32),
            room(rows, NAR, dtype=F32),
            room(rows, NAR, dtype=F32),
            room(rows, NAR, dtype=F32),
            room(rows, width),
            room(rows, width),
        ]
        + [room(16 * rows, width)] * 4
        + [room(8, rows, width), room(4, rows, width), room(2, rows, width), room(2, rows, width)]
        + [room(16, 8, rows, dtype=F32)] * 4
        + [
            room(width, 2 * ff),
            room(ff, width),
            room(4 * rows, 2 * ff, dtype=F32),
            room(4 * rows, width),
            room(group_rows, k_width, dtype=F32),
            room(group_rows, k_width, dtype=F32),
            room(2 * 16 * depth, NAR, dtype=F32),
            room(rows, width, dtype=F32),
            room(2, depth, wide + NAR, dtype=F32),
            room(depth, wide + NAR),
            room(depth, wide + NAR),
        ]
        + gather_sems(5)
        + scatter_sems(4)
        + [sems(16)] * 4
        + [sems(16), sems(16), sems(9), pltpu.SemaphoreType.DMA(()), pltpu.SemaphoreType.REGULAR((2,))],
        compiler_params=pltpu.CompilerParams(collective_id=1, has_side_effects=True, vmem_limit_bytes=64 << 20),
    )(
        tokens, w_query, key_projection, value_projection, w_router.T, norm_attn[None], norm_ffn[None], w_out,
        cotangent, expert_gate[0], expert_up[0], expert_down[0], routes.T, slot_order, doc_lengths,
        deal.reshape(1, -1),
    )
    out, tok_grad, dq, dk, dv, dwo, gains, gu_own, od_own, gur, edr, _ = res

    steps = 2

    def cut(*dims):
        return pl.BlockSpec((dims[0] // steps,) + dims[1:], lambda n: (n,) + (0,) * (len(dims) - 1))

    def cut_out(*dims):
        return pl.BlockSpec((1, dims[0] // steps) + dims[1:], lambda n: (0, n) + (0,) * (len(dims) - 1))

    def entire(*dims):
        return pl.BlockSpec(dims, lambda n: (0,) * len(dims))

    mats = ((half, ff), (half, ff), (ff, half))
    sums = ((half, 2 * ff), (ff, half))
    rest = (out, tok_grad, dq, dk, dv, dwo, gains)
    res = pl.pallas_call(
        finish_kernel,
        name="finish",
        grid=(steps,),
        out_shape=tuple(jax.ShapeDtypeStruct(r.shape, r.dtype) for r in rest[:6])
        + (shaped(1, depth, dtype=F32), shaped(1, depth, dtype=F32), shaped(experts, depth, dtype=F32))
        + tuple(shaped(1, *m, dtype=F32) for m in mats),
        in_specs=[cut(*m) for m in sums] * 2 + [entire(*r.shape) for r in rest],
        out_specs=tuple(entire(*r.shape) for r in rest[:6])
        + (entire(1, depth), entire(1, depth), entire(experts, depth))
        + tuple(cut_out(*m) for m in mats),
        compiler_params=pltpu.CompilerParams(vmem_limit_bytes=62 << 20),
    )(gu_own, od_own, gur, edr, *rest)
    out, tok_grad, dq, dk, dv, dwo, g_attn, g_ffn, g_router, eg, eu, ed = res
    return (
        out, tok_grad, g_attn.reshape(-1), dq, dk, dv, dwo, g_ffn.reshape(-1), g_router.T, eg, eu, ed,
    )


def general_body(
    tokens,
    cotangent,
    norm_attn,
    w_query,
    key_projection,
    value_projection,
    w_out,
    norm_ffn,
    w_router,
    expert_gate,
    expert_up,
    expert_down,
    routes,
    slot_order,
    doc_lengths,
    deal,
):
    gain_attn, full_query, gathered_key, gathered_value, full_out, gain_ffn, full_router = (
        lax.all_gather(norm_attn, ("dp", "expert"), axis=0, tiled=True),
        lax.all_gather(w_query, ("dp", "expert"), axis=0, tiled=True),
        lax.all_gather(key_projection, ("dp", "expert"), axis=0, tiled=True),
        lax.all_gather(value_projection, ("dp", "expert"), axis=0, tiled=True),
        lax.all_gather(w_out, ("dp", "expert"), axis=0, tiled=True),
        lax.all_gather(norm_ffn, ("dp", "expert"), axis=0, tiled=True),
        lax.all_gather(w_router, ("dp", "expert"), axis=0, tiled=True),
    )
    full_gate, full_up, full_down = (
        lax.all_gather(expert_gate[0], "dp", axis=0, tiled=True),
        lax.all_gather(expert_up[0], "dp", axis=0, tiled=True),
        lax.all_gather(expert_down[0], "dp", axis=1, tiled=True),
    )
    count_of_rows, model_width = tokens.shape
    top_count = routes.shape[1]
    experts = full_router.shape[1]
    owners = lax.axis_size("expert")
    capacity = 9 * count_of_rows * top_count // (8 * experts)
    head_count = full_query.shape[1] // HEAD_DIM
    groups = gathered_key.shape[1] // HEAD_DIM
    head_ratio = head_count // groups
    scale_attn = gain_attn.astype(jnp.float32)
    scale_ffn = gain_ffn.astype(jnp.float32)
    score_scale = HEAD_DIM ** (-0.5)
    group_places = deal[:, 0, :].reshape(-1)
    group_docs, group_offsets = doc_layout(doc_lengths[0], group_places)
    shard_start = lax.axis_index("dp") * count_of_rows
    places = lax.dynamic_slice_in_dim(group_places, shard_start, count_of_rows)
    doc_ids = lax.dynamic_slice_in_dim(group_docs, shard_start, count_of_rows)
    offsets = lax.dynamic_slice_in_dim(group_offsets, shard_start, count_of_rows)
    cosine_lookup, sine_lookup = rope_tables(offsets, HEAD_DIM)
    inputs = tokens.astype(jnp.float32)
    inverse_one = lax.rsqrt(jnp.mean(inputs * inputs, axis=1, keepdims=True) + NORM_EPS)
    normed_one = inputs * inverse_one
    attention_input = (normed_one * scale_attn).astype(jnp.bfloat16)
    query_rows = apply_rotation(
        dot_plain(attention_input, full_query).reshape(count_of_rows, head_count, HEAD_DIM),
        cosine_lookup,
        sine_lookup,
    ).astype(jnp.bfloat16)
    key_matrix_rows = apply_rotation(
        dot_plain(attention_input, gathered_key).reshape(count_of_rows, groups, HEAD_DIM),
        cosine_lookup,
        sine_lookup,
    ).astype(jnp.bfloat16)
    value_matrix_rows = dot_plain(attention_input, gathered_value).astype(jnp.bfloat16)
    all_keys, all_values = (
        lax.all_gather(key_matrix_rows.reshape(count_of_rows, -1), "dp", axis=0, tiled=True),
        lax.all_gather(value_matrix_rows, "dp", axis=0, tiled=True),
    )
    group_rows = all_keys.shape[0]
    key_span = math.gcd(group_rows, 512)
    span_count = group_rows // key_span
    key_spans = (
        all_keys.reshape(span_count, key_span, groups, HEAD_DIM),
        all_values.reshape(span_count, key_span, groups, HEAD_DIM),
        group_places.reshape(span_count, key_span),
        group_docs.reshape(span_count, key_span),
    )
    grouped_q = query_rows.reshape(count_of_rows, groups, head_ratio, HEAD_DIM)

    def span_scores(key_block, key_place, key_doc):
        visible = (doc_ids[:, None] == key_doc[None, :]) & (places[:, None] >= key_place[None, :])
        scores = (
            jnp.einsum("qgrd,kgd->grqk", grouped_q, key_block, preferred_element_type=jnp.float32)
            * score_scale
        )
        return jnp.where(visible[None, None], scores, MASK_FILL)

    def extent(carry, operands):
        run_max, run_sum = carry
        key_block, value_block, key_place, key_doc = operands
        scores = span_scores(key_block, key_place, key_doc)
        new_max = jnp.maximum(run_max, jnp.max(scores, axis=-1, keepdims=True))
        run_sum = run_sum * jnp.exp(run_max - new_max) + jnp.sum(
            jnp.exp(scores - new_max), axis=-1, keepdims=True
        )
        return ((new_max, run_sum), None)

    stat_shape = (groups, head_ratio, count_of_rows, 1)
    (row_max, row_sum), _ = lax.scan(
        extent,
        (jnp.full(stat_shape, MASK_FILL, jnp.float32), jnp.zeros(stat_shape, jnp.float32)),
        key_spans,
    )
    log_total = row_max + jnp.log(row_sum)

    def weigh_values(running, operands):
        key_block, value_block, key_place, key_doc = operands
        weights = jnp.exp(span_scores(key_block, key_place, key_doc) - log_total).astype(
            jnp.bfloat16
        )
        return (
            running
            + jnp.einsum(
                "grqk,kgd->qgrd", weights, value_block, preferred_element_type=jnp.float32
            ),
            None,
        )

    attended, _ = lax.scan(
        weigh_values,
        jnp.zeros((count_of_rows, groups, head_ratio, HEAD_DIM), jnp.float32),
        key_spans,
    )
    attended = attended.reshape(count_of_rows, head_count * HEAD_DIM).astype(jnp.bfloat16)
    hidden_state = inputs + dot_plain(attended, full_out)
    inverse_two = lax.rsqrt(jnp.mean(hidden_state * hidden_state, axis=1, keepdims=True) + NORM_EPS)
    normed_two = hidden_state * inverse_two
    ffn_in = (normed_two * scale_ffn).astype(jnp.bfloat16)
    logits = dot_plain(ffn_in, full_router)
    route_hits = (routes[:, :, None] == jnp.arange(experts, dtype=jnp.int32)[None, None, :]).astype(
        jnp.float32
    )
    chosen = jnp.sum(route_hits * logits[:, None, :], axis=-1)
    gate_values = jax.nn.softmax(chosen, axis=-1)
    pair_slot, slot_token = assign_slots(routes, slot_order[0], experts, capacity)
    padded_in = jnp.concatenate([ffn_in, jnp.zeros((1, model_width), jnp.bfloat16)], axis=0)
    outgoing = padded_in[slot_token].reshape(owners, capacity, model_width)
    arrived = lax.all_to_all(outgoing, "expert", split_axis=0, concat_axis=0, tiled=True)
    flat_rows = arrived.reshape(-1, model_width)
    gate_pre = dot_plain(flat_rows, full_gate)
    up_pre = dot_plain(flat_rows, full_up)
    hidden = (jax.nn.silu(gate_pre) * up_pre).astype(jnp.bfloat16)
    result = dot_plain(hidden, full_down).astype(jnp.bfloat16).reshape(arrived.shape)
    sent_back = lax.all_to_all(result, "expert", split_axis=0, concat_axis=0, tiled=True)
    exchanged = (
        sent_back,
        arrived,
        gate_pre.reshape(arrived.shape[0], arrived.shape[1], -1),
        up_pre.reshape(arrived.shape[0], arrived.shape[1], -1),
    )
    returned = exchanged[0]
    expert_rows = exchanged[1].reshape(-1, model_width)
    gate_pre = exchanged[2].reshape(expert_rows.shape[0], -1)
    up_pre = exchanged[3].reshape(expert_rows.shape[0], -1)
    out_grad = cotangent.astype(jnp.float32)
    padded_back = jnp.concatenate(
        [returned.reshape(-1, model_width), jnp.zeros((1, model_width), jnp.bfloat16)], axis=0
    )
    slot_grid = pair_slot.reshape(count_of_rows, top_count)
    mixture = jnp.zeros((count_of_rows, model_width), jnp.float32)
    gate_parts = []
    for column in range(top_count):
        picked = padded_back[slot_grid[:, column]].astype(jnp.float32)
        mixture = mixture + gate_values[:, column : column + 1] * picked
        gate_parts.append(jnp.sum(out_grad * picked, axis=1))
    output = (hidden_state + mixture).astype(jnp.bfloat16)
    gate_grad = jnp.stack(gate_parts, axis=1)
    slot_gate = (
        jnp.zeros((experts * capacity + 1,), jnp.float32)
        .at[pair_slot]
        .set(gate_values.reshape(-1))[: experts * capacity]
    )
    padded_grad = jnp.concatenate([out_grad, jnp.zeros((1, model_width), jnp.float32)], axis=0)
    slot_grad = (
        (slot_gate[:, None] * padded_grad[slot_token])
        .astype(jnp.bfloat16)
        .reshape(owners, capacity, model_width)
    )
    arrived_grad = lax.all_to_all(
        slot_grad, "expert", split_axis=0, concat_axis=0, tiled=True
    ).reshape(-1, model_width)
    sigmoid_gate = jax.nn.sigmoid(gate_pre)
    silu_gate = gate_pre * sigmoid_gate
    hidden = (silu_gate * up_pre).astype(jnp.bfloat16)
    hidden_grad = dot_last(arrived_grad, full_down)
    gate_pre_grad = (
        hidden_grad * up_pre * sigmoid_gate * (1.0 + gate_pre * (1.0 - sigmoid_gate))
    ).astype(jnp.bfloat16)
    up_pre_grad = (hidden_grad * silu_gate).astype(jnp.bfloat16)
    down_weight_grad = dot_first(hidden, arrived_grad)
    gate_weight_grad = dot_first(expert_rows, gate_pre_grad)
    up_weight_grad = dot_first(expert_rows, up_pre_grad)
    row_grad = (dot_last(gate_pre_grad, full_gate) + dot_last(up_pre_grad, full_up)).astype(
        jnp.bfloat16
    )
    token_rows_grad = lax.all_to_all(
        row_grad.reshape(owners, capacity, model_width),
        "expert",
        split_axis=0,
        concat_axis=0,
        tiled=True,
    )
    gate_summed, up_summed, down_summed = (
        lax.psum_scatter(
            gate_weight_grad.astype(jnp.bfloat16), "dp", scatter_dimension=0, tiled=True
        ).astype(jnp.float32),
        lax.psum_scatter(
            up_weight_grad.astype(jnp.bfloat16), "dp", scatter_dimension=0, tiled=True
        ).astype(jnp.float32),
        lax.psum_scatter(
            down_weight_grad.astype(jnp.bfloat16), "dp", scatter_dimension=1, tiled=True
        ).astype(jnp.float32),
    )
    dispatch_grad = jax.ops.segment_sum(
        token_rows_grad.reshape(-1, model_width).astype(jnp.float32),
        slot_token,
        num_segments=count_of_rows + 1,
    )[:count_of_rows]
    chosen_grad = gate_values * (
        gate_grad - jnp.sum(gate_values * gate_grad, axis=1, keepdims=True)
    )
    logit_grad = jnp.sum(route_hits * chosen_grad[:, :, None], axis=1).astype(jnp.bfloat16)
    router_grad = dot_first(ffn_in, logit_grad)
    ffn_grad = dispatch_grad + dot_last(logit_grad, full_router)
    ffn_gain_grad = jnp.sum(ffn_grad * normed_two, axis=0)
    scaled_two = ffn_grad * scale_ffn
    state_grad = out_grad + inverse_two * (
        scaled_two - normed_two * jnp.mean(scaled_two * normed_two, axis=1, keepdims=True)
    )
    branch_grad = state_grad.astype(jnp.bfloat16)
    out_weight_grad = dot_first(attended, branch_grad)
    attended_grad = (
        dot_last(branch_grad, full_out)
        .astype(jnp.bfloat16)
        .reshape(count_of_rows, groups, head_ratio, HEAD_DIM)
    )

    def spread_sum(running, operands):
        key_block, value_block, key_place, key_doc = operands
        probs = jnp.exp(span_scores(key_block, key_place, key_doc) - log_total)
        prob_grad = jnp.einsum(
            "qgrd,kgd->grqk", attended_grad, value_block, preferred_element_type=jnp.float32
        )
        return (running + jnp.sum(probs * prob_grad, axis=-1, keepdims=True), None)

    score_shift, _ = lax.scan(spread_sum, jnp.zeros(stat_shape, jnp.float32), key_spans)

    def back_span(running, operands):
        key_block, value_block, key_place, key_doc = operands
        probs = jnp.exp(span_scores(key_block, key_place, key_doc) - log_total)
        prob_grad = jnp.einsum(
            "qgrd,kgd->grqk", attended_grad, value_block, preferred_element_type=jnp.float32
        )
        score_grad = (probs * (prob_grad - score_shift)).astype(jnp.bfloat16)
        running = running + jnp.einsum(
            "grqk,kgd->qgrd", score_grad, key_block, preferred_element_type=jnp.float32
        )
        key_part = (
            jnp.einsum("grqk,qgrd->kgd", score_grad, grouped_q, preferred_element_type=jnp.float32)
            * score_scale
        )
        value_part = jnp.einsum(
            "grqk,qgrd->kgd",
            probs.astype(jnp.bfloat16),
            attended_grad,
            preferred_element_type=jnp.float32,
        )
        return (running, (key_part.reshape(key_span, -1), value_part.reshape(key_span, -1)))

    query_sum, (key_parts, value_parts) = lax.scan(
        back_span, jnp.zeros((count_of_rows, groups, head_ratio, HEAD_DIM), jnp.float32), key_spans
    )
    key_grad, value_sum = (
        lax.psum_scatter(
            key_parts.reshape(group_rows, -1).astype(jnp.bfloat16),
            "dp",
            scatter_dimension=0,
            tiled=True,
        ).astype(jnp.float32),
        lax.psum_scatter(
            value_parts.reshape(group_rows, -1).astype(jnp.bfloat16),
            "dp",
            scatter_dimension=0,
            tiled=True,
        ).astype(jnp.float32),
    )
    query_grad = query_sum * score_scale
    query_lin_grad = unrotate(
        query_grad.reshape(count_of_rows, head_count, HEAD_DIM), cosine_lookup, sine_lookup
    )
    query_lin_grad = query_lin_grad.reshape(count_of_rows, -1).astype(jnp.bfloat16)
    key_lin_grad = (
        unrotate(key_grad.reshape(count_of_rows, groups, HEAD_DIM), cosine_lookup, sine_lookup)
        .reshape(count_of_rows, -1)
        .astype(jnp.bfloat16)
    )
    value_lin_grad = value_sum.astype(jnp.bfloat16)
    query_weight_grad = dot_first(attention_input, query_lin_grad)
    key_weight_grad = dot_first(attention_input, key_lin_grad)
    value_weight_grad = dot_first(attention_input, value_lin_grad)
    attn_grad = (
        dot_last(query_lin_grad, full_query)
        + dot_last(key_lin_grad, gathered_key)
        + dot_last(value_lin_grad, gathered_value)
    )
    attn_gain_grad = jnp.sum(attn_grad * normed_one, axis=0)
    scaled_one = attn_grad * scale_attn
    tokens_grad = (
        state_grad
        + inverse_one
        * (scaled_one - normed_one * jnp.mean(scaled_one * normed_one, axis=1, keepdims=True))
    ).astype(jnp.bfloat16)
    summed = (
        lax.psum_scatter(attn_gain_grad, ("dp", "expert"), scatter_dimension=0, tiled=True),
        lax.psum_scatter(query_weight_grad, ("dp", "expert"), scatter_dimension=0, tiled=True),
        lax.psum_scatter(key_weight_grad, ("dp", "expert"), scatter_dimension=0, tiled=True),
        lax.psum_scatter(value_weight_grad, ("dp", "expert"), scatter_dimension=0, tiled=True),
        lax.psum_scatter(out_weight_grad, ("dp", "expert"), scatter_dimension=0, tiled=True),
        lax.psum_scatter(ffn_gain_grad, ("dp", "expert"), scatter_dimension=0, tiled=True),
        lax.psum_scatter(router_grad, ("dp", "expert"), scatter_dimension=0, tiled=True),
    )
    return (
        output,
        tokens_grad,
        summed[0],
        summed[1],
        summed[2],
        summed[3],
        summed[4],
        summed[5],
        summed[6],
        gate_summed[None],
        up_summed[None],
        down_summed[None],
    )


def solution(mesh):
    in_specs = (
        P(("dp", "expert"), None),
        P(("dp", "expert"), None),
        P(("dp", "expert")),
        P(("dp", "expert"), None),
        P(("dp", "expert"), None),
        P(("dp", "expert"), None),
        P(("dp", "expert"), None),
        P(("dp", "expert")),
        P(("dp", "expert"), None),
        P("expert", "dp", None),
        P("expert", "dp", None),
        P("expert", None, "dp"),
        P(("dp", "expert"), None),
        P(("dp", "expert"), None),
        P("expert", None),
        P(None, "expert", None),
    )
    out_specs = (
        P(("dp", "expert"), None),
        P(("dp", "expert"), None),
        P(("dp", "expert")),
        P(("dp", "expert"), None),
        P(("dp", "expert"), None),
        P(("dp", "expert"), None),
        P(("dp", "expert"), None),
        P(("dp", "expert")),
        P(("dp", "expert"), None),
        P("expert", "dp", None),
        P("expert", "dp", None),
        P("expert", None, "dp"),
    )
    fast = mesh.shape["dp"] == 2 and mesh.shape["expert"] == 16
    body = paired_body if fast else general_body
    return jax.shard_map(body, mesh=mesh, in_specs=in_specs, out_specs=out_specs, check_vma=False)
```

```python
import functools
import math

import jax
import jax.numpy as jnp
from jax import lax
from jax.experimental import pallas as pl
from jax.experimental.pallas import tpu as pltpu
from jax.sharding import PartitionSpec as P

HEAD_DIM = 64


NORM_EPS = 1e-05
MASK_FILL = -1e30
ROPE_BASE = 10000.0


def dot_plain(left_side, right_side):
    return jnp.dot(left_side, right_side, preferred_element_type=jnp.float32)


def dot_last(left_side, right_side):
    return lax.dot_general(
        left_side, right_side, (((1,), (1,)), ((), ())), preferred_element_type=jnp.float32
    )


def dot_first(left_side, right_side):
    return lax.dot_general(
        left_side, right_side, (((0,), (0,)), ((), ())), preferred_element_type=jnp.float32
    )


def doc_layout(lengths, places):
    doc_ends = jnp.cumsum(lengths)
    doc_starts = doc_ends - lengths
    doc_ids = jnp.sum((places[:, None] >= doc_ends[None, :]).astype(jnp.int32), axis=1)
    member = doc_ids[:, None] == jnp.arange(lengths.shape[0], dtype=jnp.int32)[None, :]
    offsets = places - jnp.sum(jnp.where(member, doc_starts[None, :], 0), axis=1)
    return (doc_ids, offsets)


def rope_tables(offsets, head_size):
    half_size = head_size // 2
    frequency = ROPE_BASE ** (-2.0 * jnp.arange(half_size, dtype=jnp.float32) / head_size)
    angles = offsets.astype(jnp.float32)[:, None] * frequency[None, :]
    return (jnp.cos(angles), jnp.sin(angles))


def apply_rotation(values, cosine_lookup, sine_lookup):
    half_size = values.shape[-1] // 2
    first_half = values[..., :half_size]
    second = values[..., half_size:]
    cos_rows = cosine_lookup[:, None, :]
    sin_rows = sine_lookup[:, None, :]
    return jnp.concatenate(
        [first_half * cos_rows - second * sin_rows, second * cos_rows + first_half * sin_rows],
        axis=-1,
    )


def unrotate(gradient, cosine_lookup, sine_lookup):
    half_size = gradient.shape[-1] // 2
    first_half = gradient[..., :half_size]
    second = gradient[..., half_size:]
    cos_rows = cosine_lookup[:, None, :]
    sin_rows = sine_lookup[:, None, :]
    return jnp.concatenate(
        [first_half * cos_rows + second * sin_rows, second * cos_rows - first_half * sin_rows],
        axis=-1,
    )


def assign_slots(routes, take_order, experts, capacity):
    count_of_rows, top_count = routes.shape
    flat_routes = routes.reshape(-1)
    chosen = flat_routes[take_order]
    expert_hits = (chosen[:, None] == jnp.arange(experts, dtype=jnp.int32)[None, :]).astype(
        jnp.int32
    )
    slot_rank = jnp.sum(jnp.cumsum(expert_hits, axis=0) * expert_hits, axis=1) - 1
    slot_index = jnp.where(slot_rank < capacity, chosen * capacity + slot_rank, experts * capacity)
    pair_slot = jnp.zeros((flat_routes.shape[0],), jnp.int32).at[take_order].set(slot_index)
    slot_token = (
        jnp.full((experts * capacity + 1,), count_of_rows, jnp.int32)
        .at[slot_index]
        .set(take_order // top_count)
    )
    return (pair_slot, slot_token[: experts * capacity])


MESH = pl.DeviceIdType.MESH
BF16 = jnp.bfloat16
F32 = jnp.float32
NAR = 128


def remote(src, dst, send_sem, recv_sem, device):
    return pltpu.make_async_remote_copy(
        src_ref=src,
        dst_ref=dst,
        send_sem=send_sem,
        recv_sem=recv_sem,
        device_id=device,
        device_id_type=MESH,
    )


class Place:
    def __init__(self):
        self.i = lax.axis_index("dp")
        self.e = lax.axis_index("expert")
        self.a = self.e // 4
        self.bc = self.e % 4
        self.y = self.bc // 2
        self.c = self.bc % 2

    def over_x(self):
        return (1 - self.i, self.e)

    def over_y(self):
        return (self.i, self.e + 2 - 4 * self.y)

    def over_core(self):
        return (self.i, self.e + 1 - 2 * self.c)

    def order(self, k):
        turn = (1 - 2 * k) * (1 - k // 2)
        inner = self.inner()
        half = self.a // 2
        step = k + inner * turn
        return step + half * (3 - 2 * step)

    def inner(self):
        return (self.a * (3 - self.a)) // 2

    def partner(self):
        return self.a + 1 - 2 * (self.a % 2)

    def barrier(self, whole_plane=False):
        sem = pltpu.get_barrier_semaphore()
        if whole_plane:
            peers = [(self.i, (self.e + shift) % 16) for shift in range(1, 16)]
        else:
            peers = [self.over_y(), self.over_core()]
            for shift in range(1, 4):
                peers.append((self.i, ((self.a + shift) % 4) * 4 + self.bc))
        peers.append(self.over_x())
        for peer in peers:
            pl.semaphore_signal(sem, inc=1, device_id=peer, device_id_type=MESH)
        pl.semaphore_wait(sem, len(peers))


class Gather:
    SENDS = 20
    RECVS = 16

    def __init__(self, place, view, sends, recvs, lean=False):
        self.p, self.view, self.sends, self.recvs = place, view, sends, recvs
        self.lean = lean

    def copy(self, block, slot, device):
        ref = self.view(block)
        return remote(ref, ref, self.sends.at[slot], self.recvs.at[block], device)

    def right(self, a1):
        return self.copy(a1 * 4 + self.p.bc, a1, (self.p.i, self.p.e + 4))

    def left(self, a1):
        return self.copy(a1 * 4 + self.p.bc, 4 + a1, (self.p.i, self.p.e - 4))

    def across(self, a1):
        return self.copy(a1 * 4 + self.p.bc, 8 + a1, self.p.over_y())

    def core(self, a1, y1):
        return self.copy(a1 * 4 + y1 * 2 + self.p.c, 12 + a1 * 2 + y1, self.p.over_core())

    def landed(self, block):
        self.copy(block, 0, self.p.over_core()).wait_recv()

    def handed(self):
        p = self.p
        device = (p.i, p.partner() * 4 + p.bc)
        return self.copy(p.a * 4 + (1 - p.y) * 2 + p.c, 8 + p.partner(), device)

    def hand(self):
        self.handed().start()

    def begin(self):
        p = self.p
        self.across(p.a).start()

        @pl.when(p.a < 3)
        def _():
            self.right(p.a).start()

        @pl.when(p.a > 0)
        def _():
            self.left(p.a).start()

        self.core(p.a, p.y).start()

    def phase(self, s):
        p = self.p
        inner = p.inner()
        if s == 1:
            self.along(1)

        @pl.when(inner == 1)
        def _():
            if s < 3:
                self.along(s + 1)

        if s > 1:

            @pl.when(inner == 0)
            def _():
                self.along(s)

    def along(self, k):
        p = self.p
        a1 = p.order(k)
        self.landed(a1 * 4 + p.bc)

        @pl.when((a1 < p.a) & (p.a < 3))
        def _():
            self.right(a1).start()

        @pl.when((a1 > p.a) & (p.a > 0))
        def _():
            self.left(a1).start()

        if k != 1 or not self.lean:
            self.across(a1).start()
        self.core(a1, p.y).start()

    def cross(self, k):
        p = self.p
        a1 = p.order(k)
        self.landed(a1 * 4 + (1 - p.y) * 2 + p.c)
        self.core(a1, 1 - p.y).start()

    def join(self, k):
        p = self.p
        a1 = p.order(k)
        self.landed(a1 * 4 + (1 - p.c))
        self.landed(a1 * 4 + 2 + (1 - p.c))

    def sent(self, k):
        p = self.p
        a1 = p.order(k)

        @pl.when((a1 <= p.a) & (p.a < 3))
        def _():
            self.right(a1).wait_send()

        @pl.when((a1 >= p.a) & (p.a > 0))
        def _():
            self.left(a1).wait_send()

        if k == 0 and self.lean:
            self.handed().wait_send()
        if k != 1 or not self.lean:
            self.across(a1).wait_send()
        self.core(a1, 0).wait_send()
        self.core(a1, 1).wait_send()

    def drain(self):
        for k in range(4):
            self.sent(k)


class Scatter:
    SENDS = 16
    RECVS = 17

    def __init__(self, place, part, core_in, y_in, a_in, pass_in, sends, recvs, lean=False):
        self.p, self.part, self.lean = place, part, lean
        self.core_in, self.y_in, self.a_in, self.pass_in = core_in, y_in, a_in, pass_in
        self.sends, self.recvs = sends, recvs

    def to_core(self, a1, y1):
        p = self.p
        slot = a1 * 2 + y1
        return remote(
            self.part(a1, y1 * 2 + 1 - p.c),
            self.core_in(a1, y1),
            self.sends.at[slot],
            self.recvs.at[slot],
            p.over_core(),
        )

    def to_y(self, a1):
        p = self.p
        return remote(
            self.part(a1, (1 - p.y) * 2 + p.c),
            self.y_in(a1),
            self.sends.at[8 + a1],
            self.recvs.at[8 + a1],
            p.over_y(),
        )

    def to_far(self, a1):
        p = self.p
        return remote(
            self.part(a1, p.bc),
            self.a_in(2),
            self.sends.at[12 + a1],
            self.recvs.at[14],
            (p.i, a1 * 4 + p.bc),
        )

    def to_inner(self, a1):
        p = self.p
        return remote(
            self.part(a1, p.bc),
            self.pass_in(a1 % 2),
            self.sends.at[12 + a1],
            self.recvs.at[15 + a1 % 2],
            (p.i, p.partner() * 4 + p.bc),
        )

    def to_partner(self, other):
        p = self.p
        a1 = p.partner()
        side = 1 - p.y if other else p.y
        return remote(
            self.part(a1, side * 2 + p.c),
            self.y_in(p.a) if other else self.a_in(1),
            self.sends.at[(8 if other else 12) + a1],
            self.recvs.at[8 + p.a if other else 13],
            (p.i, a1 * 4 + p.bc),
        )

    def from_partner(self, other):
        p = self.p
        spot = self.y_in(p.partner()) if other else self.a_in(1)
        slot = 8 + p.partner() if other else 13
        return remote(spot, spot, self.sends.at[0], self.recvs.at[slot], p.over_core())

    def start(self, k):
        a1 = self.p.order(k)
        self.to_core(a1, 0).start()
        self.to_core(a1, 1).start()

    def add(self, ref, other):
        ref[...] = (ref[...].astype(F32) + other[...].astype(F32)).astype(ref.dtype)

    def core(self, k):
        p = self.p
        a1 = p.order(k)
        for y1 in range(2):
            self.to_core(a1, y1).wait_recv()
        self.add(self.part(a1, (1 - p.y) * 2 + p.c), self.core_in(a1, 1 - p.y))
        if k > 1 or not self.lean:
            self.to_y(a1).start()
        elif k == 1:
            self.to_partner(True).start()
        self.add(self.part(a1, p.bc), self.core_in(a1, p.y))
        if k == 1 and self.lean:
            self.to_partner(False).start()

    def meet(self):
        p = self.p
        self.from_partner(True).wait_recv()
        self.add(self.part(p.a, (1 - p.y) * 2 + p.c), self.y_in(p.partner()))
        self.to_y(p.a).start()

    def cross(self, k):
        p = self.p
        a1 = p.order(k)
        self.to_y(a1).wait_recv()
        self.add(self.part(a1, p.bc), self.y_in(a1))
        if k == 1:
            self.to_partner(False).start()
        if k > 1:

            @pl.when(p.inner() == 0)
            def _():
                self.to_inner(a1).start()

    def relay(self, k):
        p = self.p
        a1 = p.order(k)

        @pl.when(p.inner() == 1)
        def _():
            self.to_inner(a1).wait_recv()
            self.add(self.part(a1, p.bc), self.pass_in(a1 % 2))
            self.to_far(a1).start()

    def finish(self):
        self.from_partner(False).wait_recv()
        self.to_far(self.p.a).wait_recv()

    def total(self):
        own = self.part(self.p.a, self.p.bc)[...].astype(F32)
        return own + self.a_in(1)[...].astype(F32) + self.a_in(2)[...].astype(F32)

    def drain(self):
        p = self.p
        for k in range(4):
            a1 = p.order(k)
            self.to_core(a1, 0).wait_send()
            self.to_core(a1, 1).wait_send()
            if k == 1:
                self.to_partner(False).wait_send()
            if k == 1 and self.lean:
                self.to_partner(True).wait_send()
            else:
                self.to_y(a1).wait_send()
            if k > 1:
                self.to_far(a1).wait_send()


class Exchange:
    def __init__(self, place, source, target, sends, recvs):
        self.p, self.source, self.target, self.sends, self.recvs = place, source, target, sends, recvs

    def copy(self, there):
        p = self.p
        return remote(
            self.source.at[there], self.target.at[p.e], self.sends.at[there], self.recvs.at[p.e], (p.i, there)
        )

    def give(self, there):
        @pl.when(there != self.p.e)
        def _():
            self.copy(there).start()

        @pl.when(there == self.p.e)
        def _():
            self.target[there] = self.source[there]

    def take(self, there):
        p = self.p

        @pl.when(there != p.e)
        def _():
            remote(
                self.target.at[there], self.target.at[there], self.sends.at[there], self.recvs.at[there], (p.i, there)
            ).wait_recv()

    def drain(self):
        @pl.loop(0, 16)
        def _(there):
            @pl.when(there != self.p.e)
            def _():
                self.copy(there).wait_send()


def lane_iota(shape):
    return lax.broadcasted_iota(jnp.int32, shape, len(shape) - 1)


def swap_halves(values):
    lane = lane_iota(values.shape) % HEAD_DIM
    half = HEAD_DIM // 2
    return jnp.where(
        lane < half,
        pltpu.roll(values, values.shape[-1] - half, 1),
        pltpu.roll(values, half, 1),
    )


def split_heads(tile):
    low = lane_iota(tile.shape) < HEAD_DIM
    turned = pltpu.roll(tile, HEAD_DIM, 1)
    zero = jnp.zeros_like(tile)
    return (
        (jnp.where(low, tile, zero), jnp.where(low, zero, turned)),
        (jnp.where(low, turned, zero), jnp.where(low, zero, tile)),
    )


def inverse_rms(values):
    return lax.rsqrt(jnp.mean(values * values, axis=1, keepdims=True) + NORM_EPS)


def gain_rows(narrow, experts):
    shape = (16, narrow.shape[1])
    row = lax.broadcasted_iota(jnp.int32, shape, 0)
    pick = jnp.where(lane_iota(shape) == row + experts, 1.0, 0.0).astype(BF16)
    return dot_last(pick, narrow)


def column_of(row):
    n = row.shape[1]
    shape = (n, n)
    same = lane_iota(shape) == lax.broadcasted_iota(jnp.int32, shape, 0)
    return jnp.sum(jnp.where(same, row, 0.0), axis=1, keepdims=True)


def row_of(column):
    n = column.shape[0]
    shape = (n, n)
    same = lane_iota(shape) == lax.broadcasted_iota(jnp.int32, shape, 0)
    return jnp.sum(jnp.where(same, column, 0.0), axis=0, keepdims=True)


def documents(places, ends):
    doc = jnp.zeros_like(places)
    start = jnp.zeros_like(places)
    for end in ends:
        past = places >= end
        doc = doc + jnp.where(past, 1.0, 0.0)
        start = jnp.where(past, end, start)
    return doc, start


def turned(values):
    m, n = values.shape
    if n < NAR:
        values = jnp.concatenate([values, jnp.zeros((m, NAR - n), F32)], axis=1)
    if m < NAR:
        values = jnp.concatenate([values, jnp.zeros((NAR - m, NAR), F32)], axis=0)
    return jnp.transpose(values)[:n, :m]


def kept_pairs(routes_by_rank, take_order, experts, capacity):
    top_count, rows = routes_by_rank.shape
    routes = turned(routes_by_rank.astype(F32)).astype(jnp.int32)
    lane = lane_iota((rows, NAR))
    token = lax.broadcasted_iota(jnp.int32, (rows, 1), 0)
    number = lane_iota((rows, take_order.shape[1])).astype(F32)
    hit = jnp.zeros((rows, NAR), jnp.bool_)
    taken = jnp.zeros((rows, NAR), F32)
    for j in range(top_count):
        at = jnp.sum(jnp.where(take_order == token * top_count + j, number, 0.0), axis=1, keepdims=True)
        mine = lane == routes[:, j : j + 1]
        hit = hit | mine
        taken = jnp.where(mine, at, taken)
    taken = jnp.where(hit, taken, 1e9)
    across = jnp.transpose(taken)
    rank = jnp.zeros((rows, NAR), F32)
    for name in range(experts):
        before = jnp.where(across[name : name + 1, :] < taken[:, name : name + 1], 1.0, 0.0)
        rank = jnp.where(lane == name, jnp.sum(before, axis=1, keepdims=True), rank)
    one, zero = jnp.ones((rows, NAR), F32), jnp.zeros((rows, NAR), F32)
    hits = jnp.where(hit, one, zero)
    return hits, jnp.where(rank < capacity, hits, zero)


def layer_kernel(
    tok, wq, wk, wv, wr, na, nf, wo, cot, eg, eu, ed, routes, slots, lengths, places,
    out, tok_grad, dq_out, dk_out, dv_out, dwo_out, gains_out, gu_own, od_own, gur, edr, mixp,
    w_all, wo_all, x_all, q, klo, khi, vlo, vhi, pr, att, hid, vis, cs, sn, hit, kept, gates, opart, orecv,
    f_all, part, og, hgu, core_in, y_in, a_in, pass_in, gate_out, gate_in, grad_out, grad_in, wgu, wd, h12, mix,
    dk, dv, small, state, wsend, wgive, wrecv,
    ga_s, ga_r, gb_s, gb_r, gw_s, gw_r, gc_s, gc_r, gf_s, gf_r, sc_s, sc_r, sm_s, sm_r, so_s, so_r, sw_s, sw_r,
    gs_s, gs_r, gg_s, gg_r, xs, xr, loc, mix_sem, ready,
):
    p = Place()
    i, e = p.i, p.e
    rows, width = tok.shape
    depth = wo.shape[0]
    plane = 16 * depth
    group = 4 * rows
    group_rows_count = 2 * rows
    half = width // 2
    ff = wd.shape[0]
    q_width = q.shape[1]
    k_width = dk.shape[1]
    experts = 16
    wide = q_width + 2 * k_width
    capacity = 9 * rows * routes.shape[0] // (8 * experts)
    ratio = q_width // k_width
    scale = HEAD_DIM**-0.5
    heads = q_width // HEAD_DIM
    near = [p.order(k) for k in range(4)]

    def w_row(ip, block):
        return pl.ds(pl.multiple_of(ip * plane + block * depth, 16), depth)

    def row_block(ip):
        return pl.ds(pl.multiple_of(ip * rows, rows), rows)

    def half_lanes(ip, n):
        return pl.ds(pl.multiple_of(ip * n, 128), n)

    def half_rows(ip):
        return pl.ds(pl.multiple_of(ip * half, half), half)

    def group_rows(a1):
        return pl.ds(pl.multiple_of(a1 * group, group), group)

    lane = lane_iota((depth, NAR))
    gain_cols = [column_of(r[...].astype(F32)) for r in (na, nf)]
    narrow_own = jnp.concatenate([turned(wr[...].astype(F32)), jnp.zeros((depth, NAR - experts), F32)], axis=1)
    narrow_own = jnp.where(lane == experts, gain_cols[0], jnp.where(lane == experts + 1, gain_cols[1], narrow_own))
    own = w_row(i, e)
    w_all[own, wide:] = narrow_own.astype(BF16)
    w_all[own, :q_width] = wq[:, half_lanes(i, q_width)]
    w_all[own, q_width : q_width + k_width] = wk[:, half_lanes(i, k_width)]
    w_all[own, q_width + k_width : wide] = wv[:, half_lanes(i, k_width)]
    p.barrier(whole_plane=True)
    cuts = (
        (wq.at[:, half_lanes(1 - i, q_width)], 0, q_width),
        (wk.at[:, half_lanes(1 - i, k_width)], q_width, k_width),
        (wv.at[:, half_lanes(1 - i, k_width)], q_width + k_width, k_width),
        (w_all.at[own, pl.ds(wide, NAR)], wide, NAR),
    )
    give_w = [
        remote(src, w_all.at[own, pl.ds(first, size)], xs.at[n], xr.at[n], p.over_x())
        for n, (src, first, size) in enumerate(cuts)
    ]
    for one in give_w:
        one.start()
    give_x = remote(tok, x_all.at[i], xs.at[4], xr.at[4], p.over_x())
    take_x = remote(x_all.at[1 - i], x_all.at[1 - i], xs.at[4], xr.at[4], p.over_x())
    give_x.start()

    ga = Gather(p, lambda block: w_all.at[w_row(i, block)], ga_s, ga_r)
    gb = Gather(p, lambda block: w_all.at[w_row(1 - i, block)], gb_s, gb_r)
    gw = Gather(p, lambda block: wo_all.at[w_row(0, block)], gw_s, gw_r)
    gc = Gather(p, lambda block: og.at[row_block(block)], gc_s, gc_r, lean=True)
    gf = Gather(p, lambda block: f_all.at[row_block(block)], gf_s, gf_r)

    ga.begin()
    own_cot = pltpu.make_async_copy(cot, og.at[row_block(e)], loc.at[0])
    own_cot.start()
    loads = [
        pltpu.make_async_copy(src, dst, loc.at[1 + n])
        for n, (src, dst) in enumerate(((eg, wgu.at[half_rows(i), pl.ds(0, ff)]), (eu, wgu.at[half_rows(i), pl.ds(ff, ff)]), (ed, wd.at[:, half_rows(i)])))
    ]
    for one in loads:
        one.start()
    wo_all[w_row(0, e), :] = wo[...]
    x_all[i] = tok[...]
    for n, (_, first, size) in enumerate(cuts):
        there = w_all.at[w_row(1 - i, e), pl.ds(first, size)]
        remote(there, there, xs.at[n], xr.at[n], p.over_x()).wait_recv()
    gb.begin()
    cut = ff // 48 * 16
    weight_moves = (
        (eg, lambda ip: wgu.at[half_rows(ip), pl.ds(0, ff)]),
        (eu, lambda ip: wgu.at[half_rows(ip), pl.ds(ff, ff)]),
        (ed.at[pl.ds(0, cut)], lambda ip: wd.at[pl.ds(0, cut), half_rows(ip)]),
        (ed.at[pl.ds(cut, ff - cut)], lambda ip: wd.at[pl.ds(cut, ff - cut), half_rows(ip)]),
    )
    give_e = [
        remote(src, dst(i), xs.at[5 + n], xr.at[5 + n], p.over_x()) for n, (src, dst) in enumerate(weight_moves)
    ]
    take_e = [
        remote(dst(1 - i), dst(1 - i), xs.at[5 + n], xr.at[5 + n], p.over_x())
        for n, (src, dst) in enumerate(weight_moves)
    ]
    for one in give_e[:3]:
        one.start()

    ends = [lengths[0, 0].astype(F32)]
    for n in range(1, lengths.shape[1]):
        ends.append(ends[-1] + lengths[0, n].astype(F32))
    place_row = places[...].astype(F32)
    place_col = column_of(place_row)
    doc_row, _ = documents(place_row, ends[:-1])
    doc_col, start_col = documents(place_col, ends[:-1])
    vis[...] = jnp.where((doc_row == doc_col) & (place_col >= place_row), 1.0, 0.0)
    lane = lane_iota((1, 128))
    quarter = HEAD_DIM // 2
    freq = jnp.exp((lane % quarter).astype(F32) * (-2.0 / HEAD_DIM * math.log(ROPE_BASE)))
    angle = (place_col - start_col) * freq
    cs[...] = jnp.cos(angle)
    sine = jnp.sin(angle)
    sn[...] = jnp.where(lane % HEAD_DIM < quarter, -sine, sine)

    both = (ga, gb)
    for g in both:
        g.phase(1)
    for k in range(3):
        for g in both:
            g.cross(k)
        if k < 2:
            for g in both:
                g.phase(k + 2)
        if k == 1:
            gw.begin()
    gw.phase(1)
    own_cot.wait()
    for g in both:
        g.cross(3)
    for k in range(4):
        for g in both:
            g.join(k)

    events = [
        functools.partial(gw.phase, 2),
        functools.partial(gw.cross, 0),
        functools.partial(gw.phase, 3),
        gc.begin,
        functools.partial(gw.cross, 1),
        functools.partial(gw.cross, 2),
        functools.partial(gw.cross, 3),
    ]

    def serve():
        if events:
            events.pop(0)()

    take_x.wait_recv()
    narrow = w_all[:, wide:]
    gains = gain_rows(narrow, experts)
    att_in = mix.at[pl.ds(2 * rows, 2 * rows)]

    def fill_att_in():
        for ip in range(2):
            x = x_all[ip].astype(F32)
            att_in[ip * rows : (ip + 1) * rows, :] = (x * inverse_rms(x) * gains[0:1]).astype(BF16)

    fill_att_in()
    serve()
    cos, sin = cs[...], sn[...]

    def rope(values):
        return values * cos + swap_halves(values) * sin

    def unrope(values):
        return values * cos - swap_halves(values) * sin

    for tile in range(wide // 256):
        lin = dot_plain(att_in[...], w_all[:, tile * 256 : (tile + 1) * 256])
        for h in range(2):
            col = tile * 256 + h * 128
            piece = lin[:, h * 128 : (h + 1) * 128]
            if col < q_width:
                q[:, col : col + 128] = rope(piece).astype(BF16)
                continue
            is_key = col < q_width + k_width
            n = (col - q_width - (0 if is_key else k_width)) // 128
            lows, highs = (klo, khi) if is_key else (vlo, vhi)
            for g, (low, high) in enumerate(split_heads(rope(piece) if is_key else piece)):
                lows[2 * n + g] = low.astype(BF16)
                highs[2 * n + g] = high.astype(BF16)
    serve()
    sides = ((klo, vlo), (khi, vhi))
    for pair in range(heads // 2):
        lanes = slice(pair * 128, (pair + 1) * 128)
        total = None
        for side, (keys, vals) in enumerate(sides):
            head = 2 * pair + side
            g = head // ratio
            scores = dot_last(q[:, lanes], keys[g]) * scale
            scores = jnp.where(vis[...] > 0, scores, MASK_FILL)
            grown = jnp.exp(scores - jnp.max(scores, axis=1, keepdims=True))
            probs = (grown / jnp.sum(grown, axis=1, keepdims=True)).astype(BF16)
            pr[head] = probs
            term = dot_plain(probs, vals[g])
            total = term if total is None else total + term
        att[:, lanes] = total.astype(BF16)
        serve()
    while events:
        serve()
    for k in range(4):
        gw.join(k)
    gc.phase(1)
    opart[...] = dot_plain(att[row_block(1 - i), :], wo_all[...]).astype(BF16)
    give_o = remote(opart, orecv, xs.at[9], xr.at[9], p.over_x())
    give_o.start()
    give_e[3].start()
    hid[...] = tok[...].astype(F32) + dot_plain(att[row_block(i), :], wo_all[...])
    gc.cross(0)
    gc.phase(2)
    hits, keeps = kept_pairs(routes[...], slots[...], experts, capacity)
    hit[...] = hits
    kept[...] = keeps
    for one in loads:
        one.wait()
    give_o.wait()
    hidden = hid[...] + orecv[...].astype(F32)
    hid[...] = hidden
    ffn_in = (hidden * inverse_rms(hidden) * gains[1:2]).astype(BF16)
    f_all[row_block(e), :] = ffn_in
    gf.begin()
    logits = dot_plain(ffn_in, narrow)
    chosen = hit[...] > 0
    logits = jnp.where(chosen, logits, MASK_FILL)
    grown = jnp.where(chosen, jnp.exp(logits - jnp.max(logits, axis=1, keepdims=True)), 0.0)
    gate = grown / jnp.sum(grown, axis=1, keepdims=True)
    gates[...] = gate
    gate_rows = jnp.transpose(gate * kept[...])
    for name in range(experts):
        gate_out[name] = jnp.broadcast_to(gate_rows[name : name + 1, :], (8, rows))
    gates_in = Exchange(p, gate_out, gate_in, gs_s, gs_r)
    grads_in = Exchange(p, grad_out, grad_in, gg_s, gg_r)

    @pl.loop(0, experts)
    def _(there):
        gates_in.give(there)

    gc.hand()
    gc.phase(3)
    sc = Scatter(
        p,
        lambda a1, b1: part.at[row_block(a1 * 4 + b1)],
        lambda a1, y1: core_in.at[a1 * 2 + y1],
        lambda a1: y_in.at[a1],
        lambda slot: a_in.at[slot - 1],
        lambda j: pass_in.at[j],
        sc_s, sc_r, lean=True,
    )

    def store_mix(a1):
        return pltpu.make_async_copy(mix, mixp.at[a1], mix_sem)

    def gate_of(k):
        return jnp.concatenate([column_of(gate_in[near[k] * 4 + b1, 0:1, :]) for b1 in range(4)], axis=0)

    def inward(k):
        here = group_rows(near[k])
        h12[...] = dot_plain(f_all[here, :], wgu[...])
        pre = h12[:, :ff]
        hgu[here, 0:ff] = (pre * jax.nn.sigmoid(pre) * h12[:, ff:]).astype(BF16)

    def outward(k):
        a1 = near[k]
        here = group_rows(a1)
        if k > 0:
            store_mix(near[k - 1]).wait()
        gate = gate_of(k)

        def project(n, gate_grad):
            cols = pl.ds(pl.multiple_of(n * 512, 512), 512)
            res = dot_plain(hgu[here, 0:ff], wd[:, cols]).astype(BF16).astype(F32)
            mix[:, cols] = (gate * res).astype(BF16)
            c = og[here, cols].astype(F32)
            og[here, cols] = (gate * c).astype(BF16)
            return gate_grad + jnp.sum(res * c, axis=1, keepdims=True)

        gc.sent(k)
        gate_grad = lax.fori_loop(0, width // 512, project, jnp.zeros((group, 1), F32))
        store_mix(a1).start()
        for b1 in range(4):
            row = row_of(gate_grad[b1 * rows : (b1 + 1) * rows])
            grad_out[a1 * 4 + b1] = jnp.broadcast_to(row, (8, rows))
            grads_in.give(a1 * 4 + b1)

    def backward(k):
        here = group_rows(near[k])
        hg = dot_last(og[here, :], wd[...])
        pre = h12[:, :ff]
        s = jax.nn.sigmoid(pre)
        hgu[here, ff : 2 * ff] = (hg * h12[:, ff:] * s * (1.0 + pre * (1.0 - s))).astype(BF16)
        hgu[here, 2 * ff :] = (hg * (pre * s)).astype(BF16)

    def send_rows(k):
        here = group_rows(near[k])

        @pl.loop(0, width // 512)
        def _(n):
            cols = pl.ds(pl.multiple_of(n * 512, 512), 512)
            part[here, cols] = dot_last(hgu[here, ff:], wgu[cols, :]).astype(BF16)

        sc.start(k)

    for one in take_e[:2]:
        one.wait_recv()

    @pl.loop(0, experts)
    def _(there):
        gates_in.take(there)

    gf.cross(0)
    gf.phase(1)
    gc.join(0)
    gf.join(0)
    inward(0)
    take_e[2].wait_recv()
    take_e[3].wait_recv()
    outward(0)
    gc.cross(1)
    gc.cross(2)
    gf.phase(2)
    backward(0)
    send_rows(0)
    gf.cross(1)
    gf.phase(3)
    gc.join(1)
    gf.join(1)
    inward(1)
    outward(1)
    gc.cross(3)
    backward(1)
    gf.cross(2)
    send_rows(1)
    gc.join(2)
    gf.join(2)
    inward(2)
    sc.core(1)
    outward(2)
    backward(2)
    gf.cross(3)
    send_rows(2)
    gc.join(3)
    gf.join(3)
    inward(3)
    sc.core(2)
    outward(3)
    backward(3)
    send_rows(3)
    sc.cross(2)

    tile = 256
    tiles = half // tile

    def rows_of(ip, n):
        return pl.ds(pl.multiple_of(ip * half + n * tile, tile), tile)

    def in_grad(ip, n):
        return dot_first(f_all[:, rows_of(ip, n)], hgu[:, ff:])

    def down_grad(ip, n):
        return dot_first(hgu[:, 0:ff], og[:, rows_of(ip, n)])

    def give_in(n):
        src, dst = wgu.at[half_rows(1 - i), pl.ds(n * ff, ff)], gur.at[:, pl.ds(n * ff, ff)]
        return remote(src, dst, xs.at[10 + n], xr.at[10 + n], p.over_x())

    give_g, give_u = give_in(0), give_in(1)
    give_d = remote(wd.at[:, half_rows(1 - i)], edr, xs.at[12], xr.at[12], p.over_x())

    for n in range(tiles):
        wgu[rows_of(1 - i, n), :] = in_grad(1 - i, n).astype(BF16)
        if n == 0:
            sc.core(3)
        if n == 1:
            sc.core(0)
            sc.meet()
    give_g.start()

    @pl.loop(0, tiles)
    def _(n):
        wd[:, rows_of(1 - i, n)] = down_grad(1 - i, n).astype(BF16)

    sc.relay(2)

    def save(n, src, dst):
        return pltpu.make_async_copy(src, dst, loc.at[n % 4])

    saves = []
    for n in range(tiles):
        spot = h12.at[pl.ds((n % 2) * tile, tile)]
        if n >= 2:
            saves[n - 2].wait()
        spot[...] = in_grad(i, n)
        saves.append(save(n, spot, gu_own.at[pl.ds(n * tile, tile)]))
        saves[n].start()
    for n in range(tiles - 2, tiles):
        saves[n].wait()
    sc.cross(3)
    saves = []
    for n in range(tiles):
        spot = h12.at[:, pl.ds(n * tile, tile)]
        spot[...] = down_grad(i, n)
        saves.append(save(n, spot, od_own.at[:, pl.ds(n * tile, tile)]))
        saves[n].start()
    store_mix(near[3]).wait()
    gf.drain()

    spare = 16 * rows - 2 * group_rows_count
    dq = hgu.at[pl.ds(spare, group_rows_count), pl.ds(0, wide)]
    bg = hgu.at[pl.ds(spare + group_rows_count, group_rows_count)]
    ag = mix.at[pl.ds(0, group_rows_count), pl.ds(0, q_width)]
    friends = [p.over_x(), p.over_core(), p.over_y()] + [(i, ((p.a + shift) % 4) * 4 + p.bc) for shift in range(1, 4)]
    for friend in friends:
        pl.semaphore_signal(ready.at[0], inc=1, device_id=friend, device_id_type=MESH)
    load_mix = [pltpu.make_async_copy(mixp.at[a1], f_all.at[group_rows(a1)], loc.at[4 + k]) for k, a1 in enumerate(near)]
    for one in load_mix:
        one.start()
    sm = Scatter(
        p,
        lambda a1, b1: f_all.at[row_block(a1 * 4 + b1)],
        lambda a1, y1: og.at[row_block(a1 * 2 + y1)],
        lambda a1: og.at[row_block(8 + a1)],
        lambda slot: og.at[row_block(11 + slot)],
        lambda j: og.at[row_block(14 + j)],
        sm_s, sm_r, lean=True,
    )

    def piece_of(n):
        return hgu.at[pl.ds(pl.multiple_of(n * depth, 16), depth)]

    so = Scatter(
        p,
        lambda a1, b1: piece_of(a1 * 4 + b1),
        lambda a1, y1: piece_of(16 + a1 * 2 + y1),
        lambda a1: piece_of(24 + a1),
        lambda slot: piece_of(27 + slot),
        lambda j: piece_of(30 + j),
        so_s, so_r,
    )
    both_rows = 2 * depth
    flat = (pl.ds(0, both_rows), pl.ds(0, wide + NAR))
    sw = Scatter(
        p,
        lambda a1, b1: part.at[pl.ds(pl.multiple_of((a1 * 4 + b1) * both_rows, 32), both_rows), pl.ds(0, wide + NAR)],
        lambda a1, y1: core_in.at[(a1 * 2 + y1,) + flat],
        lambda a1: y_in.at[(a1,) + flat],
        lambda slot: a_in.at[(slot - 1,) + flat],
        lambda j: pass_in.at[(j,) + flat],
        sw_s, sw_r,
    )
    for one in load_mix:
        one.wait()
    pl.semaphore_wait(ready.at[0], len(friends))
    for k in (3, 2, 1, 0):
        sm.start(k)
    sm.core(3)
    sm.core(2)
    sc.relay(3)
    sc.cross(0)
    sm.core(1)
    sm.core(0)

    @pl.loop(0, experts)
    def _(there):
        grads_in.take(there)

    by_expert = jnp.concatenate([grad_in[name, 0:1, :] for name in range(experts)], axis=0)
    lane = lane_iota((rows, NAR))
    gate_grad = jnp.concatenate([turned(by_expert), jnp.zeros((rows, NAR - experts), F32)], axis=1) * kept[...]
    gate = gates[...]
    logit_grad = (gate * (gate_grad - jnp.sum(gate * gate_grad, axis=1, keepdims=True))).astype(BF16)
    narrow = w_all[:, wide:]
    gains = gain_rows(narrow, experts)
    routed = dot_last(logit_grad, narrow)
    hidden = hid[...]
    r2 = inverse_rms(hidden)
    n2 = hidden * r2
    again = pltpu.make_async_copy(cot, opart, loc.at[8])
    again.start()
    again.wait()
    sc.finish()
    ffn_grad = sc.total() + routed
    d2 = ffn_grad * gains[1:2]
    state[...] = opart[...].astype(F32) + r2 * (d2 - n2 * jnp.mean(d2 * n2, axis=1, keepdims=True))
    bg[row_block(i), :] = state[...].astype(BF16)
    give_b = remote(bg.at[row_block(i)], bg.at[row_block(i)], xs.at[13], xr.at[13], p.over_x())
    take_b = remote(bg.at[row_block(1 - i)], bg.at[row_block(1 - i)], xs.at[13], xr.at[13], p.over_x())
    give_b.start()
    give_u.start()
    sc.drain()
    for friend in friends[1:]:
        pl.semaphore_signal(ready.at[1], inc=1, device_id=friend, device_id_type=MESH)
    gain_ffn = jnp.sum(ffn_grad * n2, axis=0, keepdims=True)
    ffn_in = (n2 * gains[1:2]).astype(BF16)
    small[...] = dot_first(ffn_in, logit_grad)
    for n in range(width // NAR):
        span = slice(n * NAR, (n + 1) * NAR)
        small[span, :] = jnp.where(lane == experts + 1, column_of(gain_ffn[:, span]), small[span, :])
    for one in saves:
        one.wait()
    for one in give_w + [give_x] + give_e:
        one.wait_send()
    for g in (ga, gb, gw):
        g.drain()
    gates_in.drain()
    grads_in.drain()
    fill_att_in()
    dk[...] = jnp.zeros_like(dk)
    dv[...] = jnp.zeros_like(dv)
    low_lane = lane_iota((2 * rows, 128)) < HEAD_DIM
    sm.cross(3)
    take_b.wait_recv()
    for n in range(q_width // 256):
        lanes = slice(n * 256, (n + 1) * 256)
        ag[:, lanes] = dot_last(bg[...], wo_all[lanes, :]).astype(BF16)
    for n in range(q_width // 256):
        lanes = slice(n * 256, (n + 1) * 256)
        hgu[lanes, :] = dot_first(att[:, lanes], bg[...]).astype(BF16)
    for k in (3, 2, 1, 0):
        so.start(k)
    for pair in range(heads // 2):
        lanes = slice(pair * 128, (pair + 1) * 128)
        grad_in_pair = ag[:, lanes]
        q_pair = q[:, lanes]
        q_grad = None
        for side, (keys, vals) in enumerate(sides):
            head = 2 * pair + side
            g = head // ratio
            probs = pr[head]
            prob_grad = dot_last(grad_in_pair, vals[g])
            wide_probs = probs.astype(F32)
            shift = jnp.sum(wide_probs * prob_grad, axis=1, keepdims=True)
            score_grad = (wide_probs * (prob_grad - shift)).astype(BF16)
            term = dot_plain(score_grad, keys[g])
            q_grad = term if q_grad is None else q_grad + term
            mine = low_lane if side == 0 else jnp.logical_not(low_lane)
            k_term = jnp.where(mine, dot_first(score_grad, q_pair), 0.0)
            v_term = jnp.where(mine, dot_first(probs, grad_in_pair), 0.0)
            if g % 2 != side:
                k_term = pltpu.roll(k_term, HEAD_DIM, 1)
                v_term = pltpu.roll(v_term, HEAD_DIM, 1)
            lot = slice((g // 2) * 128, (g // 2 + 1) * 128)
            dk[:, lot] += k_term
            dv[:, lot] += v_term
        dq[:, lanes] = unrope(scale * q_grad).astype(BF16)
        if pair == 0:
            for k in (3, 2, 1, 0):
                so.core(k)
            sm.cross(2)
        if pair == 1:
            sm.meet()
            sm.relay(3)
        if pair == 3:
            so.cross(3)
            sm.relay(2)
        if pair == 4:
            so.cross(2)
            so.cross(1)
        if pair == 5:
            so.relay(3)
    for n in range(k_width // 128):
        lanes = slice(n * 128, (n + 1) * 128)
        dq[:, q_width + n * 128 : q_width + (n + 1) * 128] = unrope(scale * dk[:, lanes]).astype(BF16)
        dq[:, q_width + k_width + n * 128 : q_width + k_width + (n + 1) * 128] = dv[:, lanes].astype(BF16)

    both_back = dot_last(dq[...], w_all[:, :wide])
    bg_terms = jnp.zeros((1, width), F32)
    for ip in range(2):
        x = x_all[ip].astype(F32)
        bg_terms = bg_terms + jnp.sum(both_back[ip * rows : (ip + 1) * rows] * (x * inverse_rms(x)), axis=0, keepdims=True)
    for n in range(width // NAR):
        span = slice(n * NAR, (n + 1) * NAR)
        small[span, :] = jnp.where(lane == experts, column_of(bg_terms[:, span]), small[span, :])
    h12[0 : 2 * rows, :] = both_back[:, : 2 * ff]
    h12[2 * rows :, 0 : width - 2 * ff] = both_back[:, 2 * ff :]

    def back_rows(ip):
        return jnp.concatenate([h12[row_block(ip), :], h12[row_block(2 + ip), 0 : width - 2 * ff]], axis=1)

    opart[...] = back_rows(1 - i).astype(BF16)
    give_a = remote(opart, orecv, xs.at[14], xr.at[14], p.over_x())
    give_a.start()
    give_d.start()
    step = plane // 2
    count = step // depth
    for turn in range(2):
        n = near[3 - 3 * turn] // 2
        for ip in range(2):
            span = pl.ds(pl.multiple_of(ip * plane + n * step, 128), step)
            block = dot_first(att_in[:, span], dq[...]).astype(BF16)
            extra = small[span, :].astype(BF16)
            for m in range(count):
                at = pl.ds(pl.multiple_of((n * count + m) * both_rows + ip * depth, 16), depth)
                part[at, :wide] = block[m * depth : (m + 1) * depth]
                part[at, wide : wide + NAR] = extra[m * depth : (m + 1) * depth]
        if turn == 0:
            pl.semaphore_wait(ready.at[1], len(friends) - 1)
        sw.start(3 - 2 * turn)
        sw.start(2 - 2 * turn)
    for k in (3, 2, 1, 0):
        sw.core(k)
    so.relay(2)
    so.cross(0)
    sw.cross(3)
    sw.cross(2)
    give_a.wait_recv()
    attn_grad = back_rows(i) + orecv[...].astype(F32)
    x = x_all[i].astype(F32)
    r1 = inverse_rms(x)
    n1 = x * r1
    d1 = attn_grad * gains[0:1]
    tok_grad[...] = (state[...] + r1 * (d1 - n1 * jnp.mean(d1 * n1, axis=1, keepdims=True))).astype(BF16)
    sw.relay(3)
    sw.cross(1)
    sw.relay(2)
    sw.cross(0)
    sw.finish()
    summed = sw.total()
    wsend[0] = summed[:depth]
    wsend[1] = summed[depth:]
    wgive[...] = wsend[1 - i].astype(BF16)
    give_s = remote(wgive, wrecv, xs.at[15], xr.at[15], p.over_x())
    give_s.start()

    def place_half(ip, values):
        dq_out[:, half_lanes(ip, q_width)] = values[:, :q_width]
        dk_out[:, half_lanes(ip, k_width)] = values[:, q_width : q_width + k_width]
        dv_out[:, half_lanes(ip, k_width)] = values[:, q_width + k_width : wide]

    mine = wsend[i]
    place_half(i, mine)
    sm.cross(0)
    sm.finish()
    out[...] = (hid[...] + sm.total()).astype(BF16)
    give_s.wait_recv()
    theirs = wrecv[...].astype(F32)
    place_half(1 - i, theirs)
    gains_out[...] = mine[:, wide:] + theirs[:, wide:]
    so.finish()
    dwo_out[...] = so.total()
    for one in (give_b, give_a, give_s):
        one.wait_send()
    for one in (give_g, give_u, give_d):
        one.wait()
    for s in (sm, so, sw):
        s.drain()


def finish_kernel(
    gu_own, od_own, gur, edr, out, tok, dq, dk, dv, dwo, gains,
    out_o, tok_o, dq_o, dk_o, dv_o, dwo_o, ga_o, gf_o, gr_o, eg_o, eu_o, ed_o,
):
    ff = eg_o.shape[2]
    eg_o[0] = gu_own[:, :ff] + gur[:, :ff].astype(F32)
    eu_o[0] = gu_own[:, ff:] + gur[:, ff:].astype(F32)
    ed_o[0] = od_own[...] + edr[...].astype(F32)

    @pl.when(pl.program_id(0) == 0)
    def _():
        for src, dst in ((out, out_o), (tok, tok_o), (dq, dq_o), (dk, dk_o), (dv, dv_o), (dwo, dwo_o)):
            dst[...] = src[...]
        experts = gr_o.shape[0]
        rows = turned(gains[...])
        ga_o[...] = rows[experts : experts + 1]
        gf_o[...] = rows[experts + 1 : experts + 2]
        gr_o[...] = rows[:experts]


def paired_body(
    tokens, cotangent, norm_attn, w_query, key_projection, value_projection, w_out, norm_ffn, w_router,
    expert_gate, expert_up, expert_down, routes, slot_order, doc_lengths, deal,
):
    rows, width = tokens.shape
    depth = w_query.shape[0]
    experts = 16
    q_width = w_query.shape[1] // 2
    k_width = key_projection.shape[1] // 2
    wide = q_width + 2 * k_width
    ff = expert_gate.shape[2]
    half = width // 2
    vm = pl.BlockSpec(memory_space=pltpu.VMEM)
    hb = pl.BlockSpec(memory_space=pl.ANY)
    sm = pl.BlockSpec(memory_space=pltpu.SMEM)

    def shaped(*dims, dtype=BF16):
        return jax.ShapeDtypeStruct(dims, dtype)

    def sems(n):
        return pltpu.SemaphoreType.DMA((n,))

    heads = q_width // HEAD_DIM
    groups = k_width // HEAD_DIM
    group_rows = 2 * rows

    def room(*dims, dtype=BF16):
        return pltpu.VMEM(dims, dtype)

    def gather_sems(n):
        return [sems(Gather.SENDS), sems(Gather.RECVS)] * n

    def scatter_sems(n):
        return [sems(Scatter.SENDS), sems(Scatter.RECVS)] * n

    res = pl.pallas_call(
        layer_kernel,
        name="layer",
        out_shape=(
            shaped(rows, width),
            shaped(rows, width),
            shaped(depth, 2 * q_width, dtype=F32),
            shaped(depth, 2 * k_width, dtype=F32),
            shaped(depth, 2 * k_width, dtype=F32),
            shaped(depth, width, dtype=F32),
            shaped(depth, NAR, dtype=F32),
            shaped(half, 2 * ff, dtype=F32),
            shaped(ff, half, dtype=F32),
            shaped(half, 2 * ff),
            shaped(ff, half),
            shaped(4, 4 * rows, width),
        ),
        in_specs=[vm] * 8 + [hb] * 4 + [vm, vm, sm, vm],
        out_specs=(vm,) * 7 + (hb,) * 5,
        scratch_shapes=[
            room(2 * 16 * depth, wide + NAR),
            room(16 * depth, width),
            room(2, rows, width),
            room(group_rows, q_width),
        ]
        + [room(groups, group_rows, 128)] * 4
        + [
            room(heads, group_rows, group_rows),
            room(group_rows, q_width),
            room(rows, width, dtype=F32),
            room(group_rows, group_rows, dtype=F32),
            room(group_rows, 128, dtype=F32),
            room(group_rows, 128, dtype=F32),
            room(rows, NAR, dtype=F32),
            room(rows, NAR, dtype=F32),
            room(rows, NAR, dtype=F32),
            room(rows, width),
            room(rows, width),
        ]
        + [room(16 * rows, width)] * 4
        + [room(8, rows, width), room(4, rows, width), room(2, rows, width), room(2, rows, width)]
        + [room(16, 8, rows, dtype=F32)] * 4
        + [
            room(width, 2 * ff),
            room(ff, width),
            room(4 * rows, 2 * ff, dtype=F32),
            room(4 * rows, width),
            room(group_rows, k_width, dtype=F32),
            room(group_rows, k_width, dtype=F32),
            room(2 * 16 * depth, NAR, dtype=F32),
            room(rows, width, dtype=F32),
            room(2, depth, wide + NAR, dtype=F32),
            room(depth, wide + NAR),
            room(depth, wide + NAR),
        ]
        + gather_sems(5)
        + scatter_sems(4)
        + [sems(16)] * 4
        + [sems(16), sems(16), sems(9), pltpu.SemaphoreType.DMA(()), pltpu.SemaphoreType.REGULAR((2,))],
        compiler_params=pltpu.CompilerParams(collective_id=1, has_side_effects=True, vmem_limit_bytes=64 << 20),
    )(
        tokens, w_query, key_projection, value_projection, w_router.T, norm_attn[None], norm_ffn[None], w_out,
        cotangent, expert_gate[0], expert_up[0], expert_down[0], routes.T, slot_order, doc_lengths,
        deal.reshape(1, -1),
    )
    out, tok_grad, dq, dk, dv, dwo, gains, gu_own, od_own, gur, edr, _ = res

    steps = 2

    def cut(*dims):
        return pl.BlockSpec((dims[0] // steps,) + dims[1:], lambda n: (n,) + (0,) * (len(dims) - 1))

    def cut_out(*dims):
        return pl.BlockSpec((1, dims[0] // steps) + dims[1:], lambda n: (0, n) + (0,) * (len(dims) - 1))

    def entire(*dims):
        return pl.BlockSpec(dims, lambda n: (0,) * len(dims))

    mats = ((half, ff), (half, ff), (ff, half))
    sums = ((half, 2 * ff), (ff, half))
    rest = (out, tok_grad, dq, dk, dv, dwo, gains)
    res = pl.pallas_call(
        finish_kernel,
        name="finish",
        grid=(steps,),
        out_shape=tuple(jax.ShapeDtypeStruct(r.shape, r.dtype) for r in rest[:6])
        + (shaped(1, depth, dtype=F32), shaped(1, depth, dtype=F32), shaped(experts, depth, dtype=F32))
        + tuple(shaped(1, *m, dtype=F32) for m in mats),
        in_specs=[cut(*m) for m in sums] * 2 + [entire(*r.shape) for r in rest],
        out_specs=tuple(entire(*r.shape) for r in rest[:6])
        + (entire(1, depth), entire(1, depth), entire(experts, depth))
        + tuple(cut_out(*m) for m in mats),
        compiler_params=pltpu.CompilerParams(vmem_limit_bytes=62 << 20),
    )(gu_own, od_own, gur, edr, *rest)
    out, tok_grad, dq, dk, dv, dwo, g_attn, g_ffn, g_router, eg, eu, ed = res
    return (
        out, tok_grad, g_attn.reshape(-1), dq, dk, dv, dwo, g_ffn.reshape(-1), g_router.T, eg, eu, ed,
    )


def general_body(
    tokens,
    cotangent,
    norm_attn,
    w_query,
    key_projection,
    value_projection,
    w_out,
    norm_ffn,
    w_router,
    expert_gate,
    expert_up,
    expert_down,
    routes,
    slot_order,
    doc_lengths,
    deal,
):
    gain_attn, full_query, gathered_key, gathered_value, full_out, gain_ffn, full_router = (
        lax.all_gather(norm_attn, ("dp", "expert"), axis=0, tiled=True),
        lax.all_gather(w_query, ("dp", "expert"), axis=0, tiled=True),
        lax.all_gather(key_projection, ("dp", "expert"), axis=0, tiled=True),
        lax.all_gather(value_projection, ("dp", "expert"), axis=0, tiled=True),
        lax.all_gather(w_out, ("dp", "expert"), axis=0, tiled=True),
        lax.all_gather(norm_ffn, ("dp", "expert"), axis=0, tiled=True),
        lax.all_gather(w_router, ("dp", "expert"), axis=0, tiled=True),
    )
    full_gate, full_up, full_down = (
        lax.all_gather(expert_gate[0], "dp", axis=0, tiled=True),
        lax.all_gather(expert_up[0], "dp", axis=0, tiled=True),
        lax.all_gather(expert_down[0], "dp", axis=1, tiled=True),
    )
    count_of_rows, model_width = tokens.shape
    top_count = routes.shape[1]
    experts = full_router.shape[1]
    owners = lax.axis_size("expert")
    capacity = 9 * count_of_rows * top_count // (8 * experts)
    head_count = full_query.shape[1] // HEAD_DIM
    groups = gathered_key.shape[1] // HEAD_DIM
    head_ratio = head_count // groups
    scale_attn = gain_attn.astype(jnp.float32)
    scale_ffn = gain_ffn.astype(jnp.float32)
    score_scale = HEAD_DIM ** (-0.5)
    group_places = deal[:, 0, :].reshape(-1)
    group_docs, group_offsets = doc_layout(doc_lengths[0], group_places)
    shard_start = lax.axis_index("dp") * count_of_rows
    places = lax.dynamic_slice_in_dim(group_places, shard_start, count_of_rows)
    doc_ids = lax.dynamic_slice_in_dim(group_docs, shard_start, count_of_rows)
    offsets = lax.dynamic_slice_in_dim(group_offsets, shard_start, count_of_rows)
    cosine_lookup, sine_lookup = rope_tables(offsets, HEAD_DIM)
    inputs = tokens.astype(jnp.float32)
    inverse_one = lax.rsqrt(jnp.mean(inputs * inputs, axis=1, keepdims=True) + NORM_EPS)
    normed_one = inputs * inverse_one
    attention_input = (normed_one * scale_attn).astype(jnp.bfloat16)
    query_rows = apply_rotation(
        dot_plain(attention_input, full_query).reshape(count_of_rows, head_count, HEAD_DIM),
        cosine_lookup,
        sine_lookup,
    ).astype(jnp.bfloat16)
    key_matrix_rows = apply_rotation(
        dot_plain(attention_input, gathered_key).reshape(count_of_rows, groups, HEAD_DIM),
        cosine_lookup,
        sine_lookup,
    ).astype(jnp.bfloat16)
    value_matrix_rows = dot_plain(attention_input, gathered_value).astype(jnp.bfloat16)
    all_keys, all_values = (
        lax.all_gather(key_matrix_rows.reshape(count_of_rows, -1), "dp", axis=0, tiled=True),
        lax.all_gather(value_matrix_rows, "dp", axis=0, tiled=True),
    )
    group_rows = all_keys.shape[0]
    key_span = math.gcd(group_rows, 512)
    span_count = group_rows // key_span
    key_spans = (
        all_keys.reshape(span_count, key_span, groups, HEAD_DIM),
        all_values.reshape(span_count, key_span, groups, HEAD_DIM),
        group_places.reshape(span_count, key_span),
        group_docs.reshape(span_count, key_span),
    )
    grouped_q = query_rows.reshape(count_of_rows, groups, head_ratio, HEAD_DIM)

    def span_scores(key_block, key_place, key_doc):
        visible = (doc_ids[:, None] == key_doc[None, :]) & (places[:, None] >= key_place[None, :])
        scores = (
            jnp.einsum("qgrd,kgd->grqk", grouped_q, key_block, preferred_element_type=jnp.float32)
            * score_scale
        )
        return jnp.where(visible[None, None], scores, MASK_FILL)

    def extent(carry, operands):
        run_max, run_sum = carry
        key_block, value_block, key_place, key_doc = operands
        scores = span_scores(key_block, key_place, key_doc)
        new_max = jnp.maximum(run_max, jnp.max(scores, axis=-1, keepdims=True))
        run_sum = run_sum * jnp.exp(run_max - new_max) + jnp.sum(
            jnp.exp(scores - new_max), axis=-1, keepdims=True
        )
        return ((new_max, run_sum), None)

    stat_shape = (groups, head_ratio, count_of_rows, 1)
    (row_max, row_sum), _ = lax.scan(
        extent,
        (jnp.full(stat_shape, MASK_FILL, jnp.float32), jnp.zeros(stat_shape, jnp.float32)),
        key_spans,
    )
    log_total = row_max + jnp.log(row_sum)

    def weigh_values(running, operands):
        key_block, value_block, key_place, key_doc = operands
        weights = jnp.exp(span_scores(key_block, key_place, key_doc) - log_total).astype(
            jnp.bfloat16
        )
        return (
            running
            + jnp.einsum(
                "grqk,kgd->qgrd", weights, value_block, preferred_element_type=jnp.float32
            ),
            None,
        )

    attended, _ = lax.scan(
        weigh_values,
        jnp.zeros((count_of_rows, groups, head_ratio, HEAD_DIM), jnp.float32),
        key_spans,
    )
    attended = attended.reshape(count_of_rows, head_count * HEAD_DIM).astype(jnp.bfloat16)
    hidden_state = inputs + dot_plain(attended, full_out)
    inverse_two = lax.rsqrt(jnp.mean(hidden_state * hidden_state, axis=1, keepdims=True) + NORM_EPS)
    normed_two = hidden_state * inverse_two
    ffn_in = (normed_two * scale_ffn).astype(jnp.bfloat16)
    logits = dot_plain(ffn_in, full_router)
    route_hits = (routes[:, :, None] == jnp.arange(experts, dtype=jnp.int32)[None, None, :]).astype(
        jnp.float32
    )
    chosen = jnp.sum(route_hits * logits[:, None, :], axis=-1)
    gate_values = jax.nn.softmax(chosen, axis=-1)
    pair_slot, slot_token = assign_slots(routes, slot_order[0], experts, capacity)
    padded_in = jnp.concatenate([ffn_in, jnp.zeros((1, model_width), jnp.bfloat16)], axis=0)
    outgoing = padded_in[slot_token].reshape(owners, capacity, model_width)
    arrived = lax.all_to_all(outgoing, "expert", split_axis=0, concat_axis=0, tiled=True)
    flat_rows = arrived.reshape(-1, model_width)
    gate_pre = dot_plain(flat_rows, full_gate)
    up_pre = dot_plain(flat_rows, full_up)
    hidden = (jax.nn.silu(gate_pre) * up_pre).astype(jnp.bfloat16)
    result = dot_plain(hidden, full_down).astype(jnp.bfloat16).reshape(arrived.shape)
    sent_back = lax.all_to_all(result, "expert", split_axis=0, concat_axis=0, tiled=True)
    exchanged = (
        sent_back,
        arrived,
        gate_pre.reshape(arrived.shape[0], arrived.shape[1], -1),
        up_pre.reshape(arrived.shape[0], arrived.shape[1], -1),
    )
    returned = exchanged[0]
    expert_rows = exchanged[1].reshape(-1, model_width)
    gate_pre = exchanged[2].reshape(expert_rows.shape[0], -1)
    up_pre = exchanged[3].reshape(expert_rows.shape[0], -1)
    out_grad = cotangent.astype(jnp.float32)
    padded_back = jnp.concatenate(
        [returned.reshape(-1, model_width), jnp.zeros((1, model_width), jnp.bfloat16)], axis=0
    )
    slot_grid = pair_slot.reshape(count_of_rows, top_count)
    mixture = jnp.zeros((count_of_rows, model_width), jnp.float32)
    gate_parts = []
    for column in range(top_count):
        picked = padded_back[slot_grid[:, column]].astype(jnp.float32)
        mixture = mixture + gate_values[:, column : column + 1] * picked
        gate_parts.append(jnp.sum(out_grad * picked, axis=1))
    output = (hidden_state + mixture).astype(jnp.bfloat16)
    gate_grad = jnp.stack(gate_parts, axis=1)
    slot_gate = (
        jnp.zeros((experts * capacity + 1,), jnp.float32)
        .at[pair_slot]
        .set(gate_values.reshape(-1))[: experts * capacity]
    )
    padded_grad = jnp.concatenate([out_grad, jnp.zeros((1, model_width), jnp.float32)], axis=0)
    slot_grad = (
        (slot_gate[:, None] * padded_grad[slot_token])
        .astype(jnp.bfloat16)
        .reshape(owners, capacity, model_width)
    )
    arrived_grad = lax.all_to_all(
        slot_grad, "expert", split_axis=0, concat_axis=0, tiled=True
    ).reshape(-1, model_width)
    sigmoid_gate = jax.nn.sigmoid(gate_pre)
    silu_gate = gate_pre * sigmoid_gate
    hidden = (silu_gate * up_pre).astype(jnp.bfloat16)
    hidden_grad = dot_last(arrived_grad, full_down)
    gate_pre_grad = (
        hidden_grad * up_pre * sigmoid_gate * (1.0 + gate_pre * (1.0 - sigmoid_gate))
    ).astype(jnp.bfloat16)
    up_pre_grad = (hidden_grad * silu_gate).astype(jnp.bfloat16)
    down_weight_grad = dot_first(hidden, arrived_grad)
    gate_weight_grad = dot_first(expert_rows, gate_pre_grad)
    up_weight_grad = dot_first(expert_rows, up_pre_grad)
    row_grad = (dot_last(gate_pre_grad, full_gate) + dot_last(up_pre_grad, full_up)).astype(
        jnp.bfloat16
    )
    token_rows_grad = lax.all_to_all(
        row_grad.reshape(owners, capacity, model_width),
        "expert",
        split_axis=0,
        concat_axis=0,
        tiled=True,
    )
    gate_summed, up_summed, down_summed = (
        lax.psum_scatter(
            gate_weight_grad.astype(jnp.bfloat16), "dp", scatter_dimension=0, tiled=True
        ).astype(jnp.float32),
        lax.psum_scatter(
            up_weight_grad.astype(jnp.bfloat16), "dp", scatter_dimension=0, tiled=True
        ).astype(jnp.float32),
        lax.psum_scatter(
            down_weight_grad.astype(jnp.bfloat16), "dp", scatter_dimension=1, tiled=True
        ).astype(jnp.float32),
    )
    dispatch_grad = jax.ops.segment_sum(
        token_rows_grad.reshape(-1, model_width).astype(jnp.float32),
        slot_token,
        num_segments=count_of_rows + 1,
    )[:count_of_rows]
    chosen_grad = gate_values * (
        gate_grad - jnp.sum(gate_values * gate_grad, axis=1, keepdims=True)
    )
    logit_grad = jnp.sum(route_hits * chosen_grad[:, :, None], axis=1).astype(jnp.bfloat16)
    router_grad = dot_first(ffn_in, logit_grad)
    ffn_grad = dispatch_grad + dot_last(logit_grad, full_router)
    ffn_gain_grad = jnp.sum(ffn_grad * normed_two, axis=0)
    scaled_two = ffn_grad * scale_ffn
    state_grad = out_grad + inverse_two * (
        scaled_two - normed_two * jnp.mean(scaled_two * normed_two, axis=1, keepdims=True)
    )
    branch_grad = state_grad.astype(jnp.bfloat16)
    out_weight_grad = dot_first(attended, branch_grad)
    attended_grad = (
        dot_last(branch_grad, full_out)
        .astype(jnp.bfloat16)
        .reshape(count_of_rows, groups, head_ratio, HEAD_DIM)
    )

    def spread_sum(running, operands):
        key_block, value_block, key_place, key_doc = operands
        probs = jnp.exp(span_scores(key_block, key_place, key_doc) - log_total)
        prob_grad = jnp.einsum(
            "qgrd,kgd->grqk", attended_grad, value_block, preferred_element_type=jnp.float32
        )
        return (running + jnp.sum(probs * prob_grad, axis=-1, keepdims=True), None)

    score_shift, _ = lax.scan(spread_sum, jnp.zeros(stat_shape, jnp.float32), key_spans)

    def back_span(running, operands):
        key_block, value_block, key_place, key_doc = operands
        probs = jnp.exp(span_scores(key_block, key_place, key_doc) - log_total)
        prob_grad = jnp.einsum(
            "qgrd,kgd->grqk", attended_grad, value_block, preferred_element_type=jnp.float32
        )
        score_grad = (probs * (prob_grad - score_shift)).astype(jnp.bfloat16)
        running = running + jnp.einsum(
            "grqk,kgd->qgrd", score_grad, key_block, preferred_element_type=jnp.float32
        )
        key_part = (
            jnp.einsum("grqk,qgrd->kgd", score_grad, grouped_q, preferred_element_type=jnp.float32)
            * score_scale
        )
        value_part = jnp.einsum(
            "grqk,qgrd->kgd",
            probs.astype(jnp.bfloat16),
            attended_grad,
            preferred_element_type=jnp.float32,
        )
        return (running, (key_part.reshape(key_span, -1), value_part.reshape(key_span, -1)))

    query_sum, (key_parts, value_parts) = lax.scan(
        back_span, jnp.zeros((count_of_rows, groups, head_ratio, HEAD_DIM), jnp.float32), key_spans
    )
    key_grad, value_sum = (
        lax.psum_scatter(
            key_parts.reshape(group_rows, -1).astype(jnp.bfloat16),
            "dp",
            scatter_dimension=0,
            tiled=True,
        ).astype(jnp.float32),
        lax.psum_scatter(
            value_parts.reshape(group_rows, -1).astype(jnp.bfloat16),
            "dp",
            scatter_dimension=0,
            tiled=True,
        ).astype(jnp.float32),
    )
    query_grad = query_sum * score_scale
    query_lin_grad = unrotate(
        query_grad.reshape(count_of_rows, head_count, HEAD_DIM), cosine_lookup, sine_lookup
    )
    query_lin_grad = query_lin_grad.reshape(count_of_rows, -1).astype(jnp.bfloat16)
    key_lin_grad = (
        unrotate(key_grad.reshape(count_of_rows, groups, HEAD_DIM), cosine_lookup, sine_lookup)
        .reshape(count_of_rows, -1)
        .astype(jnp.bfloat16)
    )
    value_lin_grad = value_sum.astype(jnp.bfloat16)
    query_weight_grad = dot_first(attention_input, query_lin_grad)
    key_weight_grad = dot_first(attention_input, key_lin_grad)
    value_weight_grad = dot_first(attention_input, value_lin_grad)
    attn_grad = (
        dot_last(query_lin_grad, full_query)
        + dot_last(key_lin_grad, gathered_key)
        + dot_last(value_lin_grad, gathered_value)
    )
    attn_gain_grad = jnp.sum(attn_grad * normed_one, axis=0)
    scaled_one = attn_grad * scale_attn
    tokens_grad = (
        state_grad
        + inverse_one
        * (scaled_one - normed_one * jnp.mean(scaled_one * normed_one, axis=1, keepdims=True))
    ).astype(jnp.bfloat16)
    summed = (
        lax.psum_scatter(attn_gain_grad, ("dp", "expert"), scatter_dimension=0, tiled=True),
        lax.psum_scatter(query_weight_grad, ("dp", "expert"), scatter_dimension=0, tiled=True),
        lax.psum_scatter(key_weight_grad, ("dp", "expert"), scatter_dimension=0, tiled=True),
        lax.psum_scatter(value_weight_grad, ("dp", "expert"), scatter_dimension=0, tiled=True),
        lax.psum_scatter(out_weight_grad, ("dp", "expert"), scatter_dimension=0, tiled=True),
        lax.psum_scatter(ffn_gain_grad, ("dp", "expert"), scatter_dimension=0, tiled=True),
        lax.psum_scatter(router_grad, ("dp", "expert"), scatter_dimension=0, tiled=True),
    )
    return (
        output,
        tokens_grad,
        summed[0],
        summed[1],
        summed[2],
        summed[3],
        summed[4],
        summed[5],
        summed[6],
        gate_summed[None],
        up_summed[None],
        down_summed[None],
    )


def solution(mesh):
    in_specs = (
        P(("dp", "expert"), None),
        P(("dp", "expert"), None),
        P(("dp", "expert")),
        P(("dp", "expert"), None),
        P(("dp", "expert"), None),
        P(("dp", "expert"), None),
        P(("dp", "expert"), None),
        P(("dp", "expert")),
        P(("dp", "expert"), None),
        P("expert", "dp", None),
        P("expert", "dp", None),
        P("expert", None, "dp"),
        P(("dp", "expert"), None),
        P(("dp", "expert"), None),
        P("expert", None),
        P(None, "expert", None),
    )
    out_specs = (
        P(("dp", "expert"), None),
        P(("dp", "expert"), None),
        P(("dp", "expert")),
        P(("dp", "expert"), None),
        P(("dp", "expert"), None),
        P(("dp", "expert"), None),
        P(("dp", "expert"), None),
        P(("dp", "expert")),
        P(("dp", "expert"), None),
        P("expert", "dp", None),
        P("expert", "dp", None),
        P("expert", None, "dp"),
    )
    fast = mesh.shape["dp"] == 2 and mesh.shape["expert"] == 16
    body = paired_body if fast else general_body
    return jax.shard_map(body, mesh=mesh, in_specs=in_specs, out_specs=out_specs, check_vma=False)
```
